32 devices in a mesh: dp: 2 (over y), blk: 8 (over z, x), chan: 2 (over core).
Axes of the slice: x: 2, y: 2, z: 4, core: 2. Of those that a mesh axis runs over, the one named last changes fastest.
Arguments:
- features: bfloat16 [1024, 512], P(('dp', 'blk'), 'chan'), parts along dimension 0, may hold values from -6 to 6
- chrom_len: int32 [2], P('dp'), parts along dimension 0, may hold values from 320 to 512
- band_mask: int32 [16, 4], P('dp'), parts along dimension 0, may hold values 0 or 1
- conv_weight: bfloat16 [2, 3, 512, 512], P(None, None, None, 'chan'), may hold values from -0.15625 to 0.15625
- conv_bias: bfloat16 [2, 512], P(None, 'chan'), may hold values from -3 to 3
- proj_weight: bfloat16 [512, 128], replicated, may hold values from -0.25 to 0.25
- proj_bias: bfloat16 [128], replicated, may hold values from -3 to 3
- map_weight: bfloat16 [3, 3, 64, 64], P(None, None, 'chan'), may hold values from -0.25 to 0.25
- map_bias: bfloat16 [64], P('chan'), may hold values from -3 to 3
- head_weight: bfloat16 [64], P('chan'), may hold values from -0.75 to 0.75
Outputs:
- contact: float32 [1024, 256], P(('dp', 'blk'), 'chan'), parts along dimension 0
The draws below stay inside these ranges and needn't reach their ends.
There are 2 independent parts, one for each index of `dp`. The reference program is written for one: setup_inputs(seed, part) draws one part's arguments, and reference() takes and returns one part's arrays. A program takes and returns all parts, laid end to end along the dimension named above; an argument that names none is the same for every part. Nothing has to cross between parts.
Inputs may be any that keep to these rules, and one draw needn't show every extreme that they name: Bins from chrom_len[0] on are padding. `band_mask`: 1 marks a predicted tile.
All inputs are finite; a program needn't handle non-finite values.
Results may differ from the reference program's by a relative error of at most 0.0053.
Values may be sent and summed in bfloat16 or wider, within the bound.
No kernel may reach another device: no remote copies, remote signals or barrier semaphores. Data moves between devices by JAX's collectives and lax.ppermute only.
A program may use at most 64 MiB of HBM per device.

```python
import jax
import jax.numpy as jnp
from jax import lax

C = 512
F2 = 64
BIN_DEV = 64
BAND = 3
CONV1 = 2
D2 = 2
NB = 512
N_BLK = 8


def set_ends(array, own_key, low, largest):
    extent = array.shape
    index_at = [jax.random.randint(jax.random.fold_in(own_key, axis), (), 0, extent[axis]) for axis in range(len(extent))]
    array = array.at[tuple(index_at)].set(low)
    longest = extent.index(max(extent))
    index_at[longest] = (index_at[longest] + 1) % extent[longest]
    return array.at[tuple(index_at)].set(largest)


def shard_levels(rng, shape, split, low, largest):
    loudness, own = 1.0, jax.random.fold_in(rng, 6)
    for dim, parts in split:
        draws = jnp.exp(jax.random.uniform(jax.random.fold_in(own, dim), (parts,), jnp.float32, low / len(split), largest / len(split)))
        loudness = loudness * jnp.repeat(draws, shape[dim] // parts).reshape([-1 if axis == dim else 1 for axis in range(len(shape))])
    return loudness


def noise(stream_key, extent, width, reach, cuts=(), kind=jnp.bfloat16):
    values = jax.random.normal(stream_key, extent, jnp.float32) * width
    if len(cuts) > 0:
        values = shard_levels(stream_key, extent, cuts, -0.22, 0.18) * values
    return jnp.clip(values, min=-reach, max=reach).astype(kind)


def setup_inputs(seed: int = 0, part: int = 0) -> dict:
    keys = jax.random.split(jax.random.key(seed), 11)
    part_keys = jax.random.split(jax.random.fold_in(keys[10], part), 11)
    return {
        "features": noise(part_keys[0], (NB, C), 1.0, 6.0, ((0, 8), (1, 2))),
        "chrom_len": jax.random.randint(part_keys[1], (1,), NB - 3 * BIN_DEV, NB + 1).astype(jnp.int32),
        "band_mask": set_ends((jax.random.randint(part_keys[2], (N_BLK, BAND + 1), 0, 4) < 3).astype(jnp.int32), jax.random.fold_in(part_keys[2], 1), 0, 1),
        "conv_weight": noise(keys[3], (CONV1, 3, C, C), (3 * C) ** -0.5, 0.15625, ((3, 2),)),
        "conv_bias": noise(keys[4], (CONV1, C), 0.5, 3.0, ((1, 2),)),
        "proj_weight": noise(keys[5], (C, 2 * F2), C ** -0.5, 0.25),
        "proj_bias": noise(keys[6], (2 * F2,), 0.5, 3.0),
        "map_weight": noise(keys[7], (3, 3, F2, F2), (9 * F2) ** -0.5, 0.25, ((2, 2),)),
        "map_bias": noise(keys[8], (F2,), 0.5, 3.0, ((0, 2),)),
        "head_weight": noise(keys[9], (F2,), F2 ** -0.5, 0.75, ((0, 2),)),
    }


def band_live(first_row, row_count, first_col, col_count, length, mask_table):
    row_bins = first_row + jnp.arange(row_count, dtype=jnp.int32)
    col_bins = first_col + jnp.arange(col_count, dtype=jnp.int32)
    row_blocks = jnp.floor_divide(row_bins, BIN_DEV)
    col_blocks = jnp.floor_divide(col_bins, BIN_DEV)
    offsets = col_blocks[None, :] - row_blocks[:, None]
    table_rows = jnp.take(mask_table, jnp.clip(row_blocks + 1, 0, N_BLK + 1), axis=0)
    result = jnp.zeros((row_count, col_count), jnp.float32)
    for offset_value in range(BAND + 1):
        result = result + jnp.where(offsets == offset_value, table_rows[:, offset_value:offset_value + 1], 0.0)
    row_valid = (row_bins >= 0) & (row_bins < length)
    col_valid = (col_bins >= 0) & (col_bins < length)
    return result * (row_valid[:, None] & col_valid[None, :]).astype(jnp.float32)


def reference(features, chrom_len, band_mask, conv_weight, conv_bias, proj_weight, proj_bias, map_weight, map_bias, head_weight):
    total_bins = features.shape[0]
    length = chrom_len[0]
    positions = jnp.arange(total_bins, dtype=jnp.int32)
    hidden_rows = jnp.where((positions < length)[:, None], features, jnp.zeros_like(features))
    for layer_index in range(CONV1):
        dilation = 2 ** (layer_index + 1)
        padded = jnp.pad(hidden_rows, ((dilation, dilation), (0, 0)))
        running = jnp.zeros((total_bins, C), jnp.float32)
        for tap_index in range(3):
            running = running + jnp.dot(padded[tap_index * dilation:tap_index * dilation + total_bins], conv_weight[layer_index, tap_index], preferred_element_type=jnp.float32)
        hidden_rows = (hidden_rows.astype(jnp.float32) + jax.nn.relu(running + conv_bias[layer_index].astype(jnp.float32))).astype(jnp.bfloat16)
    projected = (jnp.dot(hidden_rows, proj_weight, preferred_element_type=jnp.float32) + proj_bias.astype(jnp.float32)).astype(jnp.bfloat16)
    span_cols = (BAND + 1) * BIN_DEV
    row_proj = jnp.pad(projected[:, :F2].T, ((0, 0), (D2, D2)))
    col_proj = jnp.pad(projected[:, F2:].T, ((0, 0), (D2, span_cols + D2)))
    mask_table = jnp.pad(band_mask, ((1, 1), (0, 0))).astype(jnp.float32)
    weights_map = map_weight.astype(jnp.float32)
    bias_map = map_bias.astype(jnp.float32)[:, None, None]
    head_vector = head_weight.astype(jnp.float32)

    def strip_output(block_index):
        first_bin = block_index * BIN_DEV
        row_slab = lax.dynamic_slice_in_dim(row_proj, first_bin, BIN_DEV + 2 * D2, 1).astype(jnp.float32)
        col_slab = lax.dynamic_slice_in_dim(col_proj, first_bin, span_cols + 2 * D2, 1).astype(jnp.float32)
        live_area = band_live(first_bin - D2, BIN_DEV + 2 * D2, first_bin - D2, span_cols + 2 * D2, length, mask_table)
        pair_map = (jax.nn.relu(row_slab[:, :, None] + col_slab[:, None, :]) * live_area[None]).astype(jnp.bfloat16)
        pair_wide = pair_map.astype(jnp.float32)
        running = jnp.zeros((F2, BIN_DEV, span_cols), jnp.float32)
        for row_tap in range(3):
            for col_tap in range(3):
                window = pair_wide[:, row_tap * D2:row_tap * D2 + BIN_DEV, col_tap * D2:col_tap * D2 + span_cols]
                running = running + jnp.einsum('ok,kab->oab', weights_map[row_tap, col_tap], window, precision=lax.Precision.HIGHEST)
        centre = pair_wide[:, D2:D2 + BIN_DEV, D2:D2 + span_cols]
        mixed = centre + jax.nn.relu(running + bias_map)
        contact = jnp.einsum('o,oab->ab', head_vector, mixed, precision=lax.Precision.HIGHEST)
        return contact * live_area[D2:D2 + BIN_DEV, D2:D2 + span_cols]

    strips = lax.map(strip_output, jnp.arange(N_BLK, dtype=jnp.int32))
    return strips.reshape(total_bins, span_cols)
```

```python
import functools

import jax
import jax.numpy as jnp
from jax import lax
from jax.experimental import pallas as pl
from jax.experimental.pallas import tpu as pltpu
from jax.sharding import PartitionSpec as P

F2 = 64
BAND = 3
CONV1 = 2
D2 = 2
HALO = 16
F32 = jnp.float32
BF16 = jnp.bfloat16


def chan_swap(value):
    return lax.ppermute(value, "chan", [(0, 1), (1, 0)])


def blk_permute(value, offset_0, offset_1):
    count = lax.axis_size("blk")
    pairs = []
    for i in range(count):
        pairs.append((((i + offset_0) % count) * 2, i * 2))
        pairs.append((((i + offset_1) % count) * 2 + 1, i * 2 + 1))
    return lax.ppermute(value, ("blk", "chan"), pairs)


def contact_kernel(
    length_ref,
    mask_ref,
    own_ref,
    r1_ref,
    r2_ref,
    r3_ref,
    s1_ref,
    s3_ref,
    w_own_ref,
    w_oth_ref,
    cb_own_ref,
    cb_oth_ref,
    pw_ref,
    pb_ref,
    wbig_ref,
    bias4_ref,
    head_ref,
    out_ref,
    h_s,
    pa6_s,
    x_s,
    mix_s,
):
    bins = own_ref.shape[1]
    half = own_ref.shape[2]
    col_rows = 2 * bins + 2 * HALO
    row_rows = bins + 2 * HALO
    rows = col_rows + row_rows
    count = lax.axis_size("blk")
    i = lax.axis_index("blk")
    c = lax.axis_index("chan")
    length = length_ref[0]
    first = i * bins
    first_col = first + c * (2 * bins)

    def put(start, number, ref, source):
        for part in range(2):
            h_s[start : start + number, part * half : (part + 1) * half] = ref[
                part, source : source + number, :
            ].astype(F32)

    tail = bins - HALO
    put(0, HALO, r1_ref, tail)
    put(col_rows + HALO, bins, own_ref, 0)

    @pl.when(c == 0)
    def _():
        put(HALO, bins, own_ref, 0)
        put(HALO + bins, bins, s1_ref, 0)
        put(HALO + 2 * bins, HALO, r2_ref, 0)
        put(col_rows, HALO, r1_ref, tail)
        put(col_rows + HALO + bins, HALO, s1_ref, 0)

    @pl.when(c == 1)
    def _():
        put(HALO, bins, r2_ref, 0)
        put(HALO + bins, bins, r3_ref, 0)
        put(HALO + 2 * bins, HALO, s3_ref, 0)
        put(col_rows, HALO, s1_ref, tail)
        put(col_rows + HALO + bins, HALO, r1_ref, 0)

    place = lax.broadcasted_iota(jnp.int32, (rows, 1), 0)
    bin_index = jnp.where(
        place < col_rows, first_col - HALO + place, first - HALO - col_rows + place
    )
    valid = (bin_index >= 0) & (bin_index < length)
    inside = (bin_index >= 0) & (bin_index < count * bins)
    h_s[...] = jnp.where(valid, h_s[...], 0.0)

    for layer in range(CONV1):
        e = 2 ** (layer + 1)
        hidden = h_s[...]
        taps = [
            pltpu.roll(hidden, ((1 - t) * e) % rows, axis=0).astype(BF16) if t != 1 else hidden.astype(BF16)
            for t in range(3)
        ]
        for w_ref, cb_ref, side in ((w_own_ref, cb_own_ref, c), (w_oth_ref, cb_oth_ref, 1 - c)):
            q = jnp.dot(taps[0], w_ref[layer, 0], preferred_element_type=F32)
            q = q + jnp.dot(taps[1], w_ref[layer, 1], preferred_element_type=F32)
            q = q + jnp.dot(taps[2], w_ref[layer, 2], preferred_element_type=F32)
            lanes = pl.ds(pl.multiple_of(side * half, half), half)
            bias = cb_ref[layer : layer + 1, :].astype(F32)
            new = (h_s[:, lanes] + jnp.maximum(q + bias, 0.0)).astype(BF16).astype(F32)
            h_s[:, lanes] = jnp.where(inside, new, 0.0)

    proj = jnp.dot(h_s[...].astype(BF16), pw_ref[...], preferred_element_type=F32)
    proj = (proj + pb_ref[...].astype(F32)).astype(BF16).astype(F32)

    minus = F32(-jnp.inf)
    low = lax.broadcasted_iota(jnp.int32, (1, 2 * F2), 1) < F2
    pcol = proj[:col_rows]
    pcol = jnp.where(low, pltpu.roll(pcol, F2, axis=1), pcol)
    b_index = lax.broadcasted_iota(jnp.int32, (2 * bins, 1), 0)

    def live_at(y, variant):
        block_row = i + variant
        row_at = jnp.clip(block_row, 0, count - 1)
        scalars = []
        for u in range(-1, 3):
            o = 2 * c + u - variant
            value = mask_ref[row_at, jnp.clip(o, 0, BAND)]
            scalars.append(jnp.where((o >= 0) & (o <= BAND), value, 0))
        value = jnp.where(
            y < 0,
            scalars[0],
            jnp.where(y < bins, scalars[1], jnp.where(y < 2 * bins, scalars[2], scalars[3])),
        )
        column = first_col + y
        return (value != 0) & (column >= 0) & (column < length)

    masked = {}
    for r in range(3):
        start = HALO + (r - 1) * D2
        shifted = pltpu.roll(pcol, col_rows - start, axis=0)[: 2 * bins]
        y = b_index + (r - 1) * D2
        for variant in (-1, 0, 1):
            masked[variant, r] = jnp.where(live_at(y, variant), shifted, minus)

    def columns(v0, v1):
        return jnp.concatenate(
            [
                jnp.where(low, masked[v0, 0], masked[v0, 1]),
                jnp.where(low, masked[v0, 2], masked[v1, 0]),
                jnp.where(low, masked[v1, 1], masked[v1, 2]),
            ],
            axis=1,
        ).astype(BF16).reshape(2 * bins // 16, 16, 6 * F2)

    col_first, col_mid, col_last = columns(-1, 0), columns(0, 0), columns(0, 1)
    col_centre = masked[0, 1].astype(BF16).reshape(2 * bins // 16, 16, 2 * F2)

    prow = proj[col_rows:]
    prow = jnp.where(low, prow, pltpu.roll(prow, F2, axis=1))
    prow = jnp.where(valid[col_rows:], prow, minus)
    prow_next = pltpu.roll(prow, row_rows - D2, axis=0)
    pa6_s[:, : 2 * F2] = prow
    pa6_s[:, 2 * F2 : 4 * F2] = jnp.where(low, prow, prow_next)
    pa6_s[:, 4 * F2 :] = prow_next

    groups = bins // 8
    per_dot = x_s.shape[0] // (2 * bins)
    zero = jnp.zeros((), BF16)
    for v in range(2):
        for start in range(0, groups, per_dot):
            for slot in range(2 * start, 2 * (start + per_dot) + 1):
                at = HALO - D2 + v + 4 * slot
                row = jnp.broadcast_to(pa6_s[at : at + 1, :], (16, 6 * F2)).astype(BF16)
                cols = col_first if slot == 0 else col_last if slot == 2 * groups else col_mid
                value = jnp.maximum(row[None] + cols, zero).reshape(2 * bins, 6 * F2)
                for s in range(3):
                    if (slot - s) % 2 == 0 and start <= (slot - s) // 2 < start + per_dot:
                        at_row = ((slot - s) // 2 - start) * 2 * bins
                        x_s[at_row : at_row + 2 * bins, s * 6 * F2 : (s + 1) * 6 * F2] = value
            y = jnp.dot(x_s[...], wbig_ref[...], preferred_element_type=F32)
            y = jnp.maximum(y + bias4_ref[...], 0.0)
            for group in range(start, start + per_dot):
                at = HALO + v + 8 * group
                parts = []
                for k in range(2):
                    row = pa6_s[at + 4 * k : at + 4 * k + 1, 2 * F2 : 4 * F2]
                    row = jnp.broadcast_to(row, (16, 2 * F2)).astype(BF16)
                    parts.append(
                        jnp.maximum(row[None] + col_centre, zero).reshape(2 * bins, 2 * F2)
                    )
                centre = jnp.concatenate(parts, axis=1).astype(F32)
                at_row = (group - start) * 2 * bins
                mixed = y[at_row : at_row + 2 * bins] + centre
                mix_s[group, :, v * 4 * F2 : (v + 1) * 4 * F2] = mixed.astype(BF16)

    lane_live = live_at(lax.broadcasted_iota(jnp.int32, (1, 2 * bins), 1), 0)
    for group in range(groups):
        value = lax.dot_general(
            head_ref[...], mix_s[group], (((1,), (1,)), ((), ())), preferred_element_type=F32
        )[:8]
        row_bins = first + 8 * group + lax.broadcasted_iota(jnp.int32, (8, 1), 0)
        out_ref[8 * group : 8 * group + 8, :] = jnp.where(
            lane_live & (row_bins < length), value, 0.0
        )


def local(
    features,
    chrom_len,
    band_mask,
    conv_weight,
    conv_bias,
    proj_weight,
    proj_bias,
    map_weight,
    map_bias,
    head_weight,
):
    bins, half = features.shape
    c = lax.axis_index("chan")
    own = lax.all_gather(features, "chan", axis=0)
    r1 = blk_permute(own, -1, 1)
    r2 = blk_permute(own, 2, 2)
    r3 = blk_permute(own, 4, 3)
    s1 = chan_swap(r1)
    s3 = chan_swap(r3)
    w_oth = chan_swap(conv_weight)
    cb_oth = chan_swap(conv_bias)

    def both(value, axis):
        other = chan_swap(value)
        return jnp.where(
            c == 0,
            jnp.concatenate([value, other], axis=axis),
            jnp.concatenate([other, value], axis=axis),
        )

    kernel_all = both(map_weight, 2)
    small = both(jnp.stack([map_bias, head_weight]), 1)
    taps = jnp.transpose(kernel_all, (0, 1, 3, 2)).reshape(3, 3 * F2, F2)
    blank = jnp.zeros((3 * F2, F2), BF16)
    wbig = jnp.concatenate(
        [
            jnp.concatenate([taps[m - j] if 0 <= m - j < 3 else blank for j in range(4)], axis=1)
            for m in range(6)
        ],
        axis=0,
    )
    bias4 = jnp.tile(small[0].astype(F32), 4)[None]
    q = jnp.arange(16)[:, None]
    k = jnp.arange(8 * F2)[None]
    head = jnp.where(
        q == 2 * ((k % (4 * F2)) // F2) + k // (4 * F2), jnp.tile(small[1], 8)[None], 0
    ).astype(BF16)

    rows = 3 * bins + 4 * HALO
    vmem = pl.BlockSpec(memory_space=pltpu.VMEM)
    smem = pl.BlockSpec(memory_space=pltpu.SMEM)
    return pl.pallas_call(
        contact_kernel,
        out_shape=jax.ShapeDtypeStruct((bins, 2 * bins), F32),
        in_specs=[smem, smem] + [vmem] * 15,
        out_specs=vmem,
        scratch_shapes=[
            pltpu.VMEM((rows, 2 * half), F32),
            pltpu.VMEM((bins + 2 * HALO, 6 * F2), F32),
            pltpu.VMEM((4 * 2 * bins, 18 * F2), BF16),
            pltpu.VMEM((bins // 8, 2 * bins, 8 * F2), BF16),
        ],
        compiler_params=pltpu.CompilerParams(vmem_limit_bytes=24 * 1024 * 1024),
    )(
        chrom_len,
        band_mask,
        own,
        r1,
        r2,
        r3,
        s1,
        s3,
        conv_weight,
        w_oth,
        conv_bias,
        cb_oth,
        proj_weight,
        proj_bias[None],
        wbig,
        bias4,
        head,
    )


def solution(mesh):
    return jax.shard_map(
        local,
        mesh=mesh,
        in_specs=(
            P(("dp", "blk"), "chan"),
            P("dp"),
            P("dp", None),
            P(None, None, None, "chan"),
            P(None, "chan"),
            P(),
            P(),
            P(None, None, "chan", None),
            P("chan"),
            P("chan"),
        ),
        out_specs=P(("dp", "blk"), "chan"),
        check_vma=False,
    )
```

```python
import jax
import jax.numpy as jnp
from jax import lax
from jax.experimental import pallas as pl
from jax.experimental.pallas import tpu as pltpu
from jax.sharding import PartitionSpec as P

F2 = 64
BAND = 3
CONV1 = 2
D2 = 2
HALO = 16
F32 = jnp.float32
BF16 = jnp.bfloat16


def chan_swap(value):
    return lax.ppermute(value, "chan", [(0, 1), (1, 0)])


def blk_permute(value, offset_0, offset_1):
    count = lax.axis_size("blk")
    pairs = []
    for i in range(count):
        pairs.append((((i + offset_0) % count) * 2, i * 2))
        pairs.append((((i + offset_1) % count) * 2 + 1, i * 2 + 1))
    return lax.ppermute(value, ("blk", "chan"), pairs)


def prep_kernel(
    length_ref,
    mask_ref,
    mw_own_ref,
    mw_oth_ref,
    mb_own_ref,
    mb_oth_ref,
    hw_own_ref,
    hw_oth_ref,
    cb_own_ref,
    cb_oth_ref,
    pb_ref,
    wbig_ref,
    col_mask_ref,
    valid_ref,
    small_ref,
    head_ref,
    wt_s,
    taps_s,
):
    rows = valid_ref.shape[0]
    columns = col_mask_ref.shape[1]
    bins = columns // 2
    half = mw_own_ref.shape[2]
    col_rows = columns + 2 * HALO
    count = lax.axis_size("blk")
    i = lax.axis_index("blk")
    c = lax.axis_index("chan")
    first = i * bins
    first_col = first + c * columns
    length = length_ref[...]

    for source, side in ((mw_own_ref, c), (mw_oth_ref, 1 - c)):
        at = pl.ds(pl.multiple_of(side * half, half), half)
        for s in range(3):
            for r in range(3):
                taps_s[3 * s + r, at, :] = source[s, r].astype(F32)
    blank = jnp.zeros((F2, F2), F32)
    for j in range(4):
        pieces = []
        for m in range(6):
            for r in range(3):
                pieces.append(taps_s[3 * (m - j) + r] if 0 <= m - j < 3 else blank)
        for tile in range(9):
            wt_s[j * F2 : (j + 1) * F2, tile * 2 * F2 : (tile + 1) * 2 * F2] = jnp.concatenate(
                pieces[2 * tile : 2 * tile + 2], axis=1
            )
    wbig_ref[...] = wt_s[...].T.astype(BF16)

    def spread(own_ref, oth_ref, repeats):
        o = lax.broadcasted_iota(jnp.int32, (half, repeats * F2), 0)
        lane = lax.broadcasted_iota(jnp.int32, (half, repeats * F2), 1) % F2
        total = jnp.zeros((16, repeats * F2), F32)
        for ref, side in ((own_ref, c), (oth_ref, 1 - c)):
            pick = (lane == side * half + o).astype(BF16)
            value = jnp.broadcast_to(ref[...], (16, half)).astype(BF16)
            total = total + jnp.dot(value, pick, preferred_element_type=F32)
        return total

    head_all = spread(hw_own_ref, hw_oth_ref, 8)
    q = lax.broadcasted_iota(jnp.int32, (16, 8 * F2), 0)
    k = lax.broadcasted_iota(jnp.int32, (16, 8 * F2), 1)
    head_ref[...] = jnp.where(
        q == 2 * ((k % (4 * F2)) // F2) + k // (4 * F2), head_all, 0.0
    ).astype(BF16)
    bias_all = spread(mb_own_ref, mb_oth_ref, 4)

    minus = F32(-jnp.inf)
    block = lax.broadcasted_iota(jnp.int32, (BAND + 1, count), 1)

    def live_at(y, variant):
        at_row = jnp.sum(jnp.where(block == i + variant, mask_ref[...], 0), axis=1, keepdims=True)
        offset = lax.broadcasted_iota(jnp.int32, (BAND + 1, 1), 0)

        def entry(u):
            return jnp.sum(
                jnp.where(offset == 2 * c + u - variant, at_row, 0), axis=0, keepdims=True
            )

        value = jnp.where(
            y < 0,
            entry(-1),
            jnp.where(y < bins, entry(0), jnp.where(y < columns, entry(1), entry(2))),
        )
        column = first_col + y
        return (value != 0) & (column >= 0) & (column < length)

    b_index = lax.broadcasted_iota(jnp.int32, (columns, 2 * F2), 0)
    low = lax.broadcasted_iota(jnp.int32, (columns, 2 * F2), 1) < F2
    masks = {}
    for variant in (-1, 0, 1):
        for r in range(3):
            masks[variant, r] = jnp.where(
                live_at(b_index + (r - 1) * D2, variant), 0.0, minus
            )
    for at, (v0, v1) in enumerate(((-1, 0), (0, 0), (0, 1))):
        col_mask_ref[at, :, : 2 * F2] = jnp.where(low, masks[v0, 0], masks[v0, 1])
        col_mask_ref[at, :, 2 * F2 : 4 * F2] = jnp.where(low, masks[v0, 2], masks[v1, 0])
        col_mask_ref[at, :, 4 * F2 :] = jnp.where(low, masks[v1, 1], masks[v1, 2])

    place = lax.broadcasted_iota(jnp.int32, (rows, 2 * F2), 0)
    bin_index = jnp.where(
        place < col_rows, first_col - HALO + place, first - HALO - col_rows + place
    )
    valid_ref[...] = jnp.where((bin_index >= 0) & (bin_index < length), 1.0, 0.0)

    small_ref[0:2, :] = cb_own_ref[...].astype(F32)
    small_ref[2:4, :] = cb_oth_ref[...].astype(F32)
    small_ref[4:5, :] = bias_all[:1]
    small_ref[5:6, : 2 * F2] = pb_ref[...].astype(F32)
    small_ref[5:6, 2 * F2 :] = jnp.where(
        live_at(lax.broadcasted_iota(jnp.int32, (1, columns), 1), 0), 1.0, 0.0
    )


def contact_kernel(
    own_ref,
    r1_ref,
    r2_ref,
    r3_ref,
    s1_ref,
    s3_ref,
    w_own_ref,
    w_oth_ref,
    pw_ref,
    wbig_ref,
    col_mask_ref,
    valid_ref,
    small_ref,
    head_ref,
    out_ref,
    h_s,
    pa6_s,
    x_s,
    mix_s,
):
    bins = own_ref.shape[1]
    half = own_ref.shape[2]
    col_rows = 2 * bins + 2 * HALO
    row_rows = bins + 2 * HALO
    rows = col_rows + row_rows
    count = lax.axis_size("blk")
    i = lax.axis_index("blk")
    c = lax.axis_index("chan")
    first = i * bins
    first_col = first + c * (2 * bins)

    def put(start, number, ref, source):
        keep = valid_ref[start : start + number, :] != 0
        for part in range(2):
            for at in range(0, half, 128):
                h_s[start : start + number, part * half + at : part * half + at + 128] = jnp.where(
                    keep, ref[part, source : source + number, at : at + 128].astype(F32), 0.0
                )

    tail = bins - HALO
    put(0, HALO, r1_ref, tail)
    put(col_rows + HALO, bins, own_ref, 0)

    @pl.when(c == 0)
    def _():
        put(HALO, bins, own_ref, 0)
        put(HALO + bins, bins, s1_ref, 0)
        put(HALO + 2 * bins, HALO, r2_ref, 0)
        put(col_rows, HALO, r1_ref, tail)
        put(col_rows + HALO + bins, HALO, s1_ref, 0)

    @pl.when(c == 1)
    def _():
        put(HALO, bins, r2_ref, 0)
        put(HALO + bins, bins, r3_ref, 0)
        put(HALO + 2 * bins, HALO, s3_ref, 0)
        put(col_rows, HALO, s1_ref, tail)
        put(col_rows + HALO + bins, HALO, r1_ref, 0)

    place = lax.broadcasted_iota(jnp.int32, (rows, 1), 0)
    bin_index = jnp.where(
        place < col_rows, first_col - HALO + place, first - HALO - col_rows + place
    )
    inside = (bin_index >= 0) & (bin_index < count * bins)

    for layer in range(CONV1):
        e = 2 ** (layer + 1)
        hidden = h_s[...]
        taps = [
            (hidden if t == 1 else pltpu.roll(hidden, ((1 - t) * e) % rows, axis=0)).astype(BF16)
            for t in range(3)
        ]
        for at, (w_ref, side) in enumerate(((w_own_ref, c), (w_oth_ref, 1 - c))):
            q = jnp.dot(taps[0], w_ref[layer, 0], preferred_element_type=F32)
            q = q + jnp.dot(taps[1], w_ref[layer, 1], preferred_element_type=F32)
            q = q + jnp.dot(taps[2], w_ref[layer, 2], preferred_element_type=F32)
            lanes = pl.ds(pl.multiple_of(side * half, half), half)
            bias = small_ref[2 * at + layer : 2 * at + layer + 1, :]
            new = (h_s[:, lanes] + jnp.maximum(q + bias, 0.0)).astype(BF16).astype(F32)
            h_s[:, lanes] = jnp.where(inside, new, 0.0)

    proj = jnp.dot(h_s[...].astype(BF16), pw_ref[...], preferred_element_type=F32)
    proj = (proj + small_ref[5:6, : 2 * F2]).astype(BF16).astype(F32)

    minus = F32(-jnp.inf)
    low = lax.broadcasted_iota(jnp.int32, (1, 2 * F2), 1) < F2
    pcol = proj[:col_rows]
    pcol = jnp.where(low, pltpu.roll(pcol, F2, axis=1), pcol)
    shifted = [
        pltpu.roll(pcol, col_rows - HALO - (r - 1) * D2, axis=0)[: 2 * bins] for r in range(3)
    ]
    tiles = [
        jnp.where(low, shifted[0], shifted[1]),
        jnp.where(low, shifted[2], shifted[0]),
        jnp.where(low, shifted[1], shifted[2]),
    ]
    tiled = jnp.concatenate(tiles, axis=1)
    col_first, col_mid, col_last = [
        (tiled + col_mask_ref[at]).astype(BF16).reshape(2 * bins // 16, 16, 6 * F2)
        for at in range(3)
    ]
    col_centre = shifted[1].astype(BF16).reshape(2 * bins // 16, 16, 2 * F2)

    prow = proj[col_rows:]
    prow = jnp.where(low, prow, pltpu.roll(prow, F2, axis=1))
    prow = jnp.where(valid_ref[col_rows:, :] != 0, prow, minus)
    prow_next = pltpu.roll(prow, row_rows - D2, axis=0)
    pa6_s[:, : 2 * F2] = prow
    pa6_s[:, 2 * F2 : 4 * F2] = jnp.where(low, prow, prow_next)
    pa6_s[:, 4 * F2 :] = prow_next

    groups = bins // 8
    per_dot = x_s.shape[0] // (2 * bins)
    zero = jnp.zeros((), BF16)
    bias4 = small_ref[4:5, :]
    for v in range(2):
        for start in range(0, groups, per_dot):
            for slot in range(2 * start, 2 * (start + per_dot) + 1):
                at = HALO - D2 + v + 4 * slot
                row = jnp.broadcast_to(pa6_s[at : at + 1, :], (16, 6 * F2)).astype(BF16)
                cols = col_first if slot == 0 else col_last if slot == 2 * groups else col_mid
                value = jnp.maximum(row[None] + cols, zero).reshape(2 * bins, 6 * F2)
                for s in range(3):
                    if (slot - s) % 2 == 0 and start <= (slot - s) // 2 < start + per_dot:
                        at_row = ((slot - s) // 2 - start) * 2 * bins
                        x_s[at_row : at_row + 2 * bins, s * 6 * F2 : (s + 1) * 6 * F2] = value
            y = jnp.dot(x_s[...], wbig_ref[...], preferred_element_type=F32)
            y = jnp.maximum(y + bias4, 0.0)
            for group in range(start, start + per_dot):
                at = HALO + v + 8 * group
                parts = []
                for k in range(2):
                    row = pa6_s[at + 4 * k : at + 4 * k + 1, 2 * F2 : 4 * F2]
                    row = jnp.broadcast_to(row, (16, 2 * F2)).astype(BF16)
                    parts.append(
                        jnp.maximum(row[None] + col_centre, zero).reshape(2 * bins, 2 * F2)
                    )
                centre = jnp.concatenate(parts, axis=1).astype(F32)
                at_row = (group - start) * 2 * bins
                mixed = y[at_row : at_row + 2 * bins] + centre
                mix_s[group, :, v * 4 * F2 : (v + 1) * 4 * F2] = mixed.astype(BF16)

    lane_live = small_ref[5:6, 2 * F2 :] != 0
    for group in range(groups):
        value = lax.dot_general(
            head_ref[...], mix_s[group], (((1,), (1,)), ((), ())), preferred_element_type=F32
        )[:8]
        at = col_rows + HALO + 8 * group
        out_ref[8 * group : 8 * group + 8, :] = jnp.where(
            lane_live & (valid_ref[at : at + 8, :] != 0), value, 0.0
        )


def local(
    features,
    chrom_len,
    band_mask,
    conv_weight,
    conv_bias,
    proj_weight,
    proj_bias,
    map_weight,
    map_bias,
    head_weight,
):
    bins, half = features.shape
    own = lax.all_gather(features, "chan", axis=0)
    r2 = blk_permute(own, 2, 2)
    r1 = blk_permute(own, -1, 1)
    r3 = blk_permute(own, 4, 3)
    s1 = chan_swap(r1)
    s3 = chan_swap(r3)
    w_oth = chan_swap(conv_weight)

    rows = 3 * bins + 4 * HALO
    vmem = pl.BlockSpec(memory_space=pltpu.VMEM)
    params = pltpu.CompilerParams(vmem_limit_bytes=24 * 1024 * 1024)
    prepared = pl.pallas_call(
        prep_kernel,
        out_shape=[
            jax.ShapeDtypeStruct((18 * F2, 4 * F2), BF16),
            jax.ShapeDtypeStruct((3, 2 * bins, 6 * F2), F32),
            jax.ShapeDtypeStruct((rows, 2 * F2), F32),
            jax.ShapeDtypeStruct((8, half), F32),
            jax.ShapeDtypeStruct((16, 8 * F2), BF16),
        ],
        in_specs=[vmem] * 11,
        out_specs=[vmem] * 5,
        scratch_shapes=[
            pltpu.VMEM((4 * F2, 18 * F2), F32),
            pltpu.VMEM((9, F2, F2), F32),
        ],
        compiler_params=params,
    )(
        chrom_len[None],
        band_mask.T,
        map_weight,
        chan_swap(map_weight),
        map_bias[None],
        chan_swap(map_bias)[None],
        head_weight[None],
        chan_swap(head_weight)[None],
        conv_bias,
        chan_swap(conv_bias),
        proj_bias[None],
    )
    return pl.pallas_call(
        contact_kernel,
        out_shape=jax.ShapeDtypeStruct((bins, 2 * bins), F32),
        in_specs=[vmem] * 14,
        out_specs=vmem,
        scratch_shapes=[
            pltpu.VMEM((rows, 2 * half), F32),
            pltpu.VMEM((bins + 2 * HALO, 6 * F2), F32),
            pltpu.VMEM((4 * 2 * bins, 18 * F2), BF16),
            pltpu.VMEM((bins // 8, 2 * bins, 8 * F2), BF16),
        ],
        compiler_params=params,
    )(own, r1, r2, r3, s1, s3, conv_weight, w_oth, proj_weight, *prepared)


def solution(mesh):
    return jax.shard_map(
        local,
        mesh=mesh,
        in_specs=(
            P(("dp", "blk"), "chan"),
            P("dp"),
            P("dp", None),
            P(None, None, None, "chan"),
            P(None, "chan"),
            P(),
            P(),
            P(None, None, "chan", None),
            P("chan"),
            P("chan"),
        ),
        out_specs=P(("dp", "blk"), "chan"),
        check_vma=False,
    )
```

```python
import jax
import jax.numpy as jnp
from jax import lax
from jax.experimental import pallas as pl
from jax.experimental.pallas import tpu as pltpu
from jax.sharding import PartitionSpec as P

F2 = 64
BAND = 3
CONV1 = 2
D2 = 2
HALO = 16
F32 = jnp.float32
BF16 = jnp.bfloat16


def chan_swap(value):
    return lax.ppermute(value, "chan", [(0, 1), (1, 0)])


def blk_permute(value, offset_0, offset_1):
    count = lax.axis_size("blk")
    pairs = []
    for i in range(count):
        pairs.append((((i + offset_0) % count) * 2, i * 2))
        pairs.append((((i + offset_1) % count) * 2 + 1, i * 2 + 1))
    return lax.ppermute(value, ("blk", "chan"), pairs)


def pack_kernel(
    own_any,
    length_any,
    mask_any,
    mw_any,
    mb_any,
    hw_any,
    cb_any,
    pb_any,
    w_any,
    pw_any,
    packed_ref,
    col_mask_ref,
    valid_ref,
    small_ref,
    w_ref,
    pw_ref,
    length_s,
    mask_s,
    mw_s,
    mb_s,
    hw_s,
    cb_s,
    pb_s,
    extra_s,
    sems,
):
    pairs = (
        (length_any, length_s),
        (mask_any, mask_s),
        (mw_any, mw_s),
        (mb_any, mb_s),
        (hw_any, hw_s),
        (cb_any, cb_s),
        (pb_any, pb_s),
        (w_any, w_ref),
        (pw_any, pw_ref),
    )
    copies = [
        pltpu.make_async_copy(source, target, sems.at[at])
        for at, (source, target) in enumerate(pairs)
    ]
    for copy in copies:
        copy.start()
    for copy in copies[:7]:
        copy.wait()

    rows = valid_ref.shape[0]
    columns = col_mask_ref.shape[1]
    bins = columns // 2
    half = mw_any.shape[2]
    col_rows = columns + 2 * HALO
    count = lax.axis_size("blk")
    i = lax.axis_index("blk")
    c = lax.axis_index("chan")
    first = i * bins
    first_col = first + c * columns
    length = length_s[...]

    extra_s[...] = jnp.zeros_like(extra_s)
    biases = cb_s[...].astype(F32)
    for layer in range(CONV1):
        for quarter in range(4):
            at = 4 * layer + quarter
            extra_s[at : at + 1, :F2] = biases[layer : layer + 1, quarter * F2 : (quarter + 1) * F2]
    extra_s[8:9, :half] = mb_s[...].astype(F32)
    extra_s[9:10, :half] = hw_s[...].astype(F32)
    extra = pltpu.roll(extra_s[...], F2, axis=1)
    for s in range(3):
        for r in range(3):
            at = (3 * s + r) * half
            packed_ref[at : at + half, :F2] = mw_s[s, r]
    packed_ref[:32, F2:] = extra[:, F2:].astype(BF16)

    minus = F32(-jnp.inf)
    block = lax.broadcasted_iota(jnp.int32, (BAND + 1, count), 1)

    def live_at(y, variant):
        at_row = jnp.sum(jnp.where(block == i + variant, mask_s[...], 0), axis=1, keepdims=True)
        offset = lax.broadcasted_iota(jnp.int32, (BAND + 1, 1), 0)

        def entry(u):
            return jnp.sum(
                jnp.where(offset == 2 * c + u - variant, at_row, 0), axis=0, keepdims=True
            )

        value = jnp.where(
            y < 0,
            entry(-1),
            jnp.where(y < bins, entry(0), jnp.where(y < columns, entry(1), entry(2))),
        )
        column = first_col + y
        return (value != 0) & (column >= 0) & (column < length)

    b_index = lax.broadcasted_iota(jnp.int32, (columns, 2 * F2), 0)
    low = lax.broadcasted_iota(jnp.int32, (columns, 2 * F2), 1) < F2
    masks = {}
    for variant in (-1, 0, 1):
        for r in range(3):
            masks[variant, r] = jnp.where(
                live_at(b_index + (r - 1) * D2, variant), 0.0, minus
            )
    for at, (v0, v1) in enumerate(((-1, 0), (0, 0), (0, 1))):
        col_mask_ref[at, :, : 2 * F2] = jnp.where(low, masks[v0, 0], masks[v0, 1])
        col_mask_ref[at, :, 2 * F2 : 4 * F2] = jnp.where(low, masks[v0, 2], masks[v1, 0])
        col_mask_ref[at, :, 4 * F2 :] = jnp.where(low, masks[v1, 1], masks[v1, 2])

    place = lax.broadcasted_iota(jnp.int32, (rows, 2 * F2), 0)
    bin_index = jnp.where(
        place < col_rows, first_col - HALO + place, first - HALO - col_rows + place
    )
    valid_ref[...] = jnp.where((bin_index >= 0) & (bin_index < length), 1.0, 0.0)

    small_ref[0:2, :] = cb_s[...].astype(F32)
    small_ref[2:3, : 2 * F2] = pb_s[...].astype(F32)
    small_ref[2:3, 2 * F2 :] = jnp.where(
        live_at(lax.broadcasted_iota(jnp.int32, (1, columns), 1), 0), 1.0, 0.0
    )
    for copy in copies[7:]:
        copy.wait()


def prep_kernel(own_ref, oth_ref, wbig_ref, side_ref, head_ref, wt_s, taps_s):
    half = own_ref.shape[0] // 9
    c = lax.axis_index("chan")

    for source, side in ((own_ref, c), (oth_ref, 1 - c)):
        at = pl.ds(pl.multiple_of(side * half, half), half)
        for tap in range(9):
            taps_s[tap, at, :] = source[tap * half : (tap + 1) * half, :F2].astype(F32)
    blank = jnp.zeros((F2, F2), F32)
    for j in range(4):
        pieces = []
        for m in range(6):
            for r in range(3):
                pieces.append(taps_s[3 * (m - j) + r] if 0 <= m - j < 3 else blank)
        for tile in range(9):
            wt_s[j * F2 : (j + 1) * F2, tile * 2 * F2 : (tile + 1) * 2 * F2] = jnp.concatenate(
                pieces[2 * tile : 2 * tile + 2], axis=1
            )
    wbig_ref[...] = wt_s[...].T.astype(BF16)

    def spread(row, repeats):
        o = lax.broadcasted_iota(jnp.int32, (2 * F2, repeats * F2), 0)
        lane = lax.broadcasted_iota(jnp.int32, (2 * F2, repeats * F2), 1) % F2
        total = jnp.zeros((16, repeats * F2), F32)
        for ref, side in ((own_ref, c), (oth_ref, 1 - c)):
            pick = ((lane == side * half + o - F2) & (o >= F2) & (o < F2 + half)).astype(BF16)
            value = ref[:16, :].astype(F32)[row : row + 1]
            value = jnp.broadcast_to(value, (16, 2 * F2)).astype(BF16)
            total = total + jnp.dot(value, pick, preferred_element_type=F32)
        return total

    q = lax.broadcasted_iota(jnp.int32, (16, 8 * F2), 0)
    k = lax.broadcasted_iota(jnp.int32, (16, 8 * F2), 1)
    head_ref[...] = jnp.where(
        q == 2 * ((k % (4 * F2)) // F2) + k // (4 * F2), spread(9, 8), 0.0
    ).astype(BF16)
    side_ref[0:1, :] = spread(8, 4)[:1]
    other = oth_ref[:16, :].astype(F32)
    other = pltpu.roll(other, F2, axis=1)
    for layer in range(CONV1):
        for quarter in range(4):
            at = 4 * layer + quarter
            side_ref[1 + layer : 2 + layer, quarter * F2 : (quarter + 1) * F2] = other[
                at : at + 1, :F2
            ]


def contact_kernel(
    own_ref,
    r1_ref,
    r2_ref,
    r3_ref,
    s1_ref,
    s3_ref,
    w_own_ref,
    w_oth_ref,
    pw_ref,
    col_mask_ref,
    valid_ref,
    small_ref,
    wbig_ref,
    side_ref,
    head_ref,
    out_ref,
    h_s,
    pa6_s,
    x_s,
    mix_s,
):
    bins = own_ref.shape[1]
    half = own_ref.shape[2]
    col_rows = 2 * bins + 2 * HALO
    row_rows = bins + 2 * HALO
    rows = col_rows + row_rows
    count = lax.axis_size("blk")
    i = lax.axis_index("blk")
    c = lax.axis_index("chan")
    first = i * bins
    first_col = first + c * (2 * bins)

    def put(start, number, ref, source):
        keep = valid_ref[start : start + number, :] != 0
        for part in range(2):
            for at in range(0, half, 128):
                h_s[start : start + number, part * half + at : part * half + at + 128] = jnp.where(
                    keep, ref[part, source : source + number, at : at + 128].astype(F32), 0.0
                )

    tail = bins - HALO
    put(0, HALO, r1_ref, tail)
    put(col_rows + HALO, bins, own_ref, 0)

    @pl.when(c == 0)
    def _():
        put(HALO, bins, own_ref, 0)
        put(HALO + bins, bins, s1_ref, 0)
        put(HALO + 2 * bins, HALO, r2_ref, 0)
        put(col_rows, HALO, r1_ref, tail)
        put(col_rows + HALO + bins, HALO, s1_ref, 0)

    @pl.when(c == 1)
    def _():
        put(HALO, bins, r2_ref, 0)
        put(HALO + bins, bins, r3_ref, 0)
        put(HALO + 2 * bins, HALO, s3_ref, 0)
        put(col_rows, HALO, s1_ref, tail)
        put(col_rows + HALO + bins, HALO, r1_ref, 0)

    place = lax.broadcasted_iota(jnp.int32, (rows, 1), 0)
    bin_index = jnp.where(
        place < col_rows, first_col - HALO + place, first - HALO - col_rows + place
    )
    inside = (bin_index >= 0) & (bin_index < count * bins)

    for layer in range(CONV1):
        e = 2 ** (layer + 1)
        hidden = h_s[...]
        taps = [
            (hidden if t == 1 else pltpu.roll(hidden, ((1 - t) * e) % rows, axis=0)).astype(BF16)
            for t in range(3)
        ]
        for at, (w_ref, side) in enumerate(((w_own_ref, c), (w_oth_ref, 1 - c))):
            q = jnp.dot(taps[0], w_ref[layer, 0], preferred_element_type=F32)
            q = q + jnp.dot(taps[1], w_ref[layer, 1], preferred_element_type=F32)
            q = q + jnp.dot(taps[2], w_ref[layer, 2], preferred_element_type=F32)
            lanes = pl.ds(pl.multiple_of(side * half, half), half)
            bias = side_ref[1 + layer : 2 + layer, :] if at else small_ref[layer : layer + 1, :]
            new = (h_s[:, lanes] + jnp.maximum(q + bias, 0.0)).astype(BF16).astype(F32)
            h_s[:, lanes] = jnp.where(inside, new, 0.0)

    proj = jnp.dot(h_s[...].astype(BF16), pw_ref[...], preferred_element_type=F32)
    proj = (proj + small_ref[2:3, : 2 * F2]).astype(BF16).astype(F32)

    minus = F32(-jnp.inf)
    low = lax.broadcasted_iota(jnp.int32, (1, 2 * F2), 1) < F2
    pcol = proj[:col_rows]
    pcol = jnp.where(low, pltpu.roll(pcol, F2, axis=1), pcol)
    shifted = [
        pltpu.roll(pcol, col_rows - HALO - (r - 1) * D2, axis=0)[: 2 * bins] for r in range(3)
    ]
    tiles = [
        jnp.where(low, shifted[0], shifted[1]),
        jnp.where(low, shifted[2], shifted[0]),
        jnp.where(low, shifted[1], shifted[2]),
    ]
    tiled = jnp.concatenate(tiles, axis=1)
    col_first, col_mid, col_last = [
        (tiled + col_mask_ref[at]).astype(BF16).reshape(2 * bins // 16, 16, 6 * F2)
        for at in range(3)
    ]
    col_centre = shifted[1].astype(BF16).reshape(2 * bins // 16, 16, 2 * F2)

    prow = proj[col_rows:]
    prow = jnp.where(low, prow, pltpu.roll(prow, F2, axis=1))
    prow = jnp.where(valid_ref[col_rows:, :] != 0, prow, minus)
    prow_next = pltpu.roll(prow, row_rows - D2, axis=0)
    pa6_s[:, : 2 * F2] = prow
    pa6_s[:, 2 * F2 : 4 * F2] = jnp.where(low, prow, prow_next)
    pa6_s[:, 4 * F2 :] = prow_next

    groups = bins // 8
    per_dot = x_s.shape[0] // (2 * bins)
    zero = jnp.zeros((), BF16)
    bias4 = side_ref[0:1, :]
    for v in range(2):
        for start in range(0, groups, per_dot):
            for slot in range(2 * start, 2 * (start + per_dot) + 1):
                at = HALO - D2 + v + 4 * slot
                row = jnp.broadcast_to(pa6_s[at : at + 1, :], (16, 6 * F2)).astype(BF16)
                cols = col_first if slot == 0 else col_last if slot == 2 * groups else col_mid
                value = jnp.maximum(row[None] + cols, zero).reshape(2 * bins, 6 * F2)
                for s in range(3):
                    if (slot - s) % 2 == 0 and start <= (slot - s) // 2 < start + per_dot:
                        at_row = ((slot - s) // 2 - start) * 2 * bins
                        x_s[at_row : at_row + 2 * bins, s * 6 * F2 : (s + 1) * 6 * F2] = value
            y = jnp.dot(x_s[...], wbig_ref[...], preferred_element_type=F32)
            y = jnp.maximum(y + bias4, 0.0)
            for group in range(start, start + per_dot):
                at = HALO + v + 8 * group
                parts = []
                for k in range(2):
                    row = pa6_s[at + 4 * k : at + 4 * k + 1, 2 * F2 : 4 * F2]
                    row = jnp.broadcast_to(row, (16, 2 * F2)).astype(BF16)
                    parts.append(
                        jnp.maximum(row[None] + col_centre, zero).reshape(2 * bins, 2 * F2)
                    )
                centre = jnp.concatenate(parts, axis=1).astype(F32)
                at_row = (group - start) * 2 * bins
                mixed = y[at_row : at_row + 2 * bins] + centre
                mix_s[group, :, v * 4 * F2 : (v + 1) * 4 * F2] = mixed.astype(BF16)

    lane_live = small_ref[2:3, 2 * F2 :] != 0
    for group in range(groups):
        value = lax.dot_general(
            head_ref[...], mix_s[group], (((1,), (1,)), ((), ())), preferred_element_type=F32
        )[:8]
        at = col_rows + HALO + 8 * group
        out_ref[8 * group : 8 * group + 8, :] = jnp.where(
            lane_live & (valid_ref[at : at + 8, :] != 0), value, 0.0
        )


def local(
    features,
    chrom_len,
    band_mask,
    conv_weight,
    conv_bias,
    proj_weight,
    proj_bias,
    map_weight,
    map_bias,
    head_weight,
):
    bins, half = features.shape
    own = lax.all_gather(features, "chan", axis=0)
    r2 = blk_permute(own, 2, 2)
    r1 = blk_permute(own, -1, 1)
    r3 = blk_permute(own, 4, 3)
    s1 = chan_swap(r1)
    s3 = chan_swap(r3)
    w_oth = chan_swap(conv_weight)

    rows = 3 * bins + 4 * HALO
    half_out = map_bias.shape[0]
    vmem = pl.BlockSpec(memory_space=pltpu.VMEM)
    anywhere = pl.BlockSpec(memory_space=pl.ANY)
    params = pltpu.CompilerParams(vmem_limit_bytes=24 * 1024 * 1024)
    packed, col_mask, valid, small, w_own, pw = pl.pallas_call(
        pack_kernel,
        out_shape=[
            jax.ShapeDtypeStruct((9 * half_out, 2 * F2), BF16),
            jax.ShapeDtypeStruct((3, 2 * bins, 6 * F2), F32),
            jax.ShapeDtypeStruct((rows, 2 * F2), F32),
            jax.ShapeDtypeStruct((8, half), F32),
            jax.ShapeDtypeStruct(conv_weight.shape, BF16),
            jax.ShapeDtypeStruct(proj_weight.shape, BF16),
        ],
        in_specs=[anywhere] * 10,
        out_specs=[vmem] * 6,
        scratch_shapes=[
            pltpu.VMEM((1, 1), jnp.int32),
            pltpu.VMEM(band_mask.shape[::-1], jnp.int32),
            pltpu.VMEM(map_weight.shape, BF16),
            pltpu.VMEM((1, half_out), BF16),
            pltpu.VMEM((1, half_out), BF16),
            pltpu.VMEM(conv_bias.shape, BF16),
            pltpu.VMEM((1, 2 * F2), BF16),
            pltpu.VMEM((32, 2 * F2), F32),
            pltpu.SemaphoreType.DMA((9,)),
        ],
        compiler_params=params,
    )(
        own,
        chrom_len[None],
        band_mask.T,
        map_weight,
        map_bias[None],
        head_weight[None],
        conv_bias,
        proj_bias[None],
        conv_weight,
        proj_weight,
    )
    prepared = pl.pallas_call(
        prep_kernel,
        out_shape=[
            jax.ShapeDtypeStruct((18 * F2, 4 * F2), BF16),
            jax.ShapeDtypeStruct((8, half), F32),
            jax.ShapeDtypeStruct((16, 8 * F2), BF16),
        ],
        in_specs=[vmem] * 2,
        out_specs=[vmem] * 3,
        scratch_shapes=[
            pltpu.VMEM((4 * F2, 18 * F2), F32),
            pltpu.VMEM((9, F2, F2), F32),
        ],
        compiler_params=params,
    )(packed, chan_swap(packed))
    return pl.pallas_call(
        contact_kernel,
        out_shape=jax.ShapeDtypeStruct((bins, 2 * bins), F32),
        in_specs=[vmem] * 15,
        out_specs=vmem,
        scratch_shapes=[
            pltpu.VMEM((rows, 2 * half), F32),
            pltpu.VMEM((bins + 2 * HALO, 6 * F2), F32),
            pltpu.VMEM((4 * 2 * bins, 18 * F2), BF16),
            pltpu.VMEM((bins // 8, 2 * bins, 8 * F2), BF16),
        ],
        compiler_params=params,
    )(own, r1, r2, r3, s1, s3, w_own, w_oth, pw, col_mask, valid, small, *prepared)


def solution(mesh):
    return jax.shard_map(
        local,
        mesh=mesh,
        in_specs=(
            P(("dp", "blk"), "chan"),
            P("dp"),
            P("dp", None),
            P(None, None, None, "chan"),
            P(None, "chan"),
            P(),
            P(),
            P(None, None, "chan", None),
            P("chan"),
            P("chan"),
        ),
        out_specs=P(("dp", "blk"), "chan"),
        check_vma=False,
    )
```

```python
import jax
import jax.numpy as jnp
from jax import lax
from jax.experimental import pallas as pl
from jax.experimental.pallas import tpu as pltpu
from jax.sharding import PartitionSpec as P

F2 = 64
BAND = 3
CONV1 = 2
D2 = 2
HALO = 16
F32 = jnp.float32
BF16 = jnp.bfloat16


def chan_swap(value):
    return lax.ppermute(value, "chan", [(0, 1), (1, 0)])


def ring_permute(value, offset_0, offset_1):
    count = lax.axis_size("blk")
    pairs = []
    for i in range(count):
        pairs.append((((i + offset_0) % count) * 2, i * 2))
        pairs.append((((i + offset_1) % count) * 2 + 1, i * 2 + 1))
    return lax.ppermute(value, ("blk", "chan"), pairs)


def line_permute(value, step):
    count = lax.axis_size("blk")
    pairs = []
    for i in range(count):
        pairs.append(((i - step) * 2 if i >= step else i * 2 + 1, i * 2))
        pairs.append(((i + step) * 2 + 1 if i + step < count else i * 2, i * 2 + 1))
    return lax.ppermute(value, ("blk", "chan"), pairs)


def pack_kernel(
    length_ref,
    own_any,
    mask_any,
    mw_any,
    mb_any,
    hw_any,
    cb_any,
    pb_any,
    w_any,
    pw_any,
    packed_ref,
    col_mask_ref,
    valid_ref,
    small_ref,
    w_ref,
    pw_ref,
    mask_s,
    mw_s,
    mb_s,
    hw_s,
    cb_s,
    pb_s,
    extra_s,
    sems,
):
    pairs = (
        (mask_any, mask_s),
        (mw_any, mw_s),
        (mb_any, mb_s),
        (hw_any, hw_s),
        (cb_any, cb_s),
        (pb_any, pb_s),
        (w_any, w_ref),
        (pw_any, pw_ref),
    )
    copies = [
        pltpu.make_async_copy(source, target, sems.at[at])
        for at, (source, target) in enumerate(pairs)
    ]
    for copy in copies:
        copy.start()
    for copy in copies[:6]:
        copy.wait()

    rows = valid_ref.shape[0]
    columns = col_mask_ref.shape[1]
    bins = columns // 2
    half = mw_any.shape[2]
    col_rows = columns + 2 * HALO
    count = lax.axis_size("blk")
    i = lax.axis_index("blk")
    c = lax.axis_index("chan")
    first = i * bins
    first_col = first + c * columns
    length = length_ref[0]

    extra_s[...] = jnp.zeros_like(extra_s)
    biases = cb_s[...].astype(F32)
    for layer in range(CONV1):
        for quarter in range(4):
            at = 4 * layer + quarter
            extra_s[at : at + 1, :F2] = biases[layer : layer + 1, quarter * F2 : (quarter + 1) * F2]
    extra_s[8:9, :half] = mb_s[...].astype(F32)
    extra_s[9:10, :half] = hw_s[...].astype(F32)
    extra = pltpu.roll(extra_s[...], F2, axis=1)
    for s in range(3):
        for r in range(3):
            at = (3 * s + r) * half
            packed_ref[at : at + half, :F2] = mw_s[s, r]
    packed_ref[:32, F2:] = extra[:, F2:].astype(BF16)

    minus = F32(-jnp.inf)
    block = lax.broadcasted_iota(jnp.int32, (BAND + 1, count), 1)

    def live_at(y, variant):
        at_row = jnp.sum(jnp.where(block == i + variant, mask_s[...], 0), axis=1, keepdims=True)
        offset = lax.broadcasted_iota(jnp.int32, (BAND + 1, 1), 0)

        def entry(u):
            return jnp.sum(
                jnp.where(offset == 2 * c + u - variant, at_row, 0), axis=0, keepdims=True
            )

        value = jnp.where(
            y < 0,
            entry(-1),
            jnp.where(y < bins, entry(0), jnp.where(y < columns, entry(1), entry(2))),
        )
        column = first_col + y
        return (value != 0) & (column >= 0) & (column < length)

    b_index = lax.broadcasted_iota(jnp.int32, (columns, 2 * F2), 0)
    low = lax.broadcasted_iota(jnp.int32, (columns, 2 * F2), 1) < F2
    masks = {}
    for variant in (-1, 0, 1):
        for r in range(3):
            masks[variant, r] = jnp.where(
                live_at(b_index + (r - 1) * D2, variant), 0.0, minus
            )
    for at, (v0, v1) in enumerate(((-1, 0), (0, 0), (0, 1))):
        col_mask_ref[at, :, : 2 * F2] = jnp.where(low, masks[v0, 0], masks[v0, 1])
        col_mask_ref[at, :, 2 * F2 : 4 * F2] = jnp.where(low, masks[v0, 2], masks[v1, 0])
        col_mask_ref[at, :, 4 * F2 :] = jnp.where(low, masks[v1, 1], masks[v1, 2])

    place = lax.broadcasted_iota(jnp.int32, (rows, 2 * F2), 0)
    bin_index = jnp.where(
        place < col_rows, first_col - HALO + place, first - HALO - col_rows + place
    )
    valid_ref[...] = jnp.where((bin_index >= 0) & (bin_index < length), 1.0, 0.0)

    small_ref[0:2, :] = cb_s[...].astype(F32)
    small_ref[2:3, : 2 * F2] = pb_s[...].astype(F32)
    small_ref[2:3, 2 * F2 :] = jnp.where(
        live_at(lax.broadcasted_iota(jnp.int32, (1, columns), 1), 0), 1.0, 0.0
    )
    for copy in copies[6:]:
        copy.wait()


def prep_kernel(own_ref, oth_ref, wbig_ref, side_ref, head_ref, wt_s, taps_s):
    half = own_ref.shape[0] // 9
    c = lax.axis_index("chan")

    for source, side in ((own_ref, c), (oth_ref, 1 - c)):
        at = pl.ds(pl.multiple_of(side * half, half), half)
        for tap in range(9):
            taps_s[tap, at, :] = source[tap * half : (tap + 1) * half, :F2].astype(F32)
    blank = jnp.zeros((F2, F2), F32)
    for j in range(4):
        pieces = []
        for m in range(6):
            for r in range(3):
                pieces.append(taps_s[3 * (m - j) + r] if 0 <= m - j < 3 else blank)
        for tile in range(9):
            wt_s[j * F2 : (j + 1) * F2, tile * 2 * F2 : (tile + 1) * 2 * F2] = jnp.concatenate(
                pieces[2 * tile : 2 * tile + 2], axis=1
            )
    wbig_ref[...] = wt_s[...].T.astype(BF16)

    def spread(row, repeats):
        o = lax.broadcasted_iota(jnp.int32, (2 * F2, repeats * F2), 0)
        lane = lax.broadcasted_iota(jnp.int32, (2 * F2, repeats * F2), 1) % F2
        total = jnp.zeros((16, repeats * F2), F32)
        for ref, side in ((own_ref, c), (oth_ref, 1 - c)):
            pick = ((lane == side * half + o - F2) & (o >= F2) & (o < F2 + half)).astype(BF16)
            value = ref[:16, :].astype(F32)[row : row + 1]
            value = jnp.broadcast_to(value, (16, 2 * F2)).astype(BF16)
            total = total + jnp.dot(value, pick, preferred_element_type=F32)
        return total

    q = lax.broadcasted_iota(jnp.int32, (16, 8 * F2), 0)
    k = lax.broadcasted_iota(jnp.int32, (16, 8 * F2), 1)
    head_ref[...] = jnp.where(
        q == 2 * ((k % (4 * F2)) // F2) + k // (4 * F2), spread(9, 8), 0.0
    ).astype(BF16)
    side_ref[0:1, :] = spread(8, 4)[:1]
    other = oth_ref[:16, :].astype(F32)
    other = pltpu.roll(other, F2, axis=1)
    for layer in range(CONV1):
        for quarter in range(4):
            at = 4 * layer + quarter
            side_ref[1 + layer : 2 + layer, quarter * F2 : (quarter + 1) * F2] = other[
                at : at + 1, :F2
            ]


def contact_kernel(
    own_ref,
    r1_ref,
    r2_ref,
    r3_ref,
    s1_ref,
    s2_ref,
    s3_ref,
    w_own_ref,
    w_oth_ref,
    pw_ref,
    col_mask_ref,
    valid_ref,
    small_ref,
    wbig_ref,
    side_ref,
    head_ref,
    out_ref,
    h_s,
    pa6_s,
    x_s,
    mix_s,
):
    bins = own_ref.shape[1]
    half = own_ref.shape[2]
    col_rows = 2 * bins + 2 * HALO
    row_rows = bins + 2 * HALO
    rows = col_rows + row_rows
    count = lax.axis_size("blk")
    i = lax.axis_index("blk")
    c = lax.axis_index("chan")
    first = i * bins
    first_col = first + c * (2 * bins)

    def put(start, number, ref, source):
        keep = valid_ref[start : start + number, :] != 0
        for part in range(2):
            for at in range(0, half, 128):
                h_s[start : start + number, part * half + at : part * half + at + 128] = jnp.where(
                    keep, ref[part, source : source + number, at : at + 128].astype(F32), 0.0
                )

    tail = bins - HALO
    put(0, HALO, r1_ref, tail)
    put(col_rows + HALO, bins, own_ref, 0)

    @pl.when(c == 0)
    def _():
        put(HALO, bins, own_ref, 0)
        put(HALO + bins, bins, s1_ref, 0)
        put(HALO + 2 * bins, HALO, s2_ref, 0)
        put(col_rows, HALO, r1_ref, tail)
        put(col_rows + HALO + bins, HALO, s1_ref, 0)

    @pl.when(c == 1)
    def _():
        put(HALO, bins, r2_ref, 0)
        put(HALO + bins, bins, r3_ref, 0)
        put(HALO + 2 * bins, HALO, s3_ref, 0)
        put(col_rows, HALO, s1_ref, tail)
        put(col_rows + HALO + bins, HALO, r1_ref, 0)

    place = lax.broadcasted_iota(jnp.int32, (rows, 1), 0)
    bin_index = jnp.where(
        place < col_rows, first_col - HALO + place, first - HALO - col_rows + place
    )
    inside = (bin_index >= 0) & (bin_index < count * bins)

    for layer in range(CONV1):
        e = 2 ** (layer + 1)
        hidden = h_s[...]
        taps = [
            (hidden if t == 1 else pltpu.roll(hidden, ((1 - t) * e) % rows, axis=0)).astype(BF16)
            for t in range(3)
        ]
        for at, (w_ref, side) in enumerate(((w_own_ref, c), (w_oth_ref, 1 - c))):
            q = jnp.dot(taps[0], w_ref[layer, 0], preferred_element_type=F32)
            q = q + jnp.dot(taps[1], w_ref[layer, 1], preferred_element_type=F32)
            q = q + jnp.dot(taps[2], w_ref[layer, 2], preferred_element_type=F32)
            lanes = pl.ds(pl.multiple_of(side * half, half), half)
            bias = side_ref[1 + layer : 2 + layer, :] if at else small_ref[layer : layer + 1, :]
            new = (h_s[:, lanes] + jnp.maximum(q + bias, 0.0)).astype(BF16).astype(F32)
            h_s[:, lanes] = jnp.where(inside, new, 0.0)

    proj = jnp.dot(h_s[...].astype(BF16), pw_ref[...], preferred_element_type=F32)
    proj = (proj + small_ref[2:3, : 2 * F2]).astype(BF16).astype(F32)

    minus = F32(-jnp.inf)
    low = lax.broadcasted_iota(jnp.int32, (1, 2 * F2), 1) < F2
    pcol = proj[:col_rows]
    pcol = jnp.where(low, pltpu.roll(pcol, F2, axis=1), pcol)
    shifted = [
        pltpu.roll(pcol, col_rows - HALO - (r - 1) * D2, axis=0)[: 2 * bins] for r in range(3)
    ]
    tiles = [
        jnp.where(low, shifted[0], shifted[1]),
        jnp.where(low, shifted[2], shifted[0]),
        jnp.where(low, shifted[1], shifted[2]),
    ]
    tiled = jnp.concatenate(tiles, axis=1)
    col_first, col_mid, col_last = [
        (tiled + col_mask_ref[at]).astype(BF16).reshape(2 * bins // 16, 16, 6 * F2)
        for at in range(3)
    ]
    col_centre = shifted[1].astype(BF16).reshape(2 * bins // 16, 16, 2 * F2)

    prow = proj[col_rows:]
    prow = jnp.where(low, prow, pltpu.roll(prow, F2, axis=1))
    prow = jnp.where(valid_ref[col_rows:, :] != 0, prow, minus)
    prow_next = pltpu.roll(prow, row_rows - D2, axis=0)
    pa6_s[:, : 2 * F2] = prow
    pa6_s[:, 2 * F2 : 4 * F2] = jnp.where(low, prow, prow_next)
    pa6_s[:, 4 * F2 :] = prow_next

    groups = bins // 8
    per_dot = x_s.shape[0] // (2 * bins)
    zero = jnp.zeros((), BF16)
    bias4 = side_ref[0:1, :]
    for v in range(2):
        for start in range(0, groups, per_dot):
            for slot in range(2 * start, 2 * (start + per_dot) + 1):
                at = HALO - D2 + v + 4 * slot
                row = jnp.broadcast_to(pa6_s[at : at + 1, :], (16, 6 * F2)).astype(BF16)
                cols = col_first if slot == 0 else col_last if slot == 2 * groups else col_mid
                value = jnp.maximum(row[None] + cols, zero).reshape(2 * bins, 6 * F2)
                for s in range(3):
                    if (slot - s) % 2 == 0 and start <= (slot - s) // 2 < start + per_dot:
                        at_row = ((slot - s) // 2 - start) * 2 * bins
                        x_s[at_row : at_row + 2 * bins, s * 6 * F2 : (s + 1) * 6 * F2] = value
            y = jnp.dot(x_s[...], wbig_ref[...], preferred_element_type=F32)
            y = jnp.maximum(y + bias4, 0.0)
            for group in range(start, start + per_dot):
                at = HALO + v + 8 * group
                parts = []
                for k in range(2):
                    row = pa6_s[at + 4 * k : at + 4 * k + 1, 2 * F2 : 4 * F2]
                    row = jnp.broadcast_to(row, (16, 2 * F2)).astype(BF16)
                    parts.append(
                        jnp.maximum(row[None] + col_centre, zero).reshape(2 * bins, 2 * F2)
                    )
                centre = jnp.concatenate(parts, axis=1).astype(F32)
                at_row = (group - start) * 2 * bins
                mixed = y[at_row : at_row + 2 * bins] + centre
                mix_s[group, :, v * 4 * F2 : (v + 1) * 4 * F2] = mixed.astype(BF16)

    lane_live = small_ref[2:3, 2 * F2 :] != 0
    for group in range(groups):
        value = lax.dot_general(
            head_ref[...], mix_s[group], (((1,), (1,)), ((), ())), preferred_element_type=F32
        )[:8]
        at = col_rows + HALO + 8 * group
        out_ref[8 * group : 8 * group + 8, :] = jnp.where(
            lane_live & (valid_ref[at : at + 8, :] != 0), value, 0.0
        )


def local(
    features,
    chrom_len,
    band_mask,
    conv_weight,
    conv_bias,
    proj_weight,
    proj_bias,
    map_weight,
    map_bias,
    head_weight,
):
    bins, half = features.shape
    own = lax.all_gather(features, "chan", axis=0)
    r1 = line_permute(own, 1)
    r2 = line_permute(own, 2)
    r3 = ring_permute(own, 4, 3)
    s1 = chan_swap(r1)
    s2 = chan_swap(r2)
    s3 = chan_swap(r3)
    w_in, own = lax.optimization_barrier((conv_weight, own))
    w_oth = chan_swap(w_in)

    rows = 3 * bins + 4 * HALO
    half_out = map_bias.shape[0]
    vmem = pl.BlockSpec(memory_space=pltpu.VMEM)
    anywhere = pl.BlockSpec(memory_space=pltpu.HBM)
    params = pltpu.CompilerParams(vmem_limit_bytes=24 * 1024 * 1024)
    packed, col_mask, valid, small, w_own, pw = pl.pallas_call(
        pack_kernel,
        out_shape=[
            jax.ShapeDtypeStruct((9 * half_out, 2 * F2), BF16),
            jax.ShapeDtypeStruct((3, 2 * bins, 6 * F2), F32),
            jax.ShapeDtypeStruct((rows, 2 * F2), F32),
            jax.ShapeDtypeStruct((8, half), F32),
            jax.ShapeDtypeStruct(conv_weight.shape, BF16),
            jax.ShapeDtypeStruct(proj_weight.shape, BF16),
        ],
        in_specs=[pl.BlockSpec(memory_space=pltpu.SMEM)] + [anywhere] * 9,
        out_specs=[vmem] * 6,
        scratch_shapes=[
            pltpu.VMEM(band_mask.shape[::-1], jnp.int32),
            pltpu.VMEM(map_weight.shape, BF16),
            pltpu.VMEM((1, half_out), BF16),
            pltpu.VMEM((1, half_out), BF16),
            pltpu.VMEM(conv_bias.shape, BF16),
            pltpu.VMEM((1, 2 * F2), BF16),
            pltpu.VMEM((32, 2 * F2), F32),
            pltpu.SemaphoreType.DMA((8,)),
        ],
        compiler_params=params,
    )(
        chrom_len,
        own,
        *[
            pltpu.with_memory_space_constraint(value, pltpu.HBM)
            for value in (
                band_mask.T,
                map_weight,
                map_bias[None],
                head_weight[None],
                conv_bias,
                proj_bias[None],
                conv_weight,
                proj_weight,
            )
        ],
    )
    prepared = pl.pallas_call(
        prep_kernel,
        out_shape=[
            jax.ShapeDtypeStruct((18 * F2, 4 * F2), BF16),
            jax.ShapeDtypeStruct((8, half), F32),
            jax.ShapeDtypeStruct((16, 8 * F2), BF16),
        ],
        in_specs=[vmem] * 2,
        out_specs=[vmem] * 3,
        scratch_shapes=[
            pltpu.VMEM((4 * F2, 18 * F2), F32),
            pltpu.VMEM((9, F2, F2), F32),
        ],
        compiler_params=params,
    )(packed, chan_swap(packed))
    return pl.pallas_call(
        contact_kernel,
        out_shape=jax.ShapeDtypeStruct((bins, 2 * bins), F32),
        in_specs=[vmem] * 16,
        out_specs=vmem,
        scratch_shapes=[
            pltpu.VMEM((rows, 2 * half), F32),
            pltpu.VMEM((bins + 2 * HALO, 6 * F2), F32),
            pltpu.VMEM((4 * 2 * bins, 18 * F2), BF16),
            pltpu.VMEM((bins // 8, 2 * bins, 8 * F2), BF16),
        ],
        compiler_params=params,
    )(own, r1, r2, r3, s1, s2, s3, w_own, w_oth, pw, col_mask, valid, small, *prepared)


def solution(mesh):
    return jax.shard_map(
        local,
        mesh=mesh,
        in_specs=(
            P(("dp", "blk"), "chan"),
            P("dp"),
            P("dp", None),
            P(None, None, None, "chan"),
            P(None, "chan"),
            P(),
            P(),
            P(None, None, "chan", None),
            P("chan"),
            P("chan"),
        ),
        out_specs=P(("dp", "blk"), "chan"),
        check_vma=False,
    )
```

```python
import jax
import jax.numpy as jnp
from jax import lax
from jax.experimental import pallas as pl
from jax.experimental.pallas import tpu as pltpu
from jax.sharding import PartitionSpec as P

F2 = 64
BAND = 3
CONV1 = 2
D2 = 2
HALO = 16
F32 = jnp.float32
BF16 = jnp.bfloat16


def chan_swap(value):
    return lax.ppermute(value, "chan", [(0, 1), (1, 0)])


def ring_permute(value, offset_0, offset_1):
    count = lax.axis_size("blk")
    pairs = []
    for i in range(count):
        pairs.append((((i + offset_0) % count) * 2, i * 2))
        pairs.append((((i + offset_1) % count) * 2 + 1, i * 2 + 1))
    return lax.ppermute(value, ("blk", "chan"), pairs)


def line_permute(value, step):
    count = lax.axis_size("blk")
    pairs = []
    for i in range(count):
        pairs.append(((i - step) * 2 if i >= step else i * 2 + 1, i * 2))
        pairs.append(((i + step) * 2 + 1 if i + step < count else i * 2, i * 2 + 1))
    return lax.ppermute(value, ("blk", "chan"), pairs)


def pack_kernel(
    own_any,
    mask_any,
    mw_any,
    mb_any,
    hw_any,
    cb_any,
    pb_any,
    own_ref,
    mask_ref,
    packed_ref,
    small_ref,
    mw_s,
    mb_s,
    hw_s,
    cb_s,
    pb_s,
    extra_s,
    sems,
):
    pairs = (
        (mw_any, mw_s),
        (cb_any, cb_s),
        (mb_any, mb_s),
        (hw_any, hw_s),
        (pb_any, pb_s),
        (mask_any, mask_ref),
        (own_any, own_ref),
    )
    copies = [
        pltpu.make_async_copy(source, target, sems.at[at])
        for at, (source, target) in enumerate(pairs)
    ]
    for copy in copies:
        copy.start()
    extra_s[...] = jnp.zeros_like(extra_s)
    for copy in copies[:5]:
        copy.wait()

    half = mw_any.shape[2]
    biases = cb_s[...].astype(F32)
    for layer in range(CONV1):
        for quarter in range(4):
            at = 4 * layer + quarter
            extra_s[at : at + 1, :F2] = biases[layer : layer + 1, quarter * F2 : (quarter + 1) * F2]
    extra_s[8:9, :half] = mb_s[...].astype(F32)
    extra_s[9:10, :half] = hw_s[...].astype(F32)
    extra = pltpu.roll(extra_s[...], F2, axis=1)
    for s in range(3):
        for r in range(3):
            at = (3 * s + r) * half
            packed_ref[at : at + half, :F2] = mw_s[s, r]
    packed_ref[:32, F2:] = extra[:, F2:].astype(BF16)
    small_ref[0:2, :] = biases
    small_ref[2:3, : 2 * F2] = pb_s[...].astype(F32)
    for copy in copies[5:]:
        copy.wait()


def prep_kernel(
    length_ref,
    mask_ref,
    own_ref,
    oth_ref,
    col_mask_ref,
    valid_ref,
    wbig_ref,
    side_ref,
    head_ref,
    wt_s,
    taps_s,
):
    half = own_ref.shape[0] // 9
    rows = valid_ref.shape[0]
    columns = col_mask_ref.shape[1]
    bins = columns // 2
    col_rows = columns + 2 * HALO
    count = lax.axis_size("blk")
    i = lax.axis_index("blk")
    c = lax.axis_index("chan")
    first = i * bins
    first_col = first + c * columns
    length = length_ref[0]

    for source, side in ((own_ref, c), (oth_ref, 1 - c)):
        at = pl.ds(pl.multiple_of(side * half, half), half)
        for tap in range(9):
            taps_s[tap, at, :] = source[tap * half : (tap + 1) * half, :F2].astype(F32)
    blank = jnp.zeros((F2, F2), F32)
    for j in range(4):
        pieces = []
        for m in range(6):
            for r in range(3):
                pieces.append(taps_s[3 * (m - j) + r] if 0 <= m - j < 3 else blank)
        for tile in range(9):
            wt_s[j * F2 : (j + 1) * F2, tile * 2 * F2 : (tile + 1) * 2 * F2] = jnp.concatenate(
                pieces[2 * tile : 2 * tile + 2], axis=1
            )
    wbig_ref[...] = wt_s[...].T.astype(BF16)

    def spread(row, repeats):
        o = lax.broadcasted_iota(jnp.int32, (2 * F2, repeats * F2), 0)
        lane = lax.broadcasted_iota(jnp.int32, (2 * F2, repeats * F2), 1) % F2
        total = jnp.zeros((16, repeats * F2), F32)
        for ref, side in ((own_ref, c), (oth_ref, 1 - c)):
            pick = ((lane == side * half + o - F2) & (o >= F2) & (o < F2 + half)).astype(BF16)
            value = ref[:16, :].astype(F32)[row : row + 1]
            value = jnp.broadcast_to(value, (16, 2 * F2)).astype(BF16)
            total = total + jnp.dot(value, pick, preferred_element_type=F32)
        return total

    q = lax.broadcasted_iota(jnp.int32, (16, 8 * F2), 0)
    k = lax.broadcasted_iota(jnp.int32, (16, 8 * F2), 1)
    head_ref[...] = jnp.where(
        q == 2 * ((k % (4 * F2)) // F2) + k // (4 * F2), spread(9, 8), 0.0
    ).astype(BF16)
    side_ref[0:1, :] = spread(8, 4)[:1]
    other = oth_ref[:16, :].astype(F32)
    other = pltpu.roll(other, F2, axis=1)
    for layer in range(CONV1):
        for quarter in range(4):
            at = 4 * layer + quarter
            side_ref[1 + layer : 2 + layer, quarter * F2 : (quarter + 1) * F2] = other[
                at : at + 1, :F2
            ]

    minus = F32(-jnp.inf)
    block = lax.broadcasted_iota(jnp.int32, (BAND + 1, count), 1)

    def live_at(y, variant):
        at_row = jnp.sum(jnp.where(block == i + variant, mask_ref[...], 0), axis=1, keepdims=True)
        offset = lax.broadcasted_iota(jnp.int32, (BAND + 1, 1), 0)

        def entry(u):
            return jnp.sum(
                jnp.where(offset == 2 * c + u - variant, at_row, 0), axis=0, keepdims=True
            )

        value = jnp.where(
            y < 0,
            entry(-1),
            jnp.where(y < bins, entry(0), jnp.where(y < columns, entry(1), entry(2))),
        )
        column = first_col + y
        return (value != 0) & (column >= 0) & (column < length)

    b_index = lax.broadcasted_iota(jnp.int32, (columns, 2 * F2), 0)
    low = lax.broadcasted_iota(jnp.int32, (columns, 2 * F2), 1) < F2
    masks = {}
    for variant in (-1, 0, 1):
        for r in range(3):
            masks[variant, r] = jnp.where(
                live_at(b_index + (r - 1) * D2, variant), 0.0, minus
            )
    for at, (v0, v1) in enumerate(((-1, 0), (0, 0), (0, 1))):
        col_mask_ref[at, :, : 2 * F2] = jnp.where(low, masks[v0, 0], masks[v0, 1])
        col_mask_ref[at, :, 2 * F2 : 4 * F2] = jnp.where(low, masks[v0, 2], masks[v1, 0])
        col_mask_ref[at, :, 4 * F2 :] = jnp.where(low, masks[v1, 1], masks[v1, 2])

    place = lax.broadcasted_iota(jnp.int32, (rows, 2 * F2), 0)
    bin_index = jnp.where(
        place < col_rows, first_col - HALO + place, first - HALO - col_rows + place
    )
    valid_ref[...] = jnp.where((bin_index >= 0) & (bin_index < length), 1.0, 0.0)

    side_ref[3:4, : 2 * F2] = jnp.where(
        live_at(lax.broadcasted_iota(jnp.int32, (1, columns), 1), 0), 1.0, 0.0
    )


def contact_kernel(
    own_ref,
    r2_ref,
    s2_ref,
    r1_ref,
    s1_ref,
    r3_ref,
    s3_ref,
    w_own_ref,
    pw_ref,
    w_oth_ref,
    small_ref,
    col_mask_ref,
    valid_ref,
    wbig_ref,
    side_ref,
    head_ref,
    out_ref,
    h_s,
    pa6_s,
    x_s,
    mix_s,
):
    bins = own_ref.shape[1]
    half = own_ref.shape[2]
    col_rows = 2 * bins + 2 * HALO
    row_rows = bins + 2 * HALO
    rows = col_rows + row_rows
    count = lax.axis_size("blk")
    i = lax.axis_index("blk")
    c = lax.axis_index("chan")
    first = i * bins
    first_col = first + c * (2 * bins)

    def put(start, number, ref, source, swapped=0):
        keep = valid_ref[start : start + number, :] != 0
        for part in range(2):
            held = lax.rem(part + c + swapped, 2)
            for at in range(0, half, 128):
                h_s[start : start + number, part * half + at : part * half + at + 128] = jnp.where(
                    keep, ref[held, source : source + number, at : at + 128].astype(F32), 0.0
                )

    tail = bins - HALO
    put(0, HALO, r1_ref, tail)
    put(col_rows + HALO, bins, own_ref, 0)

    @pl.when(c == 0)
    def _():
        put(HALO, bins, own_ref, 0)
        put(HALO + bins, bins, s1_ref, 0, 1)
        put(HALO + 2 * bins, HALO, s2_ref, 0, 1)
        put(col_rows, HALO, r1_ref, tail)
        put(col_rows + HALO + bins, HALO, s1_ref, 0, 1)

    @pl.when(c == 1)
    def _():
        put(HALO, bins, r2_ref, 0)
        put(HALO + bins, bins, r3_ref, 0)
        put(HALO + 2 * bins, HALO, s3_ref, 0, 1)
        put(col_rows, HALO, s1_ref, tail, 1)
        put(col_rows + HALO + bins, HALO, r1_ref, 0)

    place = lax.broadcasted_iota(jnp.int32, (rows, 1), 0)
    bin_index = jnp.where(
        place < col_rows, first_col - HALO + place, first - HALO - col_rows + place
    )
    inside = (bin_index >= 0) & (bin_index < count * bins)

    for layer in range(CONV1):
        e = 2 ** (layer + 1)
        hidden = h_s[...]
        taps = [
            (hidden if t == 1 else pltpu.roll(hidden, ((1 - t) * e) % rows, axis=0)).astype(BF16)
            for t in range(3)
        ]
        for at, (w_ref, side) in enumerate(((w_own_ref, c), (w_oth_ref, 1 - c))):
            q = jnp.dot(taps[0], w_ref[layer, 0], preferred_element_type=F32)
            q = q + jnp.dot(taps[1], w_ref[layer, 1], preferred_element_type=F32)
            q = q + jnp.dot(taps[2], w_ref[layer, 2], preferred_element_type=F32)
            lanes = pl.ds(pl.multiple_of(side * half, half), half)
            bias = side_ref[1 + layer : 2 + layer, :] if at else small_ref[layer : layer + 1, :]
            new = (h_s[:, lanes] + jnp.maximum(q + bias, 0.0)).astype(BF16).astype(F32)
            h_s[:, lanes] = jnp.where(inside, new, 0.0)

    proj = jnp.dot(h_s[...].astype(BF16), pw_ref[...], preferred_element_type=F32)
    proj = (proj + small_ref[2:3, : 2 * F2]).astype(BF16).astype(F32)

    minus = F32(-jnp.inf)
    low = lax.broadcasted_iota(jnp.int32, (1, 2 * F2), 1) < F2
    pcol = proj[:col_rows]
    pcol = jnp.where(low, pltpu.roll(pcol, F2, axis=1), pcol)
    shifted = [
        pltpu.roll(pcol, col_rows - HALO - (r - 1) * D2, axis=0)[: 2 * bins] for r in range(3)
    ]
    tiles = [
        jnp.where(low, shifted[0], shifted[1]),
        jnp.where(low, shifted[2], shifted[0]),
        jnp.where(low, shifted[1], shifted[2]),
    ]
    tiled = jnp.concatenate(tiles, axis=1)
    col_first, col_mid, col_last = [
        (tiled + col_mask_ref[at]).astype(BF16).reshape(2 * bins // 16, 16, 6 * F2)
        for at in range(3)
    ]
    col_centre = shifted[1].astype(BF16).reshape(2 * bins // 16, 16, 2 * F2)

    prow = proj[col_rows:]
    prow = jnp.where(low, prow, pltpu.roll(prow, F2, axis=1))
    prow = jnp.where(valid_ref[col_rows:, :] != 0, prow, minus)
    prow_next = pltpu.roll(prow, row_rows - D2, axis=0)
    pa6_s[:, : 2 * F2] = prow
    pa6_s[:, 2 * F2 : 4 * F2] = jnp.where(low, prow, prow_next)
    pa6_s[:, 4 * F2 :] = prow_next

    groups = bins // 8
    per_dot = x_s.shape[0] // (2 * bins)
    zero = jnp.zeros((), BF16)
    bias4 = side_ref[0:1, :]
    for v in range(2):
        for start in range(0, groups, per_dot):
            for slot in range(2 * start, 2 * (start + per_dot) + 1):
                at = HALO - D2 + v + 4 * slot
                row = jnp.broadcast_to(pa6_s[at : at + 1, :], (16, 6 * F2)).astype(BF16)
                cols = col_first if slot == 0 else col_last if slot == 2 * groups else col_mid
                value = jnp.maximum(row[None] + cols, zero).reshape(2 * bins, 6 * F2)
                for s in range(3):
                    if (slot - s) % 2 == 0 and start <= (slot - s) // 2 < start + per_dot:
                        at_row = ((slot - s) // 2 - start) * 2 * bins
                        x_s[at_row : at_row + 2 * bins, s * 6 * F2 : (s + 1) * 6 * F2] = value
            y = jnp.dot(x_s[...], wbig_ref[...], preferred_element_type=F32)
            y = jnp.maximum(y + bias4, 0.0)
            for group in range(start, start + per_dot):
                at = HALO + v + 8 * group
                parts = []
                for k in range(2):
                    row = pa6_s[at + 4 * k : at + 4 * k + 1, 2 * F2 : 4 * F2]
                    row = jnp.broadcast_to(row, (16, 2 * F2)).astype(BF16)
                    parts.append(
                        jnp.maximum(row[None] + col_centre, zero).reshape(2 * bins, 2 * F2)
                    )
                centre = jnp.concatenate(parts, axis=1).astype(F32)
                at_row = (group - start) * 2 * bins
                mixed = y[at_row : at_row + 2 * bins] + centre
                mix_s[group, :, v * 4 * F2 : (v + 1) * 4 * F2] = mixed.astype(BF16)

    lane_live = side_ref[3:4, : 2 * F2] != 0
    for group in range(groups):
        value = lax.dot_general(
            head_ref[...], mix_s[group], (((1,), (1,)), ((), ())), preferred_element_type=F32
        )[:8]
        at = col_rows + HALO + 8 * group
        out_ref[8 * group : 8 * group + 8, :] = jnp.where(
            lane_live & (valid_ref[at : at + 8, :] != 0), value, 0.0
        )


def local(
    features,
    chrom_len,
    band_mask,
    conv_weight,
    conv_bias,
    proj_weight,
    proj_bias,
    map_weight,
    map_bias,
    head_weight,
):
    bins, half = features.shape
    rows = 3 * bins + 4 * HALO
    half_out = map_bias.shape[0]
    smem = pl.BlockSpec(memory_space=pltpu.SMEM)
    vmem = pl.BlockSpec(memory_space=pltpu.VMEM)
    anywhere = pl.BlockSpec(memory_space=pl.ANY)
    params = pltpu.CompilerParams(vmem_limit_bytes=24 * 1024 * 1024)

    def in_hbm(value):
        return pltpu.with_memory_space_constraint(value, pltpu.HBM)

    other = chan_swap(features)
    own, mask, packed, small = pl.pallas_call(
        pack_kernel,
        out_shape=[
            jax.ShapeDtypeStruct(features.shape, BF16),
            jax.ShapeDtypeStruct(band_mask.shape[::-1], jnp.int32),
            jax.ShapeDtypeStruct((9 * half_out, 2 * F2), BF16),
            jax.ShapeDtypeStruct((8, half), F32),
        ],
        in_specs=[anywhere] * 7,
        out_specs=[vmem] * 4,
        scratch_shapes=[
            pltpu.VMEM(map_weight.shape, BF16),
            pltpu.VMEM((1, half_out), BF16),
            pltpu.VMEM((1, half_out), BF16),
            pltpu.VMEM(conv_bias.shape, BF16),
            pltpu.VMEM((1, 2 * F2), BF16),
            pltpu.VMEM((32, 2 * F2), F32),
            pltpu.SemaphoreType.DMA((7,)),
        ],
        cost_estimate=pl.CostEstimate(flops=4000000000, bytes_accessed=1000000, transcendentals=0),
        compiler_params=params,
    )(
        in_hbm(features),
        in_hbm(band_mask.T),
        in_hbm(map_weight),
        in_hbm(map_bias[None]),
        in_hbm(head_weight[None]),
        in_hbm(conv_bias),
        in_hbm(proj_bias[None]),
    )
    own = jnp.stack([own, other])
    r1 = line_permute(own, 1)
    r2 = line_permute(own, 2)
    r3 = ring_permute(own, 4, 3)
    s1 = chan_swap(r1)
    s2 = chan_swap(r2)
    s3 = chan_swap(r3)
    w_in, own = lax.optimization_barrier((conv_weight, own))
    w_oth = chan_swap(w_in)
    prepared = pl.pallas_call(
        prep_kernel,
        out_shape=[
            jax.ShapeDtypeStruct((3, 2 * bins, 6 * F2), F32),
            jax.ShapeDtypeStruct((rows, 2 * F2), F32),
            jax.ShapeDtypeStruct((18 * F2, 4 * F2), BF16),
            jax.ShapeDtypeStruct((8, half), F32),
            jax.ShapeDtypeStruct((16, 8 * F2), BF16),
        ],
        in_specs=[smem] + [vmem] * 3,
        out_specs=[vmem] * 5,
        scratch_shapes=[
            pltpu.VMEM((4 * F2, 18 * F2), F32),
            pltpu.VMEM((9, F2, F2), F32),
        ],
        compiler_params=params,
    )(chrom_len, mask, packed, chan_swap(packed))
    return pl.pallas_call(
        contact_kernel,
        out_shape=jax.ShapeDtypeStruct((bins, 2 * bins), F32),
        in_specs=[vmem] * 16,
        out_specs=vmem,
        scratch_shapes=[
            pltpu.VMEM((rows, 2 * half), F32),
            pltpu.VMEM((bins + 2 * HALO, 6 * F2), F32),
            pltpu.VMEM((4 * 2 * bins, 18 * F2), BF16),
            pltpu.VMEM((bins // 8, 2 * bins, 8 * F2), BF16),
        ],
        compiler_params=params,
    )(
        own,
        r2,
        s2,
        r1,
        s1,
        r3,
        s3,
        conv_weight,
        proj_weight,
        w_oth,
        small,
        *prepared,
    )


def solution(mesh):
    return jax.shard_map(
        local,
        mesh=mesh,
        in_specs=(
            P(("dp", "blk"), "chan"),
            P("dp"),
            P("dp", None),
            P(None, None, None, "chan"),
            P(None, "chan"),
            P(),
            P(),
            P(None, None, "chan", None),
            P("chan"),
            P("chan"),
        ),
        out_specs=P(("dp", "blk"), "chan"),
        check_vma=False,
    )
```

```python
import jax
import jax.numpy as jnp
from jax import lax
from jax.experimental import pallas as pl
from jax.experimental.pallas import tpu as pltpu
from jax.sharding import PartitionSpec as P

F2 = 64
BAND = 3
CONV1 = 2
D2 = 2
HALO = 16
F32 = jnp.float32
BF16 = jnp.bfloat16


def chan_swap(value):
    return lax.ppermute(value, "chan", [(0, 1), (1, 0)])


def line_permute(value, step):
    count = lax.axis_size("blk")
    pairs = []
    for i in range(count):
        pairs.append(((i - step) * 2 if i >= step else i * 2 + 1, i * 2))
        pairs.append(((i + step) * 2 + 1 if i + step < count else i * 2, i * 2 + 1))
    return lax.ppermute(value, ("blk", "chan"), pairs)


def front_kernel(own_any, own_ref, sem):
    copy = pltpu.make_async_copy(own_any, own_ref, sem)
    copy.start()
    copy.wait()


def pack_kernel(
    after_any,
    mask_any,
    mw_any,
    mb_any,
    hw_any,
    cb_any,
    pb_any,
    mask_ref,
    packed_ref,
    small_ref,
    mw_s,
    mb_s,
    hw_s,
    cb_s,
    pb_s,
    extra_s,
    sems,
):
    pairs = (
        (mw_any, mw_s),
        (cb_any, cb_s),
        (mb_any, mb_s),
        (hw_any, hw_s),
        (pb_any, pb_s),
        (mask_any, mask_ref),
    )
    copies = [
        pltpu.make_async_copy(source, target, sems.at[at])
        for at, (source, target) in enumerate(pairs)
    ]
    for copy in copies:
        copy.start()
    extra_s[...] = jnp.zeros_like(extra_s)
    for copy in copies[:5]:
        copy.wait()

    half = mw_any.shape[2]
    biases = cb_s[...].astype(F32)
    for layer in range(CONV1):
        for quarter in range(4):
            at = 4 * layer + quarter
            extra_s[at : at + 1, :F2] = biases[layer : layer + 1, quarter * F2 : (quarter + 1) * F2]
    extra_s[8:9, :half] = mb_s[...].astype(F32)
    extra_s[9:10, :half] = hw_s[...].astype(F32)
    extra = pltpu.roll(extra_s[...], F2, axis=1)
    for s in range(3):
        for r in range(3):
            at = (3 * s + r) * half
            packed_ref[at : at + half, :F2] = mw_s[s, r]
    packed_ref[:32, F2:] = extra[:, F2:].astype(BF16)
    small_ref[0:2, :] = biases
    small_ref[2:3, : 2 * F2] = pb_s[...].astype(F32)
    for copy in copies[5:]:
        copy.wait()


def prep_kernel(
    length_ref,
    mask_ref,
    own_ref,
    oth_ref,
    col_mask_ref,
    wbig_ref,
    side_ref,
    head_ref,
    wt_s,
    taps_s,
):
    half = own_ref.shape[0] // 9
    columns = col_mask_ref.shape[1]
    bins = columns // 2
    count = lax.axis_size("blk")
    i = lax.axis_index("blk")
    c = lax.axis_index("chan")
    first_col = i * bins + c * columns
    length = length_ref[0]

    for source, side in ((own_ref, c), (oth_ref, 1 - c)):
        at = pl.ds(pl.multiple_of(side * half, half), half)
        for tap in range(9):
            taps_s[tap, at, :] = source[tap * half : (tap + 1) * half, :F2].astype(F32)
    blank = jnp.zeros((F2, F2), F32)
    for j in range(4):
        pieces = []
        for m in range(6):
            for r in range(3):
                pieces.append(taps_s[3 * (m - j) + r] if 0 <= m - j < 3 else blank)
        for tile in range(9):
            wt_s[j * F2 : (j + 1) * F2, tile * 2 * F2 : (tile + 1) * 2 * F2] = jnp.concatenate(
                pieces[2 * tile : 2 * tile + 2], axis=1
            )
    wbig_ref[...] = wt_s[...].T.astype(BF16)

    def spread(row, repeats):
        o = lax.broadcasted_iota(jnp.int32, (2 * F2, repeats * F2), 0)
        lane = lax.broadcasted_iota(jnp.int32, (2 * F2, repeats * F2), 1) % F2
        total = jnp.zeros((16, repeats * F2), F32)
        for ref, side in ((own_ref, c), (oth_ref, 1 - c)):
            pick = ((lane == side * half + o - F2) & (o >= F2) & (o < F2 + half)).astype(BF16)
            value = ref[:16, :].astype(F32)[row : row + 1]
            value = jnp.broadcast_to(value, (16, 2 * F2)).astype(BF16)
            total = total + jnp.dot(value, pick, preferred_element_type=F32)
        return total

    q = lax.broadcasted_iota(jnp.int32, (16, 8 * F2), 0)
    k = lax.broadcasted_iota(jnp.int32, (16, 8 * F2), 1)
    head_ref[...] = jnp.where(
        q == 2 * ((k % (4 * F2)) // F2) + k // (4 * F2), spread(9, 8), 0.0
    ).astype(BF16)
    side_ref[0:1, :] = spread(8, 4)[:1]
    minus = F32(-jnp.inf)
    block = lax.broadcasted_iota(jnp.int32, (BAND + 1, count), 1)

    def live_at(y, variant):
        at_row = jnp.sum(jnp.where(block == i + variant, mask_ref[...], 0), axis=1, keepdims=True)
        offset = lax.broadcasted_iota(jnp.int32, (BAND + 1, 1), 0)

        def entry(u):
            return jnp.sum(
                jnp.where(offset == 2 * c + u - variant, at_row, 0), axis=0, keepdims=True
            )

        value = jnp.where(
            y < 0,
            entry(-1),
            jnp.where(y < bins, entry(0), jnp.where(y < columns, entry(1), entry(2))),
        )
        column = first_col + y
        return (value != 0) & (column >= 0) & (column < length)

    b_index = lax.broadcasted_iota(jnp.int32, (columns, 2 * F2), 0)
    low = lax.broadcasted_iota(jnp.int32, (columns, 2 * F2), 1) < F2
    masks = {}
    for variant in (-1, 0, 1):
        for r in range(3):
            masks[variant, r] = jnp.where(
                live_at(b_index + (r - 1) * D2, variant), 0.0, minus
            )
    for at, (v0, v1) in enumerate(((-1, 0), (0, 0), (0, 1))):
        col_mask_ref[at, :, : 2 * F2] = jnp.where(low, masks[v0, 0], masks[v0, 1])
        col_mask_ref[at, :, 2 * F2 : 4 * F2] = jnp.where(low, masks[v0, 2], masks[v1, 0])
        col_mask_ref[at, :, 4 * F2 :] = jnp.where(low, masks[v1, 1], masks[v1, 2])

    side_ref[1:2, : 2 * F2] = jnp.where(
        live_at(lax.broadcasted_iota(jnp.int32, (1, columns), 1), 0), 1.0, 0.0
    )


def trunk_kernel(
    length_ref,
    own_ref,
    r2_ref,
    s2_ref,
    r1_ref,
    s1_ref,
    w_own_ref,
    pw_ref,
    w_oth_ref,
    small_ref,
    oth_ref,
    cols_ref,
    rows_ref,
    h_s,
    bias_s,
):
    bins = own_ref.shape[1]
    half = own_ref.shape[2]
    rows = cols_ref.shape[0]
    row_rows = rows_ref.shape[0]
    count = lax.axis_size("blk")
    i = lax.axis_index("blk")
    c = lax.axis_index("chan")
    bin_index = i * bins - HALO + lax.broadcasted_iota(jnp.int32, (rows, 2 * F2), 0)
    valid = (bin_index >= 0) & (bin_index < length_ref[0])
    inside = ((bin_index >= 0) & (bin_index < count * bins))[:, :1]

    def put(start, number, ref, source, swapped=0):
        keep = valid[start : start + number, :]
        for part in range(2):
            held = lax.rem(part + c + swapped, 2)
            for at in range(0, half, 128):
                h_s[start : start + number, part * half + at : part * half + at + 128] = jnp.where(
                    keep, ref[held, source : source + number, at : at + 128].astype(F32), 0.0
                )

    tail = bins - HALO
    put(HALO, bins, own_ref, 0)

    @pl.when(c == 0)
    def _():
        put(0, HALO, r1_ref, tail)
        put(HALO + bins, bins, s1_ref, 0, 1)
        put(HALO + 2 * bins, HALO, s2_ref, 0, 1)

    @pl.when(c == 1)
    def _():
        put(0, HALO, s1_ref, tail, 1)
        put(HALO + bins, bins, r1_ref, 0)
        put(HALO + 2 * bins, HALO, r2_ref, 0)

    other = pltpu.roll(oth_ref[:16, :].astype(F32), F2, axis=1)
    for layer in range(CONV1):
        for quarter in range(4):
            at = 4 * layer + quarter
            bias_s[layer : layer + 1, quarter * F2 : (quarter + 1) * F2] = other[at : at + 1, :F2]

    for layer in range(CONV1):
        e = 2 ** (layer + 1)
        hidden = h_s[...]
        taps = [
            (hidden if t == 1 else pltpu.roll(hidden, ((1 - t) * e) % rows, axis=0)).astype(BF16)
            for t in range(3)
        ]
        for w_ref, bias_ref, side in (
            (w_own_ref, small_ref, c),
            (w_oth_ref, bias_s, 1 - c),
        ):
            q = jnp.dot(taps[0], w_ref[layer, 0], preferred_element_type=F32)
            q = q + jnp.dot(taps[1], w_ref[layer, 1], preferred_element_type=F32)
            q = q + jnp.dot(taps[2], w_ref[layer, 2], preferred_element_type=F32)
            lanes = pl.ds(pl.multiple_of(side * half, half), half)
            bias = bias_ref[layer : layer + 1, :]
            new = (h_s[:, lanes] + jnp.maximum(q + bias, 0.0)).astype(BF16).astype(F32)
            h_s[:, lanes] = jnp.where(inside, new, 0.0)

    proj = jnp.dot(h_s[...].astype(BF16), pw_ref[...], preferred_element_type=F32)
    proj = (proj + small_ref[2:3, : 2 * F2]).astype(BF16).astype(F32)
    low = lax.broadcasted_iota(jnp.int32, (1, 2 * F2), 1) < F2
    turned = pltpu.roll(proj, F2, axis=1)
    cols_ref[...] = jnp.where(low, turned, proj).astype(BF16)
    rows_ref[...] = jnp.where(valid, jnp.where(low, proj, turned), -jnp.inf)[:row_rows]


def contact_kernel(
    length_ref,
    cols_own_ref,
    cols_far_ref,
    rows_ref,
    col_mask_ref,
    wbig_ref,
    side_ref,
    head_ref,
    out_ref,
    pa6_s,
    x_s,
    mix_s,
):
    bins = out_ref.shape[0]
    col_rows = cols_own_ref.shape[0]
    row_rows = rows_ref.shape[0]
    i = lax.axis_index("blk")
    c = lax.axis_index("chan")

    low = lax.broadcasted_iota(jnp.int32, (1, 2 * F2), 1) < F2
    pcol = jnp.where(c == 0, cols_own_ref[...].astype(F32), cols_far_ref[...].astype(F32))
    shifted = [
        pltpu.roll(pcol, col_rows - HALO - (r - 1) * D2, axis=0)[: 2 * bins] for r in range(3)
    ]
    tiles = [
        jnp.where(low, shifted[0], shifted[1]),
        jnp.where(low, shifted[2], shifted[0]),
        jnp.where(low, shifted[1], shifted[2]),
    ]
    tiled = jnp.concatenate(tiles, axis=1)
    col_first, col_mid, col_last = [
        (tiled + col_mask_ref[at]).astype(BF16).reshape(2 * bins // 16, 16, 6 * F2)
        for at in range(3)
    ]
    col_centre = shifted[1].astype(BF16).reshape(2 * bins // 16, 16, 2 * F2)

    prow = rows_ref[...]
    prow_next = pltpu.roll(prow, row_rows - D2, axis=0)
    pa6_s[:, : 2 * F2] = prow
    pa6_s[:, 2 * F2 : 4 * F2] = jnp.where(low, prow, prow_next)
    pa6_s[:, 4 * F2 :] = prow_next

    groups = bins // 8
    per_dot = x_s.shape[0] // (2 * bins)
    zero = jnp.zeros((), BF16)
    bias4 = side_ref[0:1, :]
    for v in range(2):
        for start in range(0, groups, per_dot):
            for slot in range(2 * start, 2 * (start + per_dot) + 1):
                at = HALO - D2 + v + 4 * slot
                row = jnp.broadcast_to(pa6_s[at : at + 1, :], (16, 6 * F2)).astype(BF16)
                cols = col_first if slot == 0 else col_last if slot == 2 * groups else col_mid
                value = jnp.maximum(row[None] + cols, zero).reshape(2 * bins, 6 * F2)
                for s in range(3):
                    if (slot - s) % 2 == 0 and start <= (slot - s) // 2 < start + per_dot:
                        at_row = ((slot - s) // 2 - start) * 2 * bins
                        x_s[at_row : at_row + 2 * bins, s * 6 * F2 : (s + 1) * 6 * F2] = value
            y = jnp.dot(x_s[...], wbig_ref[...], preferred_element_type=F32)
            y = jnp.maximum(y + bias4, 0.0)
            for group in range(start, start + per_dot):
                at = HALO + v + 8 * group
                parts = []
                for k in range(2):
                    row = pa6_s[at + 4 * k : at + 4 * k + 1, 2 * F2 : 4 * F2]
                    row = jnp.broadcast_to(row, (16, 2 * F2)).astype(BF16)
                    parts.append(
                        jnp.maximum(row[None] + col_centre, zero).reshape(2 * bins, 2 * F2)
                    )
                centre = jnp.concatenate(parts, axis=1).astype(F32)
                at_row = (group - start) * 2 * bins
                mixed = y[at_row : at_row + 2 * bins] + centre
                mix_s[group, :, v * 4 * F2 : (v + 1) * 4 * F2] = mixed.astype(BF16)

    lane_live = side_ref[1:2, : 2 * F2] != 0
    for group in range(groups):
        value = lax.dot_general(
            head_ref[...], mix_s[group], (((1,), (1,)), ((), ())), preferred_element_type=F32
        )[:8]
        bin_index = i * bins + 8 * group + lax.broadcasted_iota(jnp.int32, (8, 2 * bins), 0)
        out_ref[8 * group : 8 * group + 8, :] = jnp.where(
            lane_live & (bin_index < length_ref[0]), value, 0.0
        )


def local(
    features,
    chrom_len,
    band_mask,
    conv_weight,
    conv_bias,
    proj_weight,
    proj_bias,
    map_weight,
    map_bias,
    head_weight,
):
    bins, half = features.shape
    rows = 2 * bins + 2 * HALO
    half_out = map_bias.shape[0]
    smem = pl.BlockSpec(memory_space=pltpu.SMEM)
    vmem = pl.BlockSpec(memory_space=pltpu.VMEM)
    anywhere = pl.BlockSpec(memory_space=pl.ANY)
    params = pltpu.CompilerParams(vmem_limit_bytes=24 * 1024 * 1024)

    def in_hbm(value):
        return pltpu.with_memory_space_constraint(value, pltpu.HBM)

    other = chan_swap(features)
    own = pl.pallas_call(
        front_kernel,
        out_shape=jax.ShapeDtypeStruct(features.shape, BF16),
        in_specs=[anywhere],
        out_specs=vmem,
        scratch_shapes=[pltpu.SemaphoreType.DMA],
        cost_estimate=pl.CostEstimate(flops=4000000000, bytes_accessed=1000000, transcendentals=0),
        compiler_params=params,
    )(in_hbm(features))
    own = jnp.stack([own, other])
    mask, packed, small = pl.pallas_call(
        pack_kernel,
        out_shape=[
            jax.ShapeDtypeStruct(band_mask.shape[::-1], jnp.int32),
            jax.ShapeDtypeStruct((9 * half_out, 2 * F2), BF16),
            jax.ShapeDtypeStruct((8, half), F32),
        ],
        in_specs=[anywhere] * 7,
        out_specs=[vmem] * 3,
        scratch_shapes=[
            pltpu.VMEM(map_weight.shape, BF16),
            pltpu.VMEM((1, half_out), BF16),
            pltpu.VMEM((1, half_out), BF16),
            pltpu.VMEM(conv_bias.shape, BF16),
            pltpu.VMEM((1, 2 * F2), BF16),
            pltpu.VMEM((32, 2 * F2), F32),
            pltpu.SemaphoreType.DMA((6,)),
        ],
        compiler_params=params,
    )(
        own,
        in_hbm(band_mask.T),
        in_hbm(map_weight),
        in_hbm(map_bias[None]),
        in_hbm(head_weight[None]),
        in_hbm(conv_bias),
        in_hbm(proj_bias[None]),
    )
    r1 = line_permute(own, 1)
    r2 = line_permute(own[:, :HALO], 2)
    r1, r2 = lax.optimization_barrier((r1, r2))
    s1 = chan_swap(r1)
    s2 = chan_swap(r2)
    w_in, own = lax.optimization_barrier((conv_weight, own))
    w_oth = chan_swap(w_in)
    oth = chan_swap(packed)
    cols, row_features = pl.pallas_call(
        trunk_kernel,
        out_shape=[
            jax.ShapeDtypeStruct((rows, 2 * F2), BF16),
            jax.ShapeDtypeStruct((bins + 2 * HALO, 2 * F2), F32),
        ],
        in_specs=[smem] + [vmem] * 10,
        out_specs=[vmem] * 2,
        scratch_shapes=[
            pltpu.VMEM((rows, 2 * half), F32),
            pltpu.VMEM((8, half), F32),
        ],
        compiler_params=params,
    )(chrom_len, own, r2, s2, r1, s1, conv_weight, proj_weight, w_oth, small, oth)
    cols_far = line_permute(cols, 2)
    prepared = pl.pallas_call(
        prep_kernel,
        out_shape=[
            jax.ShapeDtypeStruct((3, 2 * bins, 6 * F2), F32),
            jax.ShapeDtypeStruct((18 * F2, 4 * F2), BF16),
            jax.ShapeDtypeStruct((8, half), F32),
            jax.ShapeDtypeStruct((16, 8 * F2), BF16),
        ],
        in_specs=[smem] + [vmem] * 3,
        out_specs=[vmem] * 4,
        scratch_shapes=[
            pltpu.VMEM((4 * F2, 18 * F2), F32),
            pltpu.VMEM((9, F2, F2), F32),
        ],
        compiler_params=params,
    )(chrom_len, mask, packed, oth)
    return pl.pallas_call(
        contact_kernel,
        out_shape=jax.ShapeDtypeStruct((bins, 2 * bins), F32),
        in_specs=[smem] + [vmem] * 7,
        out_specs=vmem,
        scratch_shapes=[
            pltpu.VMEM((bins + 2 * HALO, 6 * F2), F32),
            pltpu.VMEM((4 * 2 * bins, 18 * F2), BF16),
            pltpu.VMEM((bins // 8, 2 * bins, 8 * F2), BF16),
        ],
        compiler_params=params,
    )(chrom_len, cols, cols_far, row_features, *prepared)


def solution(mesh):
    return jax.shard_map(
        local,
        mesh=mesh,
        in_specs=(
            P(("dp", "blk"), "chan"),
            P("dp"),
            P("dp", None),
            P(None, None, None, "chan"),
            P(None, "chan"),
            P(),
            P(),
            P(None, None, "chan", None),
            P("chan"),
            P("chan"),
        ),
        out_specs=P(("dp", "blk"), "chan"),
        check_vma=False,
    )
```

```python
import functools

import jax
import jax.numpy as jnp
from jax import lax
from jax.experimental import pallas as pl
from jax.experimental.pallas import tpu as pltpu
from jax.sharding import PartitionSpec as P

F2 = 64
BAND = 3
CONV1 = 2
D2 = 2
HALO = 16
F32 = jnp.float32
BF16 = jnp.bfloat16


def chan_swap(value):
    return lax.ppermute(value, "chan", [(0, 1), (1, 0)])


def line_permute(value, step):
    count = lax.axis_size("blk")
    pairs = []
    for i in range(count):
        pairs.append(((i - step) * 2 if i >= step else i * 2 + 1, i * 2))
        pairs.append(((i + step) * 2 + 1 if i + step < count else i * 2, i * 2 + 1))
    return lax.ppermute(value, ("blk", "chan"), pairs)


def front_kernel(own_any, own_ref, sem):
    copy = pltpu.make_async_copy(own_any, own_ref, sem)
    copy.start()
    copy.wait()


def pack_kernel(
    after_any,
    mask_any,
    mw_any,
    mb_any,
    hw_any,
    cb_any,
    pb_any,
    mask_ref,
    packed_ref,
    small_ref,
    mw_s,
    mb_s,
    hw_s,
    cb_s,
    pb_s,
    extra_s,
    sems,
):
    pairs = (
        (mw_any, mw_s),
        (cb_any, cb_s),
        (mb_any, mb_s),
        (hw_any, hw_s),
        (pb_any, pb_s),
        (mask_any, mask_ref),
    )
    copies = [
        pltpu.make_async_copy(source, target, sems.at[at])
        for at, (source, target) in enumerate(pairs)
    ]
    for copy in copies:
        copy.start()
    extra_s[...] = jnp.zeros_like(extra_s)
    for copy in copies[:5]:
        copy.wait()

    half = mw_any.shape[2]
    biases = cb_s[...].astype(F32)
    for layer in range(CONV1):
        for quarter in range(4):
            at = 4 * layer + quarter
            extra_s[at : at + 1, :F2] = biases[layer : layer + 1, quarter * F2 : (quarter + 1) * F2]
    extra_s[8:9, :half] = mb_s[...].astype(F32)
    extra_s[9:10, :half] = hw_s[...].astype(F32)
    extra = pltpu.roll(extra_s[...], F2, axis=1)
    for s in range(3):
        for r in range(3):
            at = (3 * s + r) * half
            packed_ref[at : at + half, :F2] = mw_s[s, r]
    packed_ref[:32, F2:] = extra[:, F2:].astype(BF16)
    small_ref[0:2, :] = biases
    small_ref[2:3, : 2 * F2] = pb_s[...].astype(F32)
    for copy in copies[5:]:
        copy.wait()


def prep_kernel(
    length_ref,
    mask_ref,
    own_ref,
    oth_ref,
    col_mask_ref,
    wbig_ref,
    side_ref,
    head_ref,
    wt_s,
    taps_s,
):
    half = own_ref.shape[0] // 9
    columns = col_mask_ref.shape[1]
    bins = columns // 2
    count = lax.axis_size("blk")
    i = lax.axis_index("blk")
    c = lax.axis_index("chan")
    first_col = i * bins + c * columns
    length = length_ref[0]

    for source, side in ((own_ref, c), (oth_ref, 1 - c)):
        at = pl.ds(pl.multiple_of(side * half, half), half)
        for tap in range(9):
            taps_s[tap, at, :] = source[tap * half : (tap + 1) * half, :F2].astype(F32)
    blank = jnp.zeros((F2, F2), F32)
    for j in range(4):
        pieces = []
        for m in range(6):
            for r in range(3):
                pieces.append(taps_s[3 * (m - j) + r] if 0 <= m - j < 3 else blank)
        for tile in range(9):
            wt_s[j * F2 : (j + 1) * F2, tile * 2 * F2 : (tile + 1) * 2 * F2] = jnp.concatenate(
                pieces[2 * tile : 2 * tile + 2], axis=1
            )
    wbig_ref[...] = wt_s[...].T.astype(BF16)

    def spread(row, repeats):
        o = lax.broadcasted_iota(jnp.int32, (2 * F2, repeats * F2), 0)
        lane = lax.broadcasted_iota(jnp.int32, (2 * F2, repeats * F2), 1) % F2
        total = jnp.zeros((16, repeats * F2), F32)
        for ref, side in ((own_ref, c), (oth_ref, 1 - c)):
            pick = ((lane == side * half + o - F2) & (o >= F2) & (o < F2 + half)).astype(BF16)
            value = ref[:16, :].astype(F32)[row : row + 1]
            value = jnp.broadcast_to(value, (16, 2 * F2)).astype(BF16)
            total = total + jnp.dot(value, pick, preferred_element_type=F32)
        return total

    q = lax.broadcasted_iota(jnp.int32, (16, 8 * F2), 0)
    k = lax.broadcasted_iota(jnp.int32, (16, 8 * F2), 1)
    head_ref[...] = jnp.where(
        q == 2 * ((k % (4 * F2)) // F2) + k // (4 * F2), spread(9, 8), 0.0
    ).astype(BF16)
    side_ref[0:1, :] = spread(8, 4)[:1]
    minus = F32(-jnp.inf)
    block = lax.broadcasted_iota(jnp.int32, (BAND + 1, count), 1)

    def live_at(y, variant):
        at_row = jnp.sum(jnp.where(block == i + variant, mask_ref[...], 0), axis=1, keepdims=True)
        offset = lax.broadcasted_iota(jnp.int32, (BAND + 1, 1), 0)

        def entry(u):
            return jnp.sum(
                jnp.where(offset == 2 * c + u - variant, at_row, 0), axis=0, keepdims=True
            )

        value = jnp.where(
            y < 0,
            entry(-1),
            jnp.where(y < bins, entry(0), jnp.where(y < columns, entry(1), entry(2))),
        )
        column = first_col + y
        return (value != 0) & (column >= 0) & (column < length)

    b_index = lax.broadcasted_iota(jnp.int32, (columns, 2 * F2), 0)
    low = lax.broadcasted_iota(jnp.int32, (columns, 2 * F2), 1) < F2
    masks = {}
    for variant in (-1, 0, 1):
        for r in range(3):
            masks[variant, r] = jnp.where(
                live_at(b_index + (r - 1) * D2, variant), 0.0, minus
            )
    for at, (v0, v1) in enumerate(((-1, 0), (0, 0), (0, 1))):
        col_mask_ref[at, :, : 2 * F2] = jnp.where(low, masks[v0, 0], masks[v0, 1])
        col_mask_ref[at, :, 2 * F2 : 4 * F2] = jnp.where(low, masks[v0, 2], masks[v1, 0])
        col_mask_ref[at, :, 4 * F2 :] = jnp.where(low, masks[v1, 1], masks[v1, 2])

    side_ref[1:2, : 2 * F2] = jnp.where(
        live_at(lax.broadcasted_iota(jnp.int32, (1, columns), 1), 0), 1.0, 0.0
    )


def trunk_kernel(
    length_ref,
    own_ref,
    r2_ref,
    s2_ref,
    r1_ref,
    s1_ref,
    w_own_ref,
    pw_ref,
    w_oth_ref,
    small_ref,
    oth_ref,
    cols_ref,
    rows_ref,
    h_s,
    bias_s,
):
    bins = own_ref.shape[1]
    half = own_ref.shape[2]
    rows = cols_ref.shape[0]
    row_rows = rows_ref.shape[0]
    count = lax.axis_size("blk")
    i = lax.axis_index("blk")
    c = lax.axis_index("chan")
    bin_index = i * bins - HALO + lax.broadcasted_iota(jnp.int32, (rows, 2 * F2), 0)
    valid = (bin_index >= 0) & (bin_index < length_ref[0])
    inside = ((bin_index >= 0) & (bin_index < count * bins))[:, :1]

    def put(start, number, ref, source, swapped=0):
        keep = valid[start : start + number, :]
        for part in range(2):
            held = lax.rem(part + c + swapped, 2)
            for at in range(0, half, 128):
                h_s[start : start + number, part * half + at : part * half + at + 128] = jnp.where(
                    keep, ref[held, source : source + number, at : at + 128].astype(F32), 0.0
                )

    tail = bins - HALO
    put(HALO, bins, own_ref, 0)

    @pl.when(c == 0)
    def _():
        put(0, HALO, r1_ref, tail)
        put(HALO + bins, bins, s1_ref, 0, 1)
        put(HALO + 2 * bins, HALO, s2_ref, 0, 1)

    @pl.when(c == 1)
    def _():
        put(0, HALO, s1_ref, tail, 1)
        put(HALO + bins, bins, r1_ref, 0)
        put(HALO + 2 * bins, HALO, r2_ref, 0)

    other = pltpu.roll(oth_ref[:16, :].astype(F32), F2, axis=1)
    for layer in range(CONV1):
        for quarter in range(4):
            at = 4 * layer + quarter
            bias_s[layer : layer + 1, quarter * F2 : (quarter + 1) * F2] = other[at : at + 1, :F2]

    for layer in range(CONV1):
        e = 2 ** (layer + 1)
        hidden = h_s[...]
        taps = [
            (hidden if t == 1 else pltpu.roll(hidden, ((1 - t) * e) % rows, axis=0)).astype(BF16)
            for t in range(3)
        ]
        for w_ref, bias_ref, side in (
            (w_own_ref, small_ref, c),
            (w_oth_ref, bias_s, 1 - c),
        ):
            q = jnp.dot(taps[0], w_ref[layer, 0], preferred_element_type=F32)
            q = q + jnp.dot(taps[1], w_ref[layer, 1], preferred_element_type=F32)
            q = q + jnp.dot(taps[2], w_ref[layer, 2], preferred_element_type=F32)
            lanes = pl.ds(pl.multiple_of(side * half, half), half)
            bias = bias_ref[layer : layer + 1, :]
            new = (h_s[:, lanes] + jnp.maximum(q + bias, 0.0)).astype(BF16).astype(F32)
            h_s[:, lanes] = jnp.where(inside, new, 0.0)

    proj = jnp.dot(h_s[...].astype(BF16), pw_ref[...], preferred_element_type=F32)
    proj = (proj + small_ref[2:3, : 2 * F2]).astype(BF16).astype(F32)
    low = lax.broadcasted_iota(jnp.int32, (1, 2 * F2), 1) < F2
    turned = pltpu.roll(proj, F2, axis=1)
    cols_ref[...] = jnp.where(low, turned, proj).astype(BF16)
    rows_ref[...] = jnp.where(valid, jnp.where(low, proj, turned), -jnp.inf)[:row_rows]


def near_kernel(*refs):
    @pl.when(lax.axis_index("chan") == 0)
    def _():
        contact_tiles(*refs)


def far_kernel(near_ref, *refs):
    @pl.when(lax.axis_index("chan") == 0)
    def _():
        refs[7][...] = near_ref[...]

    @pl.when(lax.axis_index("chan") == 1)
    def _():
        contact_tiles(*refs)


def contact_tiles(
    length_ref,
    cols_ref,
    rows_ref,
    col_mask_ref,
    wbig_ref,
    side_ref,
    head_ref,
    out_ref,
    pa6_s,
    x_s,
    mix_s,
):
    bins = out_ref.shape[0]
    col_rows = cols_ref.shape[0]
    row_rows = rows_ref.shape[0]
    i = lax.axis_index("blk")

    low = lax.broadcasted_iota(jnp.int32, (1, 2 * F2), 1) < F2
    pcol = cols_ref[...].astype(F32)
    shifted = [
        pltpu.roll(pcol, col_rows - HALO - (r - 1) * D2, axis=0)[: 2 * bins] for r in range(3)
    ]
    tiles = [
        jnp.where(low, shifted[0], shifted[1]),
        jnp.where(low, shifted[2], shifted[0]),
        jnp.where(low, shifted[1], shifted[2]),
    ]
    tiled = jnp.concatenate(tiles, axis=1)
    col_first, col_mid, col_last = [
        (tiled + col_mask_ref[at]).astype(BF16).reshape(2 * bins // 16, 16, 6 * F2)
        for at in range(3)
    ]
    col_centre = shifted[1].astype(BF16).reshape(2 * bins // 16, 16, 2 * F2)

    prow = rows_ref[...]
    prow_next = pltpu.roll(prow, row_rows - D2, axis=0)
    pa6_s[:, : 2 * F2] = prow
    pa6_s[:, 2 * F2 : 4 * F2] = jnp.where(low, prow, prow_next)
    pa6_s[:, 4 * F2 :] = prow_next

    groups = bins // 8
    per_dot = x_s.shape[0] // (2 * bins)
    zero = jnp.zeros((), BF16)
    bias4 = side_ref[0:1, :]
    for v in range(2):
        for start in range(0, groups, per_dot):
            for slot in range(2 * start, 2 * (start + per_dot) + 1):
                at = HALO - D2 + v + 4 * slot
                row = jnp.broadcast_to(pa6_s[at : at + 1, :], (16, 6 * F2)).astype(BF16)
                cols = col_first if slot == 0 else col_last if slot == 2 * groups else col_mid
                value = jnp.maximum(row[None] + cols, zero).reshape(2 * bins, 6 * F2)
                for s in range(3):
                    if (slot - s) % 2 == 0 and start <= (slot - s) // 2 < start + per_dot:
                        at_row = ((slot - s) // 2 - start) * 2 * bins
                        x_s[at_row : at_row + 2 * bins, s * 6 * F2 : (s + 1) * 6 * F2] = value
            y = jnp.dot(x_s[...], wbig_ref[...], preferred_element_type=F32)
            y = jnp.maximum(y + bias4, 0.0)
            for group in range(start, start + per_dot):
                at = HALO + v + 8 * group
                parts = []
                for k in range(2):
                    row = pa6_s[at + 4 * k : at + 4 * k + 1, 2 * F2 : 4 * F2]
                    row = jnp.broadcast_to(row, (16, 2 * F2)).astype(BF16)
                    parts.append(
                        jnp.maximum(row[None] + col_centre, zero).reshape(2 * bins, 2 * F2)
                    )
                centre = jnp.concatenate(parts, axis=1).astype(F32)
                at_row = (group - start) * 2 * bins
                mixed = y[at_row : at_row + 2 * bins] + centre
                mix_s[group, :, v * 4 * F2 : (v + 1) * 4 * F2] = mixed.astype(BF16)

    lane_live = side_ref[1:2, : 2 * F2] != 0
    for group in range(groups):
        value = lax.dot_general(
            head_ref[...], mix_s[group], (((1,), (1,)), ((), ())), preferred_element_type=F32
        )[:8]
        bin_index = i * bins + 8 * group + lax.broadcasted_iota(jnp.int32, (8, 2 * bins), 0)
        out_ref[8 * group : 8 * group + 8, :] = jnp.where(
            lane_live & (bin_index < length_ref[0]), value, 0.0
        )


def local(
    features,
    chrom_len,
    band_mask,
    conv_weight,
    conv_bias,
    proj_weight,
    proj_bias,
    map_weight,
    map_bias,
    head_weight,
):
    bins, half = features.shape
    rows = 2 * bins + 2 * HALO
    half_out = map_bias.shape[0]
    smem = pl.BlockSpec(memory_space=pltpu.SMEM)
    vmem = pl.BlockSpec(memory_space=pltpu.VMEM)
    anywhere = pl.BlockSpec(memory_space=pl.ANY)
    params = pltpu.CompilerParams(vmem_limit_bytes=24 * 1024 * 1024)

    def in_hbm(value):
        return pltpu.with_memory_space_constraint(value, pltpu.HBM)

    other = chan_swap(features)
    own = pl.pallas_call(
        front_kernel,
        out_shape=jax.ShapeDtypeStruct(features.shape, BF16),
        in_specs=[anywhere],
        out_specs=vmem,
        scratch_shapes=[pltpu.SemaphoreType.DMA],
        cost_estimate=pl.CostEstimate(flops=4000000000, bytes_accessed=1000000, transcendentals=0),
        compiler_params=params,
    )(in_hbm(features))
    own = jnp.stack([own, other])
    mask, packed, small = pl.pallas_call(
        pack_kernel,
        out_shape=[
            jax.ShapeDtypeStruct(band_mask.shape[::-1], jnp.int32),
            jax.ShapeDtypeStruct((9 * half_out, 2 * F2), BF16),
            jax.ShapeDtypeStruct((8, half), F32),
        ],
        in_specs=[anywhere] * 7,
        out_specs=[vmem] * 3,
        scratch_shapes=[
            pltpu.VMEM(map_weight.shape, BF16),
            pltpu.VMEM((1, half_out), BF16),
            pltpu.VMEM((1, half_out), BF16),
            pltpu.VMEM(conv_bias.shape, BF16),
            pltpu.VMEM((1, 2 * F2), BF16),
            pltpu.VMEM((32, 2 * F2), F32),
            pltpu.SemaphoreType.DMA((6,)),
        ],
        compiler_params=params,
    )(
        own,
        in_hbm(band_mask.T),
        in_hbm(map_weight),
        in_hbm(map_bias[None]),
        in_hbm(head_weight[None]),
        in_hbm(conv_bias),
        in_hbm(proj_bias[None]),
    )
    r1 = line_permute(own, 1)
    r2 = line_permute(own[:, :HALO], 2)
    r1, r2 = lax.optimization_barrier((r1, r2))
    s1 = chan_swap(r1)
    s2 = chan_swap(r2)
    w_in, own = lax.optimization_barrier((conv_weight, own))
    w_oth = chan_swap(w_in)
    oth = chan_swap(packed)
    cols, row_features = pl.pallas_call(
        trunk_kernel,
        out_shape=[
            jax.ShapeDtypeStruct((rows, 2 * F2), BF16),
            jax.ShapeDtypeStruct((bins + 2 * HALO, 2 * F2), F32),
        ],
        in_specs=[smem] + [vmem] * 10,
        out_specs=[vmem] * 2,
        scratch_shapes=[
            pltpu.VMEM((rows, 2 * half), F32),
            pltpu.VMEM((8, half), F32),
        ],
        compiler_params=params,
    )(chrom_len, own, r2, s2, r1, s1, conv_weight, proj_weight, w_oth, small, oth)
    cols_far = line_permute(cols, 2)
    prepared = pl.pallas_call(
        prep_kernel,
        out_shape=[
            jax.ShapeDtypeStruct((3, 2 * bins, 6 * F2), F32),
            jax.ShapeDtypeStruct((18 * F2, 4 * F2), BF16),
            jax.ShapeDtypeStruct((8, half), F32),
            jax.ShapeDtypeStruct((16, 8 * F2), BF16),
        ],
        in_specs=[smem] + [vmem] * 3,
        out_specs=[vmem] * 4,
        scratch_shapes=[
            pltpu.VMEM((4 * F2, 18 * F2), F32),
            pltpu.VMEM((9, F2, F2), F32),
        ],
        compiler_params=params,
    )(chrom_len, mask, packed, oth)
    tiles = functools.partial(
        pl.pallas_call,
        out_shape=jax.ShapeDtypeStruct((bins, 2 * bins), F32),
        out_specs=vmem,
        scratch_shapes=[
            pltpu.VMEM((bins + 2 * HALO, 6 * F2), F32),
            pltpu.VMEM((4 * 2 * bins, 18 * F2), BF16),
            pltpu.VMEM((bins // 8, 2 * bins, 8 * F2), BF16),
        ],
        compiler_params=params,
    )
    near = tiles(near_kernel, in_specs=[smem] + [vmem] * 6)(
        chrom_len, cols, row_features, *prepared
    )
    return tiles(far_kernel, in_specs=[vmem, smem] + [vmem] * 6)(
        near, chrom_len, cols_far, row_features, *prepared
    )


def solution(mesh):
    return jax.shard_map(
        local,
        mesh=mesh,
        in_specs=(
            P(("dp", "blk"), "chan"),
            P("dp"),
            P("dp", None),
            P(None, None, None, "chan"),
            P(None, "chan"),
            P(),
            P(),
            P(None, None, "chan", None),
            P("chan"),
            P("chan"),
        ),
        out_specs=P(("dp", "blk"), "chan"),
        check_vma=False,
    )
```

```python
import functools

import jax
import jax.numpy as jnp
from jax import lax
from jax.experimental import pallas as pl
from jax.experimental.pallas import tpu as pltpu
from jax.sharding import PartitionSpec as P

F2 = 64
BAND = 3
CONV1 = 2
D2 = 2
HALO = 8
RIM = 16
F32 = jnp.float32
BF16 = jnp.bfloat16


def chan_swap(value):
    return lax.ppermute(value, "chan", [(0, 1), (1, 0)])


def line_permute(value, step):
    count = lax.axis_size("blk")
    pairs = []
    for i in range(count):
        pairs.append(((i - step) * 2 if i >= step else i * 2 + 1, i * 2))
        pairs.append(((i + step) * 2 + 1 if i + step < count else i * 2, i * 2 + 1))
    return lax.ppermute(value, ("blk", "chan"), pairs)


def pair_permute(value, low):
    count = lax.axis_size("blk")
    partner = {}
    for i in range(low, count - 1, 2):
        partner[i], partner[i + 1] = i + 1, i
    pairs = []
    for i in range(count):
        for core in range(2):
            source = partner[i] * 2 + core if i in partner else i * 2 + 1 - core
            pairs.append((source, i * 2 + core))
    return lax.ppermute(value, ("blk", "chan"), pairs)


def front_kernel(own_any, cb_any, pb_any, own_ref, small_ref, cb_s, pb_s, sems):
    pairs = ((cb_any, cb_s), (pb_any, pb_s), (own_any, own_ref))
    copies = [
        pltpu.make_async_copy(source, target, sems.at[at])
        for at, (source, target) in enumerate(pairs)
    ]
    for copy in copies:
        copy.start()
    copies[0].wait()
    copies[1].wait()
    small_ref[0:CONV1, :] = cb_s[...].astype(F32)
    small_ref[CONV1 : CONV1 + 1, : 2 * F2] = pb_s[...].astype(F32)
    copies[2].wait()


def pack_kernel(
    after_any,
    mask_any,
    mw_any,
    mb_any,
    hw_any,
    mask_ref,
    packed_ref,
    mw_s,
    mb_s,
    hw_s,
    extra_s,
    sems,
):
    pairs = ((mw_any, mw_s), (mb_any, mb_s), (hw_any, hw_s), (mask_any, mask_ref))
    copies = [
        pltpu.make_async_copy(source, target, sems.at[at])
        for at, (source, target) in enumerate(pairs)
    ]
    for copy in copies:
        copy.start()
    extra_s[...] = jnp.zeros_like(extra_s)
    for copy in copies:
        copy.wait()

    half = mw_any.shape[2]
    extra_s[8:9, :half] = mb_s[...].astype(F32)
    extra_s[9:10, :half] = hw_s[...].astype(F32)
    extra = pltpu.roll(extra_s[...], F2, axis=1)
    for s in range(3):
        for r in range(3):
            at = (3 * s + r) * half
            packed_ref[at : at + half, :F2] = mw_s[s, r]
    packed_ref[:32, F2:] = extra[:, F2:].astype(BF16)


def prep_kernel(
    length_ref,
    mask_ref,
    own_ref,
    oth_ref,
    col_mask_ref,
    wbig_ref,
    side_ref,
    head_ref,
    wt_s,
    taps_s,
):
    half = own_ref.shape[0] // 9
    columns = col_mask_ref.shape[1]
    bins = columns // 2
    count = lax.axis_size("blk")
    i = lax.axis_index("blk")
    c = lax.axis_index("chan")
    first_col = i * bins + c * columns
    length = length_ref[0]

    for source, side in ((own_ref, c), (oth_ref, 1 - c)):
        at = pl.ds(pl.multiple_of(side * half, half), half)
        for tap in range(9):
            taps_s[tap, at, :] = source[tap * half : (tap + 1) * half, :F2].astype(F32)
    blank = jnp.zeros((F2, F2), F32)
    for j in range(4):
        pieces = []
        for m in range(6):
            for r in range(3):
                pieces.append(taps_s[3 * (m - j) + r] if 0 <= m - j < 3 else blank)
        for tile in range(9):
            wt_s[j * F2 : (j + 1) * F2, tile * 2 * F2 : (tile + 1) * 2 * F2] = jnp.concatenate(
                pieces[2 * tile : 2 * tile + 2], axis=1
            )
    wbig_ref[...] = wt_s[...].T.astype(BF16)

    def spread(row, repeats):
        o = lax.broadcasted_iota(jnp.int32, (2 * F2, repeats * F2), 0)
        lane = lax.broadcasted_iota(jnp.int32, (2 * F2, repeats * F2), 1) % F2
        total = jnp.zeros((16, repeats * F2), F32)
        for ref, side in ((own_ref, c), (oth_ref, 1 - c)):
            pick = ((lane == side * half + o - F2) & (o >= F2) & (o < F2 + half)).astype(BF16)
            value = ref[:16, :].astype(F32)[row : row + 1]
            value = jnp.broadcast_to(value, (16, 2 * F2)).astype(BF16)
            total = total + jnp.dot(value, pick, preferred_element_type=F32)
        return total

    q = lax.broadcasted_iota(jnp.int32, (16, 8 * F2), 0)
    k = lax.broadcasted_iota(jnp.int32, (16, 8 * F2), 1)
    head_ref[...] = jnp.where(
        q == 2 * ((k % (4 * F2)) // F2) + k // (4 * F2), spread(9, 8), 0.0
    ).astype(BF16)
    side_ref[0:1, :] = spread(8, 4)[:1]
    minus = F32(-jnp.inf)
    block = lax.broadcasted_iota(jnp.int32, (BAND + 1, count), 1)

    def live_at(y, variant):
        at_row = jnp.sum(jnp.where(block == i + variant, mask_ref[...], 0), axis=1, keepdims=True)
        offset = lax.broadcasted_iota(jnp.int32, (BAND + 1, 1), 0)

        def entry(u):
            return jnp.sum(
                jnp.where(offset == 2 * c + u - variant, at_row, 0), axis=0, keepdims=True
            )

        value = jnp.where(
            y < 0,
            entry(-1),
            jnp.where(y < bins, entry(0), jnp.where(y < columns, entry(1), entry(2))),
        )
        column = first_col + y
        return (value != 0) & (column >= 0) & (column < length)

    b_index = lax.broadcasted_iota(jnp.int32, (columns, 2 * F2), 0)
    low = lax.broadcasted_iota(jnp.int32, (columns, 2 * F2), 1) < F2
    masks = {}
    for variant in (-1, 0, 1):
        for r in range(3):
            masks[variant, r] = jnp.where(
                live_at(b_index + (r - 1) * D2, variant), 0.0, minus
            )
    for at, (v0, v1) in enumerate(((-1, 0), (0, 0), (0, 1))):
        col_mask_ref[at, :, : 2 * F2] = jnp.where(low, masks[v0, 0], masks[v0, 1])
        col_mask_ref[at, :, 2 * F2 : 4 * F2] = jnp.where(low, masks[v0, 2], masks[v1, 0])
        col_mask_ref[at, :, 4 * F2 :] = jnp.where(low, masks[v1, 1], masks[v1, 2])

    side_ref[1:2, : 2 * F2] = jnp.where(
        live_at(lax.broadcasted_iota(jnp.int32, (1, columns), 1), 0), 1.0, 0.0
    )


def window_kernel(own_ref, r2_ref, even_ref, odd_ref, h_ref):
    core = lax.axis_index("chan")
    parity = lax.rem(lax.axis_index("blk"), 2)
    bins = own_ref.shape[1]
    half = own_ref.shape[2]

    def fill(before_ref, after_ref):
        for part in range(2):
            lanes = slice(part * half, (part + 1) * half)
            held = 1 - part
            before = before_ref[held, bins - RIM :, :].astype(F32)
            h_ref[:HALO, lanes] = before[RIM - HALO :]
            h_ref[HALO : HALO + bins, lanes] = own_ref[held].astype(F32)
            h_ref[HALO + bins : HALO + 2 * bins, lanes] = after_ref[held].astype(F32)
            h_ref[HALO + 2 * bins :, lanes] = r2_ref[held].astype(F32)[:HALO]

    @pl.when((core == 1) & (parity == 0))
    def _():
        fill(odd_ref, even_ref)

    @pl.when((core == 1) & (parity == 1))
    def _():
        fill(even_ref, odd_ref)


def trunk_kernel(*refs):
    @pl.when(lax.axis_index("chan") == 1)
    def _():
        trunk(*refs)


def trunk(
    length_ref,
    window_ref,
    w_own_ref,
    pw_ref,
    w_oth_ref,
    small_ref,
    cb_oth_ref,
    cols_ref,
    both_ref,
    h_s,
):
    rows = window_ref.shape[0]
    half = window_ref.shape[1] // 2
    held = cols_ref.shape[0]
    bins = held - 2 * HALO
    count = lax.axis_size("blk")
    i = lax.axis_index("blk")
    bin_index = i * bins - HALO + lax.broadcasted_iota(jnp.int32, (rows, 2 * F2), 0)
    valid = (bin_index >= 0) & (bin_index < length_ref[0])
    inside = ((bin_index >= 0) & (bin_index < count * bins))[:, :1]

    for at in range(0, 2 * half, 128):
        h_s[:, at : at + 128] = jnp.where(valid, window_ref[:, at : at + 128], 0.0)

    for layer in range(CONV1):
        e = 2 ** (layer + 1)
        hidden = h_s[...]
        taps = [
            (hidden if t == 1 else pltpu.roll(hidden, ((1 - t) * e) % rows, axis=0)).astype(BF16)
            for t in range(3)
        ]
        for at, w_ref, bias_ref in ((half, w_own_ref, small_ref), (0, w_oth_ref, cb_oth_ref)):
            q = jnp.dot(taps[0], w_ref[layer, 0], preferred_element_type=F32)
            q = q + jnp.dot(taps[1], w_ref[layer, 1], preferred_element_type=F32)
            q = q + jnp.dot(taps[2], w_ref[layer, 2], preferred_element_type=F32)
            bias = bias_ref[...].astype(F32)[layer : layer + 1, :]
            lanes = slice(at, at + half)
            new = (h_s[:, lanes] + jnp.maximum(q + bias, 0.0)).astype(BF16).astype(F32)
            h_s[:, lanes] = jnp.where(inside, new, 0.0)

    proj = jnp.dot(h_s[...].astype(BF16), pw_ref[...], preferred_element_type=F32)
    proj = (proj + small_ref[CONV1 : CONV1 + 1, : 2 * F2]).astype(BF16).astype(F32)
    low = lax.broadcasted_iota(jnp.int32, (1, 2 * F2), 1) < F2
    turned = pltpu.roll(proj, F2, axis=1)
    cols = jnp.where(low, turned[:held], proj[rows - held :]).astype(BF16)
    cols_ref[...] = cols
    both_ref[:held, :] = cols
    both_ref[held:, :] = jnp.where(valid, jnp.where(low, proj, turned), -jnp.inf)[:held].astype(
        BF16
    )


def near_kernel(*refs):
    @pl.when(lax.axis_index("chan") == 0)
    def _():
        contact_tiles(*refs)


def far_kernel(near_ref, *refs):
    @pl.when(lax.axis_index("chan") == 0)
    def _():
        refs[7][...] = near_ref[...]

    @pl.when(lax.axis_index("chan") == 1)
    def _():
        contact_tiles(*refs)


def contact_tiles(
    length_ref,
    cols_ref,
    rows_ref,
    col_mask_ref,
    wbig_ref,
    side_ref,
    head_ref,
    out_ref,
    pa6_s,
    mix_s,
):
    bins = out_ref.shape[0]
    col_rows = 2 * bins + 2 * HALO
    row_rows = bins + 2 * HALO
    i = lax.axis_index("blk")

    low = lax.broadcasted_iota(jnp.int32, (1, 2 * F2), 1) < F2
    held = bins + 2 * HALO
    pcol = cols_ref[: bins + 2 * HALO, :].astype(F32)
    turned = pltpu.roll(pcol, F2, axis=1)
    pcol = jnp.concatenate(
        [jnp.where(low, pcol, turned), jnp.where(low, turned, pcol)[2 * held - col_rows :]], axis=0
    )
    shifted = [
        pltpu.roll(pcol, col_rows - HALO - (r - 1) * D2, axis=0)[: 2 * bins] for r in range(3)
    ]
    tiles = [
        jnp.where(low, shifted[0], shifted[1]),
        jnp.where(low, shifted[2], shifted[0]),
        jnp.where(low, shifted[1], shifted[2]),
    ]
    tiled = jnp.concatenate(tiles, axis=1)
    col_first, col_mid, col_last = [
        (tiled + col_mask_ref[at]).astype(BF16).reshape(2 * bins // 16, 16, 6 * F2)
        for at in range(3)
    ]
    col_centre = shifted[1].astype(BF16).reshape(2 * bins // 16, 16, 2 * F2)

    prow = rows_ref[row_rows:, :].astype(F32)
    prow_next = pltpu.roll(prow, row_rows - D2, axis=0)
    pa6_s[:, : 2 * F2] = prow
    pa6_s[:, 2 * F2 : 4 * F2] = jnp.where(low, prow, prow_next)
    pa6_s[:, 4 * F2 :] = prow_next

    groups = bins // 8
    per_dot = 4
    zero = jnp.zeros((), BF16)
    bias4 = side_ref[0:1, :]
    for v in range(2):
        for start in range(0, groups, per_dot):
            values = {}
            for slot in range(2 * start, 2 * (start + per_dot) + 1):
                at = HALO - D2 + v + 4 * slot
                row = jnp.broadcast_to(pa6_s[at : at + 1, :], (16, 6 * F2)).astype(BF16)
                cols = col_first if slot == 0 else col_last if slot == 2 * groups else col_mid
                values[slot] = jnp.maximum(row[None] + cols, zero).reshape(2 * bins, 6 * F2)
            x = jnp.concatenate(
                [
                    jnp.concatenate([values[2 * g + s] for s in range(3)], axis=1)
                    for g in range(start, start + per_dot)
                ],
                axis=0,
            )
            y = jnp.dot(x, wbig_ref[...], preferred_element_type=F32)
            y = jnp.maximum(y + bias4, 0.0)
            for group in range(start, start + per_dot):
                at = HALO + v + 8 * group
                parts = []
                for k in range(2):
                    row = pa6_s[at + 4 * k : at + 4 * k + 1, 2 * F2 : 4 * F2]
                    row = jnp.broadcast_to(row, (16, 2 * F2)).astype(BF16)
                    parts.append(
                        jnp.maximum(row[None] + col_centre, zero).reshape(2 * bins, 2 * F2)
                    )
                centre = jnp.concatenate(parts, axis=1).astype(F32)
                at_row = (group - start) * 2 * bins
                mixed = y[at_row : at_row + 2 * bins] + centre
                mix_s[group, :, v * 4 * F2 : (v + 1) * 4 * F2] = mixed.astype(BF16)

    lane_live = side_ref[1:2, : 2 * F2] != 0
    for group in range(groups):
        value = lax.dot_general(
            head_ref[...], mix_s[group], (((1,), (1,)), ((), ())), preferred_element_type=F32
        )[:8]
        bin_index = i * bins + 8 * group + lax.broadcasted_iota(jnp.int32, (8, 2 * bins), 0)
        out_ref[8 * group : 8 * group + 8, :] = jnp.where(
            lane_live & (bin_index < length_ref[0]), value, 0.0
        )


def local(
    features,
    chrom_len,
    band_mask,
    conv_weight,
    conv_bias,
    proj_weight,
    proj_bias,
    map_weight,
    map_bias,
    head_weight,
):
    bins, half = features.shape
    rows = 2 * bins + 2 * HALO
    half_out = map_bias.shape[0]
    smem = pl.BlockSpec(memory_space=pltpu.SMEM)
    vmem = pl.BlockSpec(memory_space=pltpu.VMEM)
    anywhere = pl.BlockSpec(memory_space=pl.ANY)
    params = pltpu.CompilerParams(vmem_limit_bytes=24 * 1024 * 1024)

    def in_hbm(value):
        return pltpu.with_memory_space_constraint(value, pltpu.HBM)

    other = chan_swap(features)
    cb_oth = chan_swap(conv_bias)
    own, small = pl.pallas_call(
        front_kernel,
        out_shape=[
            jax.ShapeDtypeStruct(features.shape, BF16),
            jax.ShapeDtypeStruct((8, half), F32),
        ],
        in_specs=[anywhere] * 3,
        out_specs=[vmem] * 2,
        scratch_shapes=[
            pltpu.VMEM(conv_bias.shape, BF16),
            pltpu.VMEM((1, 2 * F2), BF16),
            pltpu.SemaphoreType.DMA((3,)),
        ],
        cost_estimate=pl.CostEstimate(flops=4000000000, bytes_accessed=1000000, transcendentals=0),
        compiler_params=params,
    )(in_hbm(features), in_hbm(conv_bias), in_hbm(proj_bias[None]))
    own, cb_oth = lax.optimization_barrier((jnp.stack([own, other]), cb_oth))
    even = pair_permute(own, 0)
    odd = pair_permute(own, 1)
    r2 = line_permute(own[:, :RIM], 2)
    w_in, own = lax.optimization_barrier((conv_weight, own))
    w_oth = chan_swap(w_in)
    window = pl.pallas_call(
        window_kernel,
        out_shape=jax.ShapeDtypeStruct((rows, 2 * half), F32),
        in_specs=[vmem] * 4,
        out_specs=vmem,
        cost_estimate=pl.CostEstimate(flops=4000000000, bytes_accessed=1000000, transcendentals=0),
        compiler_params=params,
    )(own, r2, even, odd)
    cols, both = pl.pallas_call(
        trunk_kernel,
        out_shape=[
            jax.ShapeDtypeStruct((bins + 2 * HALO, 2 * F2), BF16),
            jax.ShapeDtypeStruct((2 * bins + 4 * HALO, 2 * F2), BF16),
        ],
        in_specs=[smem] + [vmem] * 6,
        out_specs=[vmem] * 2,
        scratch_shapes=[pltpu.VMEM((rows, 2 * half), F32)],
        compiler_params=params,
    )(chrom_len, window, conv_weight, proj_weight, w_oth, small, cb_oth)
    cols_far = line_permute(cols, 2)
    near_both = chan_swap(both)
    mask, packed = pl.pallas_call(
        pack_kernel,
        out_shape=[
            jax.ShapeDtypeStruct(band_mask.shape[::-1], jnp.int32),
            jax.ShapeDtypeStruct((9 * half_out, 2 * F2), BF16),
        ],
        in_specs=[anywhere] * 5,
        out_specs=[vmem] * 2,
        scratch_shapes=[
            pltpu.VMEM(map_weight.shape, BF16),
            pltpu.VMEM((1, half_out), BF16),
            pltpu.VMEM((1, half_out), BF16),
            pltpu.VMEM((32, 2 * F2), F32),
            pltpu.SemaphoreType.DMA((4,)),
        ],
        compiler_params=params,
    )(
        own,
        in_hbm(band_mask.T),
        in_hbm(map_weight),
        in_hbm(map_bias[None]),
        in_hbm(head_weight[None]),
    )
    oth = chan_swap(packed)
    prepared = pl.pallas_call(
        prep_kernel,
        out_shape=[
            jax.ShapeDtypeStruct((3, 2 * bins, 6 * F2), F32),
            jax.ShapeDtypeStruct((18 * F2, 4 * F2), BF16),
            jax.ShapeDtypeStruct((8, half), F32),
            jax.ShapeDtypeStruct((16, 8 * F2), BF16),
        ],
        in_specs=[smem] + [vmem] * 3,
        out_specs=[vmem] * 4,
        scratch_shapes=[
            pltpu.VMEM((4 * F2, 18 * F2), F32),
            pltpu.VMEM((9, F2, F2), F32),
        ],
        compiler_params=params,
    )(chrom_len, mask, packed, oth)
    tiles = functools.partial(
        pl.pallas_call,
        out_shape=jax.ShapeDtypeStruct((bins, 2 * bins), F32),
        out_specs=vmem,
        scratch_shapes=[
            pltpu.VMEM((bins + 2 * HALO, 6 * F2), F32),
            pltpu.VMEM((bins // 8, 2 * bins, 8 * F2), BF16),
        ],
        compiler_params=params,
    )
    near = tiles(near_kernel, in_specs=[smem] + [vmem] * 6)(
        chrom_len, near_both, near_both, *prepared
    )
    return tiles(far_kernel, in_specs=[vmem, smem] + [vmem] * 6)(
        near, chrom_len, cols_far, both, *prepared
    )


def solution(mesh):
    return jax.shard_map(
        local,
        mesh=mesh,
        in_specs=(
            P(("dp", "blk"), "chan"),
            P("dp"),
            P("dp", None),
            P(None, None, None, "chan"),
            P(None, "chan"),
            P(),
            P(),
            P(None, None, "chan", None),
            P("chan"),
            P("chan"),
        ),
        out_specs=P(("dp", "blk"), "chan"),
        check_vma=False,
    )
```

```python
import functools

import jax
import jax.numpy as jnp
from jax import lax
from jax.experimental import pallas as pl
from jax.experimental.pallas import tpu as pltpu
from jax.sharding import PartitionSpec as P

F2 = 64
BAND = 3
CONV1 = 2
D2 = 2
HALO = 8
RIM = 16
F32 = jnp.float32
BF16 = jnp.bfloat16


def chan_swap(value):
    return lax.ppermute(value, "chan", [(0, 1), (1, 0)])


def line_permute(value, step):
    count = lax.axis_size("blk")
    pairs = []
    for i in range(count):
        pairs.append(((i - step) * 2 if i >= step else i * 2 + 1, i * 2))
        pairs.append(((i + step) * 2 + 1 if i + step < count else i * 2, i * 2 + 1))
    return lax.ppermute(value, ("blk", "chan"), pairs)


def pair_permute(value, low):
    count = lax.axis_size("blk")
    source = {}
    for i in range(count):
        source[i, 0] = (i ^ 1, 0)
    for i in range(low, count - 1, 2):
        source[i, 1], source[i + 1, 1] = (i + 1, 1), (i, 1)
    for i in range(count):
        if (i, 1) not in source:
            source[i, 1] = (i ^ 1, 0)
            source[i, 0] = (i, 1)
    pairs = [(j * 2 + d, i * 2 + c) for (i, c), (j, d) in source.items()]
    return lax.ppermute(value, ("blk", "chan"), pairs)


def front_kernel(own_any, cb_any, pb_any, own_ref, small_ref, cb_s, pb_s, sems):
    pairs = ((cb_any, cb_s), (pb_any, pb_s), (own_any, own_ref))
    copies = [
        pltpu.make_async_copy(source, target, sems.at[at])
        for at, (source, target) in enumerate(pairs)
    ]
    for copy in copies:
        copy.start()
    copies[0].wait()
    copies[1].wait()
    small_ref[0:CONV1, :] = cb_s[...].astype(F32)
    small_ref[CONV1 : CONV1 + 1, : 2 * F2] = pb_s[...].astype(F32)
    copies[2].wait()


def pack_kernel(
    after_any,
    mask_any,
    mw_any,
    mb_any,
    hw_any,
    mask_ref,
    packed_ref,
    mw_s,
    mb_s,
    hw_s,
    extra_s,
    sems,
):
    pairs = ((mw_any, mw_s), (mb_any, mb_s), (hw_any, hw_s), (mask_any, mask_ref))
    copies = [
        pltpu.make_async_copy(source, target, sems.at[at])
        for at, (source, target) in enumerate(pairs)
    ]
    for copy in copies:
        copy.start()
    extra_s[...] = jnp.zeros_like(extra_s)
    for copy in copies:
        copy.wait()

    half = mw_any.shape[2]
    extra_s[8:9, :half] = mb_s[...].astype(F32)
    extra_s[9:10, :half] = hw_s[...].astype(F32)
    extra = pltpu.roll(extra_s[...], F2, axis=1)
    for s in range(3):
        for r in range(3):
            at = (3 * s + r) * half
            packed_ref[at : at + half, :F2] = mw_s[s, r]
    packed_ref[:32, F2:] = extra[:, F2:].astype(BF16)


def prep_kernel(
    length_ref,
    mask_ref,
    own_ref,
    oth_ref,
    col_mask_ref,
    wbig_ref,
    side_ref,
    head_ref,
    wt_s,
    taps_s,
):
    half = own_ref.shape[0] // 9
    columns = col_mask_ref.shape[1]
    bins = columns // 2
    count = lax.axis_size("blk")
    i = lax.axis_index("blk")
    c = lax.axis_index("chan")
    first_col = i * bins + c * columns
    length = length_ref[0]

    for source, side in ((own_ref, c), (oth_ref, 1 - c)):
        at = pl.ds(pl.multiple_of(side * half, half), half)
        for tap in range(9):
            taps_s[tap, at, :] = source[tap * half : (tap + 1) * half, :F2].astype(F32)
    blank = jnp.zeros((F2, F2), F32)
    for j in range(4):
        pieces = []
        for m in range(6):
            for r in range(3):
                pieces.append(taps_s[3 * (m - j) + r] if 0 <= m - j < 3 else blank)
        for tile in range(9):
            wt_s[j * F2 : (j + 1) * F2, tile * 2 * F2 : (tile + 1) * 2 * F2] = jnp.concatenate(
                pieces[2 * tile : 2 * tile + 2], axis=1
            )
    wbig_ref[...] = wt_s[...].T.astype(BF16)

    def spread(row, repeats):
        o = lax.broadcasted_iota(jnp.int32, (2 * F2, repeats * F2), 0)
        lane = lax.broadcasted_iota(jnp.int32, (2 * F2, repeats * F2), 1) % F2
        total = jnp.zeros((16, repeats * F2), F32)
        for ref, side in ((own_ref, c), (oth_ref, 1 - c)):
            pick = ((lane == side * half + o - F2) & (o >= F2) & (o < F2 + half)).astype(BF16)
            value = ref[:16, :].astype(F32)[row : row + 1]
            value = jnp.broadcast_to(value, (16, 2 * F2)).astype(BF16)
            total = total + jnp.dot(value, pick, preferred_element_type=F32)
        return total

    q = lax.broadcasted_iota(jnp.int32, (16, 8 * F2), 0)
    k = lax.broadcasted_iota(jnp.int32, (16, 8 * F2), 1)
    head_ref[...] = jnp.where(
        q == 2 * ((k % (4 * F2)) // F2) + k // (4 * F2), spread(9, 8), 0.0
    ).astype(BF16)
    side_ref[0:1, :] = spread(8, 4)[:1]
    minus = F32(-jnp.inf)
    block = lax.broadcasted_iota(jnp.int32, (BAND + 1, count), 1)

    def live_at(y, variant):
        at_row = jnp.sum(jnp.where(block == i + variant, mask_ref[...], 0), axis=1, keepdims=True)
        offset = lax.broadcasted_iota(jnp.int32, (BAND + 1, 1), 0)

        def entry(u):
            return jnp.sum(
                jnp.where(offset == 2 * c + u - variant, at_row, 0), axis=0, keepdims=True
            )

        value = jnp.where(
            y < 0,
            entry(-1),
            jnp.where(y < bins, entry(0), jnp.where(y < columns, entry(1), entry(2))),
        )
        column = first_col + y
        return (value != 0) & (column >= 0) & (column < length)

    b_index = lax.broadcasted_iota(jnp.int32, (columns, 2 * F2), 0)
    low = lax.broadcasted_iota(jnp.int32, (columns, 2 * F2), 1) < F2
    masks = {}
    for variant in (-1, 0, 1):
        for r in range(3):
            masks[variant, r] = jnp.where(
                live_at(b_index + (r - 1) * D2, variant), 0.0, minus
            )
    for at, (v0, v1) in enumerate(((-1, 0), (0, 0), (0, 1))):
        col_mask_ref[at, :, : 2 * F2] = jnp.where(low, masks[v0, 0], masks[v0, 1])
        col_mask_ref[at, :, 2 * F2 : 4 * F2] = jnp.where(low, masks[v0, 2], masks[v1, 0])
        col_mask_ref[at, :, 4 * F2 :] = jnp.where(low, masks[v1, 1], masks[v1, 2])

    side_ref[1:2, : 2 * F2] = jnp.where(
        live_at(lax.broadcasted_iota(jnp.int32, (1, columns), 1), 0), 1.0, 0.0
    )


def window_kernel(own_ref, r2_ref, even_ref, odd_ref, h_ref):
    core = lax.axis_index("chan")
    parity = lax.rem(lax.axis_index("blk"), 2)
    bins = own_ref.shape[1]
    half = own_ref.shape[2]

    def fill(before_ref, after_ref):
        for part in range(2):
            lanes = slice(part * half, (part + 1) * half)
            held = 1 - part
            before = before_ref[held, bins - RIM :, :].astype(F32)
            h_ref[:HALO, lanes] = before[RIM - HALO :]
            h_ref[HALO : HALO + bins, lanes] = own_ref[held].astype(F32)
            h_ref[HALO + bins : HALO + 2 * bins, lanes] = after_ref[held].astype(F32)
            h_ref[HALO + 2 * bins :, lanes] = r2_ref[held].astype(F32)[:HALO]

    @pl.when((core == 1) & (parity == 0))
    def _():
        fill(odd_ref, even_ref)

    @pl.when((core == 1) & (parity == 1))
    def _():
        fill(even_ref, odd_ref)


def trunk_kernel(*refs):
    @pl.when(lax.axis_index("chan") == 0)
    def _():
        for ref in refs[-3:-1]:
            ref[...] = jnp.zeros_like(ref)

    @pl.when(lax.axis_index("chan") == 1)
    def _():
        trunk(*refs)


def trunk(
    length_ref,
    window_ref,
    w_own_ref,
    pw_ref,
    w_oth_ref,
    small_ref,
    cb_oth_ref,
    cols_ref,
    both_ref,
    h_s,
):
    rows = window_ref.shape[0]
    half = window_ref.shape[1] // 2
    held = cols_ref.shape[0]
    bins = held - 2 * HALO
    count = lax.axis_size("blk")
    i = lax.axis_index("blk")
    bin_index = i * bins - HALO + lax.broadcasted_iota(jnp.int32, (rows, 2 * F2), 0)
    valid = (bin_index >= 0) & (bin_index < length_ref[0])
    inside = ((bin_index >= 0) & (bin_index < count * bins))[:, :1]

    for at in range(0, 2 * half, 128):
        h_s[:, at : at + 128] = jnp.where(valid, window_ref[:, at : at + 128], 0.0)

    for layer in range(CONV1):
        e = 2 ** (layer + 1)
        hidden = h_s[...]
        taps = [
            (hidden if t == 1 else pltpu.roll(hidden, ((1 - t) * e) % rows, axis=0)).astype(BF16)
            for t in range(3)
        ]
        for at, w_ref, bias_ref in ((half, w_own_ref, small_ref), (0, w_oth_ref, cb_oth_ref)):
            q = jnp.dot(taps[0], w_ref[layer, 0], preferred_element_type=F32)
            q = q + jnp.dot(taps[1], w_ref[layer, 1], preferred_element_type=F32)
            q = q + jnp.dot(taps[2], w_ref[layer, 2], preferred_element_type=F32)
            bias = bias_ref[...].astype(F32)[layer : layer + 1, :]
            lanes = slice(at, at + half)
            new = (h_s[:, lanes] + jnp.maximum(q + bias, 0.0)).astype(BF16).astype(F32)
            h_s[:, lanes] = jnp.where(inside, new, 0.0)

    proj = jnp.dot(h_s[...].astype(BF16), pw_ref[...], preferred_element_type=F32)
    proj = (proj + small_ref[CONV1 : CONV1 + 1, : 2 * F2]).astype(BF16).astype(F32)
    low = lax.broadcasted_iota(jnp.int32, (1, 2 * F2), 1) < F2
    turned = pltpu.roll(proj, F2, axis=1)
    cols = jnp.where(low, turned[:held], proj[rows - held :]).astype(BF16)
    cols_ref[...] = cols
    both_ref[:held, :] = cols
    both_ref[held:, :] = jnp.where(valid, jnp.where(low, proj, turned), -jnp.inf)[:held].astype(
        BF16
    )


def near_kernel(*refs):
    @pl.when(lax.axis_index("chan") == 0)
    def _():
        contact_tiles(*refs)


def far_kernel(near_ref, *refs):
    @pl.when(lax.axis_index("chan") == 0)
    def _():
        refs[7][...] = near_ref[...]

    @pl.when(lax.axis_index("chan") == 1)
    def _():
        contact_tiles(*refs)


def contact_tiles(
    length_ref,
    cols_ref,
    rows_ref,
    col_mask_ref,
    wbig_ref,
    side_ref,
    head_ref,
    out_ref,
    pa6_s,
    mix_s,
):
    bins = out_ref.shape[0]
    col_rows = 2 * bins + 2 * HALO
    row_rows = bins + 2 * HALO
    i = lax.axis_index("blk")

    low = lax.broadcasted_iota(jnp.int32, (1, 2 * F2), 1) < F2
    held = bins + 2 * HALO
    pcol = cols_ref[: bins + 2 * HALO, :].astype(F32)
    turned = pltpu.roll(pcol, F2, axis=1)
    pcol = jnp.concatenate(
        [jnp.where(low, pcol, turned), jnp.where(low, turned, pcol)[2 * held - col_rows :]], axis=0
    )
    shifted = [
        pltpu.roll(pcol, col_rows - HALO - (r - 1) * D2, axis=0)[: 2 * bins] for r in range(3)
    ]
    tiles = [
        jnp.where(low, shifted[0], shifted[1]),
        jnp.where(low, shifted[2], shifted[0]),
        jnp.where(low, shifted[1], shifted[2]),
    ]
    tiled = jnp.concatenate(tiles, axis=1)
    col_first, col_mid, col_last = [
        (tiled + col_mask_ref[at]).astype(BF16).reshape(2 * bins // 16, 16, 6 * F2)
        for at in range(3)
    ]
    col_centre = shifted[1].astype(BF16).reshape(2 * bins // 16, 16, 2 * F2)

    prow = rows_ref[row_rows:, :].astype(F32)
    prow_next = pltpu.roll(prow, row_rows - D2, axis=0)
    pa6_s[:, : 2 * F2] = prow
    pa6_s[:, 2 * F2 : 4 * F2] = jnp.where(low, prow, prow_next)
    pa6_s[:, 4 * F2 :] = prow_next

    groups = bins // 8
    per_dot = 4
    zero = jnp.zeros((), BF16)
    bias4 = side_ref[0:1, :]
    for v in range(2):
        for start in range(0, groups, per_dot):
            values = {}
            for slot in range(2 * start, 2 * (start + per_dot) + 1):
                at = HALO - D2 + v + 4 * slot
                row = jnp.broadcast_to(pa6_s[at : at + 1, :], (16, 6 * F2)).astype(BF16)
                cols = col_first if slot == 0 else col_last if slot == 2 * groups else col_mid
                values[slot] = jnp.maximum(row[None] + cols, zero).reshape(2 * bins, 6 * F2)
            x = jnp.concatenate(
                [
                    jnp.concatenate([values[2 * g + s] for s in range(3)], axis=1)
                    for g in range(start, start + per_dot)
                ],
                axis=0,
            )
            y = jnp.dot(x, wbig_ref[...], preferred_element_type=F32)
            y = jnp.maximum(y + bias4, 0.0)
            for group in range(start, start + per_dot):
                at = HALO + v + 8 * group
                parts = []
                for k in range(2):
                    row = pa6_s[at + 4 * k : at + 4 * k + 1, 2 * F2 : 4 * F2]
                    row = jnp.broadcast_to(row, (16, 2 * F2)).astype(BF16)
                    parts.append(
                        jnp.maximum(row[None] + col_centre, zero).reshape(2 * bins, 2 * F2)
                    )
                centre = jnp.concatenate(parts, axis=1).astype(F32)
                at_row = (group - start) * 2 * bins
                mixed = y[at_row : at_row + 2 * bins] + centre
                mix_s[group, :, v * 4 * F2 : (v + 1) * 4 * F2] = mixed.astype(BF16)

    lane_live = side_ref[1:2, : 2 * F2] != 0
    for group in range(groups):
        value = lax.dot_general(
            head_ref[...], mix_s[group], (((1,), (1,)), ((), ())), preferred_element_type=F32
        )[:8]
        bin_index = i * bins + 8 * group + lax.broadcasted_iota(jnp.int32, (8, 2 * bins), 0)
        out_ref[8 * group : 8 * group + 8, :] = jnp.where(
            lane_live & (bin_index < length_ref[0]), value, 0.0
        )


def local(
    features,
    chrom_len,
    band_mask,
    conv_weight,
    conv_bias,
    proj_weight,
    proj_bias,
    map_weight,
    map_bias,
    head_weight,
):
    bins, half = features.shape
    rows = 2 * bins + 2 * HALO
    half_out = map_bias.shape[0]
    smem = pl.BlockSpec(memory_space=pltpu.SMEM)
    vmem = pl.BlockSpec(memory_space=pltpu.VMEM)
    anywhere = pl.BlockSpec(memory_space=pl.ANY)
    params = pltpu.CompilerParams(vmem_limit_bytes=24 * 1024 * 1024)

    def in_hbm(value):
        return pltpu.with_memory_space_constraint(value, pltpu.HBM)

    other = chan_swap(features)
    cb_oth = chan_swap(conv_bias)
    own, small = pl.pallas_call(
        front_kernel,
        out_shape=[
            jax.ShapeDtypeStruct(features.shape, BF16),
            jax.ShapeDtypeStruct((8, half), F32),
        ],
        in_specs=[anywhere] * 3,
        out_specs=[vmem] * 2,
        scratch_shapes=[
            pltpu.VMEM(conv_bias.shape, BF16),
            pltpu.VMEM((1, 2 * F2), BF16),
            pltpu.SemaphoreType.DMA((3,)),
        ],
        cost_estimate=pl.CostEstimate(flops=4000000000, bytes_accessed=1000000, transcendentals=0),
        compiler_params=params,
    )(in_hbm(features), in_hbm(conv_bias), in_hbm(proj_bias[None]))
    own, cb_oth = lax.optimization_barrier((jnp.stack([own, other]), cb_oth))
    even = pair_permute(own, 0)
    odd = pair_permute(own, 1)
    r2 = line_permute(own[:, :RIM], 2)
    w_in, own = lax.optimization_barrier((conv_weight, own))
    w_oth = chan_swap(w_in)
    window = pl.pallas_call(
        window_kernel,
        out_shape=jax.ShapeDtypeStruct((rows, 2 * half), F32),
        in_specs=[vmem] * 4,
        out_specs=vmem,
        cost_estimate=pl.CostEstimate(flops=4000000000, bytes_accessed=1000000, transcendentals=0),
        compiler_params=params,
    )(own, r2, even, odd)
    cols, both = pl.pallas_call(
        trunk_kernel,
        out_shape=[
            jax.ShapeDtypeStruct((bins + 2 * HALO, 2 * F2), BF16),
            jax.ShapeDtypeStruct((2 * bins + 4 * HALO, 2 * F2), BF16),
        ],
        in_specs=[smem] + [vmem] * 6,
        out_specs=[vmem] * 2,
        scratch_shapes=[pltpu.VMEM((rows, 2 * half), F32)],
        compiler_params=params,
    )(chrom_len, window, conv_weight, proj_weight, w_oth, small, cb_oth)
    cols_far = line_permute(cols, 2)
    near_both = chan_swap(both)
    mask, packed = pl.pallas_call(
        pack_kernel,
        out_shape=[
            jax.ShapeDtypeStruct(band_mask.shape[::-1], jnp.int32),
            jax.ShapeDtypeStruct((9 * half_out, 2 * F2), BF16),
        ],
        in_specs=[anywhere] * 5,
        out_specs=[vmem] * 2,
        scratch_shapes=[
            pltpu.VMEM(map_weight.shape, BF16),
            pltpu.VMEM((1, half_out), BF16),
            pltpu.VMEM((1, half_out), BF16),
            pltpu.VMEM((32, 2 * F2), F32),
            pltpu.SemaphoreType.DMA((4,)),
        ],
        compiler_params=params,
    )(
        own,
        in_hbm(band_mask.T),
        in_hbm(map_weight),
        in_hbm(map_bias[None]),
        in_hbm(head_weight[None]),
    )
    oth = chan_swap(packed)
    prepared = pl.pallas_call(
        prep_kernel,
        out_shape=[
            jax.ShapeDtypeStruct((3, 2 * bins, 6 * F2), F32),
            jax.ShapeDtypeStruct((18 * F2, 4 * F2), BF16),
            jax.ShapeDtypeStruct((8, half), F32),
            jax.ShapeDtypeStruct((16, 8 * F2), BF16),
        ],
        in_specs=[smem] + [vmem] * 3,
        out_specs=[vmem] * 4,
        scratch_shapes=[
            pltpu.VMEM((4 * F2, 18 * F2), F32),
            pltpu.VMEM((9, F2, F2), F32),
        ],
        compiler_params=params,
    )(chrom_len, mask, packed, oth)
    tiles = functools.partial(
        pl.pallas_call,
        out_shape=jax.ShapeDtypeStruct((bins, 2 * bins), F32),
        out_specs=vmem,
        scratch_shapes=[
            pltpu.VMEM((bins + 2 * HALO, 6 * F2), F32),
            pltpu.VMEM((bins // 8, 2 * bins, 8 * F2), BF16),
        ],
        compiler_params=params,
    )
    near = tiles(near_kernel, in_specs=[smem] + [vmem] * 6)(
        chrom_len, near_both, near_both, *prepared
    )
    return tiles(far_kernel, in_specs=[vmem, smem] + [vmem] * 6)(
        near, chrom_len, cols_far, both, *prepared
    )


def solution(mesh):
    return jax.shard_map(
        local,
        mesh=mesh,
        in_specs=(
            P(("dp", "blk"), "chan"),
            P("dp"),
            P("dp", None),
            P(None, None, None, "chan"),
            P(None, "chan"),
            P(),
            P(),
            P(None, None, "chan", None),
            P("chan"),
            P("chan"),
        ),
        out_specs=P(("dp", "blk"), "chan"),
        check_vma=False,
    )
```

```python
import functools

import jax
import jax.numpy as jnp
from jax import lax
from jax.experimental import pallas as pl
from jax.experimental.pallas import tpu as pltpu
from jax.sharding import PartitionSpec as P

F2 = 64
BAND = 3
CONV1 = 2
D2 = 2
HALO = 8
RIM = 16
F32 = jnp.float32
BF16 = jnp.bfloat16


def chan_swap(value):
    return lax.ppermute(value, "chan", [(0, 1), (1, 0)])


def line_permute(value, step):
    count = lax.axis_size("blk")
    pairs = []
    for i in range(count):
        pairs.append(((i - step) * 2 if i >= step else i * 2 + 1, i * 2))
        pairs.append(((i + step) * 2 + 1 if i + step < count else i * 2, i * 2 + 1))
    return lax.ppermute(value, ("blk", "chan"), pairs)


def pair_permute(value, low):
    count = lax.axis_size("blk")
    source = {}
    for i in range(count):
        source[i, 0] = (i ^ 1, 0)
    for i in range(low, count - 1, 2):
        source[i, 1], source[i + 1, 1] = (i + 1, 1), (i, 1)
    for i in range(count):
        if (i, 1) not in source:
            source[i, 1] = (i ^ 1, 0)
            source[i, 0] = (i, 1)
    pairs = [(j * 2 + d, i * 2 + c) for (i, c), (j, d) in source.items()]
    return lax.ppermute(value, ("blk", "chan"), pairs)


def front_kernel(own_any, cb_any, pb_any, own_ref, small_ref, cb_s, pb_s, sems):
    pairs = ((cb_any, cb_s), (pb_any, pb_s), (own_any, own_ref))
    copies = [
        pltpu.make_async_copy(source, target, sems.at[at])
        for at, (source, target) in enumerate(pairs)
    ]
    for copy in copies:
        copy.start()
    copies[0].wait()
    copies[1].wait()
    small_ref[0:CONV1, :] = cb_s[...].astype(F32)
    small_ref[CONV1 : CONV1 + 1, : 2 * F2] = pb_s[...].astype(F32)
    copies[2].wait()


def pack_kernel(
    after_any,
    mask_any,
    mw_any,
    mb_any,
    hw_any,
    mask_ref,
    packed_ref,
    mw_s,
    mb_s,
    hw_s,
    extra_s,
    sems,
):
    pairs = ((mw_any, mw_s), (mb_any, mb_s), (hw_any, hw_s), (mask_any, mask_ref))
    copies = [
        pltpu.make_async_copy(source, target, sems.at[at])
        for at, (source, target) in enumerate(pairs)
    ]
    for copy in copies:
        copy.start()
    extra_s[...] = jnp.zeros_like(extra_s)
    for copy in copies:
        copy.wait()

    half = mw_any.shape[2]
    extra_s[8:9, :half] = mb_s[...].astype(F32)
    extra_s[9:10, :half] = hw_s[...].astype(F32)
    extra = pltpu.roll(extra_s[...], F2, axis=1)
    for s in range(3):
        for r in range(3):
            at = (3 * s + r) * half
            packed_ref[at : at + half, :F2] = mw_s[s, r]
    packed_ref[:32, F2:] = extra[:, F2:].astype(BF16)


def prep_kernel(
    length_ref,
    mask_ref,
    own_ref,
    oth_ref,
    col_mask_ref,
    wbig_ref,
    side_ref,
    head_ref,
    wt_s,
    taps_s,
):
    half = own_ref.shape[0] // 9
    behind = oth_ref.shape[0] - own_ref.shape[0]
    columns = col_mask_ref.shape[1]
    bins = columns // 2
    count = lax.axis_size("blk")
    i = lax.axis_index("blk")
    c = lax.axis_index("chan")
    first_col = i * bins + c * columns
    length = length_ref[0]

    for source, skip, side in ((own_ref, 0, c), (oth_ref, behind, 1 - c)):
        at = pl.ds(pl.multiple_of(side * half, half), half)
        for tap in range(9):
            row = skip + tap * half
            taps_s[tap, at, :] = source[row : row + half, :F2].astype(F32)
    blank = jnp.zeros((F2, F2), F32)
    for j in range(4):
        pieces = []
        for m in range(6):
            for r in range(3):
                pieces.append(taps_s[3 * (m - j) + r] if 0 <= m - j < 3 else blank)
        for tile in range(9):
            wt_s[j * F2 : (j + 1) * F2, tile * 2 * F2 : (tile + 1) * 2 * F2] = jnp.concatenate(
                pieces[2 * tile : 2 * tile + 2], axis=1
            )
    wbig_ref[...] = wt_s[...].T.astype(BF16)

    def spread(row, repeats):
        o = lax.broadcasted_iota(jnp.int32, (2 * F2, repeats * F2), 0)
        lane = lax.broadcasted_iota(jnp.int32, (2 * F2, repeats * F2), 1) % F2
        total = jnp.zeros((16, repeats * F2), F32)
        for ref, skip, side in ((own_ref, 0, c), (oth_ref, behind, 1 - c)):
            pick = ((lane == side * half + o - F2) & (o >= F2) & (o < F2 + half)).astype(BF16)
            value = ref[skip : skip + 16, :].astype(F32)[row : row + 1]
            value = jnp.broadcast_to(value, (16, 2 * F2)).astype(BF16)
            total = total + jnp.dot(value, pick, preferred_element_type=F32)
        return total

    q = lax.broadcasted_iota(jnp.int32, (16, 8 * F2), 0)
    k = lax.broadcasted_iota(jnp.int32, (16, 8 * F2), 1)
    head_ref[...] = jnp.where(
        q == 2 * ((k % (4 * F2)) // F2) + k // (4 * F2), spread(9, 8), 0.0
    ).astype(BF16)
    side_ref[0:1, :] = spread(8, 4)[:1]
    minus = F32(-jnp.inf)
    block = lax.broadcasted_iota(jnp.int32, (BAND + 1, count), 1)

    def live_at(y, variant):
        at_row = jnp.sum(jnp.where(block == i + variant, mask_ref[...], 0), axis=1, keepdims=True)
        offset = lax.broadcasted_iota(jnp.int32, (BAND + 1, 1), 0)

        def entry(u):
            return jnp.sum(
                jnp.where(offset == 2 * c + u - variant, at_row, 0), axis=0, keepdims=True
            )

        value = jnp.where(
            y < 0,
            entry(-1),
            jnp.where(y < bins, entry(0), jnp.where(y < columns, entry(1), entry(2))),
        )
        column = first_col + y
        return (value != 0) & (column >= 0) & (column < length)

    b_index = lax.broadcasted_iota(jnp.int32, (columns, 2 * F2), 0)
    low = lax.broadcasted_iota(jnp.int32, (columns, 2 * F2), 1) < F2
    masks = {}
    for variant in (-1, 0, 1):
        for r in range(3):
            masks[variant, r] = jnp.where(
                live_at(b_index + (r - 1) * D2, variant), 0.0, minus
            )
    for at, (v0, v1) in enumerate(((-1, 0), (0, 0), (0, 1))):
        col_mask_ref[at, :, : 2 * F2] = jnp.where(low, masks[v0, 0], masks[v0, 1])
        col_mask_ref[at, :, 2 * F2 : 4 * F2] = jnp.where(low, masks[v0, 2], masks[v1, 0])
        col_mask_ref[at, :, 4 * F2 :] = jnp.where(low, masks[v1, 1], masks[v1, 2])

    side_ref[1:2, : 2 * F2] = jnp.where(
        live_at(lax.broadcasted_iota(jnp.int32, (1, columns), 1), 0), 1.0, 0.0
    )


def window_kernel(own_ref, r2_ref, odd_ref, even_ref, h_ref):
    core = lax.axis_index("chan")
    parity = lax.rem(lax.axis_index("blk"), 2)
    bins = own_ref.shape[1]
    half = own_ref.shape[2]

    def fill(before_ref, after_ref):
        for part in range(2):
            lanes = slice(part * half, (part + 1) * half)
            held = 1 - part
            before = before_ref[held, bins - RIM :, :].astype(F32)
            h_ref[:HALO, lanes] = before[RIM - HALO :]
            h_ref[HALO : HALO + bins, lanes] = own_ref[held].astype(F32)
            h_ref[HALO + bins : HALO + 2 * bins, lanes] = after_ref[held].astype(F32)
            h_ref[HALO + 2 * bins :, lanes] = r2_ref[held].astype(F32)[:HALO]

    @pl.when((core == 1) & (parity == 0))
    def _():
        fill(odd_ref, even_ref)

    @pl.when((core == 1) & (parity == 1))
    def _():
        fill(even_ref, odd_ref)


def trunk_kernel(*refs):
    packed_ref, cols_ref, both_ref = refs[-4:-1]
    ready = both_ref.shape[0] - packed_ref.shape[0]
    both_ref[ready:, :] = packed_ref[...]

    @pl.when(lax.axis_index("chan") == 0)
    def _():
        cols_ref[...] = jnp.zeros_like(cols_ref)
        both_ref[:ready, :] = jnp.zeros((ready, 2 * F2), BF16)

    @pl.when(lax.axis_index("chan") == 1)
    def _():
        trunk(*refs)


def trunk(
    length_ref,
    window_ref,
    w_own_ref,
    pw_ref,
    w_oth_ref,
    small_ref,
    cb_oth_ref,
    packed_ref,
    cols_ref,
    both_ref,
    h_s,
):
    rows = window_ref.shape[0]
    half = window_ref.shape[1] // 2
    held = cols_ref.shape[0]
    bins = held - 2 * HALO
    count = lax.axis_size("blk")
    i = lax.axis_index("blk")
    bin_index = i * bins - HALO + lax.broadcasted_iota(jnp.int32, (rows, 2 * F2), 0)
    valid = (bin_index >= 0) & (bin_index < length_ref[0])
    inside = ((bin_index >= 0) & (bin_index < count * bins))[:, :1]

    for at in range(0, 2 * half, 128):
        h_s[:, at : at + 128] = jnp.where(valid, window_ref[:, at : at + 128], 0.0)

    for layer in range(CONV1):
        e = 2 ** (layer + 1)
        hidden = h_s[...]
        taps = [
            (hidden if t == 1 else pltpu.roll(hidden, ((1 - t) * e) % rows, axis=0)).astype(BF16)
            for t in range(3)
        ]
        for at, w_ref, bias_ref in ((half, w_own_ref, small_ref), (0, w_oth_ref, cb_oth_ref)):
            q = jnp.dot(taps[0], w_ref[layer, 0], preferred_element_type=F32)
            q = q + jnp.dot(taps[1], w_ref[layer, 1], preferred_element_type=F32)
            q = q + jnp.dot(taps[2], w_ref[layer, 2], preferred_element_type=F32)
            bias = bias_ref[...].astype(F32)[layer : layer + 1, :]
            lanes = slice(at, at + half)
            new = (h_s[:, lanes] + jnp.maximum(q + bias, 0.0)).astype(BF16).astype(F32)
            h_s[:, lanes] = jnp.where(inside, new, 0.0)

    proj = jnp.dot(h_s[...].astype(BF16), pw_ref[...], preferred_element_type=F32)
    proj = (proj + small_ref[CONV1 : CONV1 + 1, : 2 * F2]).astype(BF16).astype(F32)
    low = lax.broadcasted_iota(jnp.int32, (1, 2 * F2), 1) < F2
    turned = pltpu.roll(proj, F2, axis=1)
    cols = jnp.where(low, turned[:held], proj[rows - held :]).astype(BF16)
    cols_ref[...] = cols
    both_ref[:held, :] = cols
    both_ref[held : 2 * held, :] = jnp.where(valid, jnp.where(low, proj, turned), -jnp.inf)[:held].astype(
        BF16
    )


def near_kernel(*refs):
    @pl.when(lax.axis_index("chan") == 0)
    def _():
        contact_tiles(*refs)


def far_kernel(near_ref, *refs):
    @pl.when(lax.axis_index("chan") == 0)
    def _():
        refs[7][...] = near_ref[...]

    @pl.when(lax.axis_index("chan") == 1)
    def _():
        contact_tiles(*refs)


def contact_tiles(
    length_ref,
    cols_ref,
    rows_ref,
    col_mask_ref,
    wbig_ref,
    side_ref,
    head_ref,
    out_ref,
    pa6_s,
    mix_s,
):
    bins = out_ref.shape[0]
    col_rows = 2 * bins + 2 * HALO
    row_rows = bins + 2 * HALO
    i = lax.axis_index("blk")

    low = lax.broadcasted_iota(jnp.int32, (1, 2 * F2), 1) < F2
    held = bins + 2 * HALO
    pcol = cols_ref[: bins + 2 * HALO, :].astype(F32)
    turned = pltpu.roll(pcol, F2, axis=1)
    pcol = jnp.concatenate(
        [jnp.where(low, pcol, turned), jnp.where(low, turned, pcol)[2 * held - col_rows :]], axis=0
    )
    shifted = [
        pltpu.roll(pcol, col_rows - HALO - (r - 1) * D2, axis=0)[: 2 * bins] for r in range(3)
    ]
    tiles = [
        jnp.where(low, shifted[0], shifted[1]),
        jnp.where(low, shifted[2], shifted[0]),
        jnp.where(low, shifted[1], shifted[2]),
    ]
    tiled = jnp.concatenate(tiles, axis=1)
    col_first, col_mid, col_last = [
        (tiled + col_mask_ref[at]).astype(BF16).reshape(2 * bins // 16, 16, 6 * F2)
        for at in range(3)
    ]
    col_centre = shifted[1].astype(BF16).reshape(2 * bins // 16, 16, 2 * F2)

    prow = rows_ref[row_rows : 2 * row_rows, :].astype(F32)
    prow_next = pltpu.roll(prow, row_rows - D2, axis=0)
    pa6_s[:, : 2 * F2] = prow
    pa6_s[:, 2 * F2 : 4 * F2] = jnp.where(low, prow, prow_next)
    pa6_s[:, 4 * F2 :] = prow_next

    groups = bins // 8
    per_dot = 4
    zero = jnp.zeros((), BF16)
    bias4 = side_ref[0:1, :]
    for v in range(2):
        for start in range(0, groups, per_dot):
            values = {}
            for slot in range(2 * start, 2 * (start + per_dot) + 1):
                at = HALO - D2 + v + 4 * slot
                row = jnp.broadcast_to(pa6_s[at : at + 1, :], (16, 6 * F2)).astype(BF16)
                cols = col_first if slot == 0 else col_last if slot == 2 * groups else col_mid
                values[slot] = jnp.maximum(row[None] + cols, zero).reshape(2 * bins, 6 * F2)
            x = jnp.concatenate(
                [
                    jnp.concatenate([values[2 * g + s] for s in range(3)], axis=1)
                    for g in range(start, start + per_dot)
                ],
                axis=0,
            )
            y = jnp.dot(x, wbig_ref[...], preferred_element_type=F32)
            y = jnp.maximum(y + bias4, 0.0)
            for group in range(start, start + per_dot):
                at = HALO + v + 8 * group
                parts = []
                for k in range(2):
                    row = pa6_s[at + 4 * k : at + 4 * k + 1, 2 * F2 : 4 * F2]
                    row = jnp.broadcast_to(row, (16, 2 * F2)).astype(BF16)
                    parts.append(
                        jnp.maximum(row[None] + col_centre, zero).reshape(2 * bins, 2 * F2)
                    )
                centre = jnp.concatenate(parts, axis=1).astype(F32)
                at_row = (group - start) * 2 * bins
                mixed = y[at_row : at_row + 2 * bins] + centre
                mix_s[group, :, v * 4 * F2 : (v + 1) * 4 * F2] = mixed.astype(BF16)

    lane_live = side_ref[1:2, : 2 * F2] != 0
    for group in range(groups):
        value = lax.dot_general(
            head_ref[...], mix_s[group], (((1,), (1,)), ((), ())), preferred_element_type=F32
        )[:8]
        bin_index = i * bins + 8 * group + lax.broadcasted_iota(jnp.int32, (8, 2 * bins), 0)
        out_ref[8 * group : 8 * group + 8, :] = jnp.where(
            lane_live & (bin_index < length_ref[0]), value, 0.0
        )


def local(
    features,
    chrom_len,
    band_mask,
    conv_weight,
    conv_bias,
    proj_weight,
    proj_bias,
    map_weight,
    map_bias,
    head_weight,
):
    bins, half = features.shape
    rows = 2 * bins + 2 * HALO
    half_out = map_bias.shape[0]
    smem = pl.BlockSpec(memory_space=pltpu.SMEM)
    vmem = pl.BlockSpec(memory_space=pltpu.VMEM)
    anywhere = pl.BlockSpec(memory_space=pl.ANY)
    params = pltpu.CompilerParams(vmem_limit_bytes=24 * 1024 * 1024)

    def in_hbm(value):
        return pltpu.with_memory_space_constraint(value, pltpu.HBM)

    other = chan_swap(features)
    cb_oth = chan_swap(conv_bias)
    own, small = pl.pallas_call(
        front_kernel,
        out_shape=[
            jax.ShapeDtypeStruct(features.shape, BF16),
            jax.ShapeDtypeStruct((8, half), F32),
        ],
        in_specs=[anywhere] * 3,
        out_specs=[vmem] * 2,
        scratch_shapes=[
            pltpu.VMEM(conv_bias.shape, BF16),
            pltpu.VMEM((1, 2 * F2), BF16),
            pltpu.SemaphoreType.DMA((3,)),
        ],
        cost_estimate=pl.CostEstimate(flops=500000000, bytes_accessed=1000000, transcendentals=0),
        compiler_params=params,
    )(in_hbm(features), in_hbm(conv_bias), in_hbm(proj_bias[None]))
    own, cb_oth = lax.optimization_barrier((jnp.stack([own, other]), cb_oth))
    even = pair_permute(own, 0)
    odd = pair_permute(own, 1)
    r2 = line_permute(own[:, :RIM], 2)
    w_in, own = lax.optimization_barrier((conv_weight, own))
    w_oth = chan_swap(w_in)
    window = pl.pallas_call(
        window_kernel,
        out_shape=jax.ShapeDtypeStruct((rows, 2 * half), F32),
        in_specs=[vmem] * 4,
        out_specs=vmem,
        cost_estimate=pl.CostEstimate(flops=4000000000, bytes_accessed=1000000, transcendentals=0),
        compiler_params=params,
    )(own, r2, odd, even)
    mask, packed = pl.pallas_call(
        pack_kernel,
        out_shape=[
            jax.ShapeDtypeStruct(band_mask.shape[::-1], jnp.int32),
            jax.ShapeDtypeStruct((9 * half_out, 2 * F2), BF16),
        ],
        in_specs=[anywhere] * 5,
        out_specs=[vmem] * 2,
        scratch_shapes=[
            pltpu.VMEM(map_weight.shape, BF16),
            pltpu.VMEM((1, half_out), BF16),
            pltpu.VMEM((1, half_out), BF16),
            pltpu.VMEM((32, 2 * F2), F32),
            pltpu.SemaphoreType.DMA((4,)),
        ],
        compiler_params=params,
    )(
        own,
        in_hbm(band_mask.T),
        in_hbm(map_weight),
        in_hbm(map_bias[None]),
        in_hbm(head_weight[None]),
    )
    cols, both = pl.pallas_call(
        trunk_kernel,
        out_shape=[
            jax.ShapeDtypeStruct((bins + 2 * HALO, 2 * F2), BF16),
            jax.ShapeDtypeStruct((2 * bins + 4 * HALO + 9 * half_out, 2 * F2), BF16),
        ],
        in_specs=[smem] + [vmem] * 7,
        out_specs=[vmem] * 2,
        scratch_shapes=[pltpu.VMEM((rows, 2 * half), F32)],
        compiler_params=params,
    )(chrom_len, window, conv_weight, proj_weight, w_oth, small, cb_oth, packed)
    cols_far = line_permute(cols, 2)
    near_both = chan_swap(both)
    prepared = pl.pallas_call(
        prep_kernel,
        out_shape=[
            jax.ShapeDtypeStruct((3, 2 * bins, 6 * F2), F32),
            jax.ShapeDtypeStruct((18 * F2, 4 * F2), BF16),
            jax.ShapeDtypeStruct((8, half), F32),
            jax.ShapeDtypeStruct((16, 8 * F2), BF16),
        ],
        in_specs=[smem] + [vmem] * 3,
        out_specs=[vmem] * 4,
        scratch_shapes=[
            pltpu.VMEM((4 * F2, 18 * F2), F32),
            pltpu.VMEM((9, F2, F2), F32),
        ],
        compiler_params=params,
    )(chrom_len, mask, packed, near_both)
    tiles = functools.partial(
        pl.pallas_call,
        out_shape=jax.ShapeDtypeStruct((bins, 2 * bins), F32),
        out_specs=vmem,
        scratch_shapes=[
            pltpu.VMEM((bins + 2 * HALO, 6 * F2), F32),
            pltpu.VMEM((bins // 8, 2 * bins, 8 * F2), BF16),
        ],
        compiler_params=params,
    )
    near = tiles(near_kernel, in_specs=[smem] + [vmem] * 6)(
        chrom_len, near_both, near_both, *prepared
    )
    return tiles(far_kernel, in_specs=[vmem, smem] + [vmem] * 6)(
        near, chrom_len, cols_far, both, *prepared
    )


def solution(mesh):
    return jax.shard_map(
        local,
        mesh=mesh,
        in_specs=(
            P(("dp", "blk"), "chan"),
            P("dp"),
            P("dp", None),
            P(None, None, None, "chan"),
            P(None, "chan"),
            P(),
            P(),
            P(None, None, "chan", None),
            P("chan"),
            P("chan"),
        ),
        out_specs=P(("dp", "blk"), "chan"),
        check_vma=False,
    )
```

```python
import functools

import jax
import jax.numpy as jnp
from jax import lax
from jax.experimental import pallas as pl
from jax.experimental.pallas import tpu as pltpu
from jax.sharding import PartitionSpec as P

F2 = 64
BAND = 3
CONV1 = 2
D2 = 2
HALO = 8
RIM = 16
F32 = jnp.float32
BF16 = jnp.bfloat16


def chan_swap(value):
    return lax.ppermute(value, "chan", [(0, 1), (1, 0)])


def line_permute(value, step):
    count = lax.axis_size("blk")
    pairs = []
    for i in range(count):
        pairs.append(((i - step) * 2 if i >= step else i * 2 + 1, i * 2))
        pairs.append(((i + step) * 2 + 1 if i + step < count else i * 2, i * 2 + 1))
    return lax.ppermute(value, ("blk", "chan"), pairs)


def pair_permute(value, low):
    count = lax.axis_size("blk")
    source = {}
    for i in range(count):
        source[i, 0] = (i ^ 1, 0)
    for i in range(low, count - 1, 2):
        source[i, 1], source[i + 1, 1] = (i + 1, 1), (i, 1)
    for i in range(count):
        if (i, 1) not in source:
            source[i, 1] = (i ^ 1, 0)
            source[i, 0] = (i, 1)
    pairs = [(j * 2 + d, i * 2 + c) for (i, c), (j, d) in source.items()]
    return lax.ppermute(value, ("blk", "chan"), pairs)


def front_kernel(
    own_any, cb_any, pb_any, pw_any, own_ref, small_ref, pw_ref, cb_s, pb_s, sems
):
    pairs = ((cb_any, cb_s), (pb_any, pb_s), (own_any, own_ref), (pw_any, pw_ref))
    copies = [
        pltpu.make_async_copy(source, target, sems.at[at])
        for at, (source, target) in enumerate(pairs)
    ]
    for copy in copies:
        copy.start()
    copies[0].wait()
    copies[1].wait()
    small_ref[0:CONV1, :] = cb_s[...].astype(F32)
    small_ref[CONV1 : CONV1 + 1, : 2 * F2] = pb_s[...].astype(F32)
    for copy in copies[2:]:
        copy.wait()


def pack_kernel(
    after_any,
    mask_any,
    mw_any,
    mb_any,
    hw_any,
    mask_ref,
    packed_ref,
    mw_s,
    mb_s,
    hw_s,
    extra_s,
    sems,
):
    pairs = ((mw_any, mw_s), (mb_any, mb_s), (hw_any, hw_s), (mask_any, mask_ref))
    copies = [
        pltpu.make_async_copy(source, target, sems.at[at])
        for at, (source, target) in enumerate(pairs)
    ]
    for copy in copies:
        copy.start()
    extra_s[...] = jnp.zeros_like(extra_s)
    for copy in copies:
        copy.wait()

    half = mw_any.shape[2]
    extra_s[8:9, :half] = mb_s[...].astype(F32)
    extra_s[9:10, :half] = hw_s[...].astype(F32)
    extra = pltpu.roll(extra_s[...], F2, axis=1)
    for s in range(3):
        for r in range(3):
            at = (3 * s + r) * half
            packed_ref[at : at + half, :F2] = mw_s[s, r]
    packed_ref[:32, F2:] = extra[:, F2:].astype(BF16)


def prep_kernel(
    length_ref,
    mask_ref,
    own_ref,
    oth_ref,
    col_mask_ref,
    wbig_ref,
    side_ref,
    head_ref,
    wt_s,
    taps_s,
):
    half = own_ref.shape[0] // 9
    behind = oth_ref.shape[0] - own_ref.shape[0]
    columns = col_mask_ref.shape[1]
    bins = columns // 2
    count = lax.axis_size("blk")
    i = lax.axis_index("blk")
    c = lax.axis_index("chan")
    first_col = i * bins + c * columns
    length = length_ref[0]

    for source, skip, side in ((own_ref, 0, c), (oth_ref, behind, 1 - c)):
        at = pl.ds(pl.multiple_of(side * half, half), half)
        for tap in range(9):
            row = skip + tap * half
            taps_s[tap, at, :] = source[row : row + half, :F2].astype(F32)
    blank = jnp.zeros((F2, F2), F32)
    for j in range(4):
        pieces = []
        for m in range(6):
            for r in range(3):
                pieces.append(taps_s[3 * (m - j) + r] if 0 <= m - j < 3 else blank)
        for tile in range(9):
            wt_s[j * F2 : (j + 1) * F2, tile * 2 * F2 : (tile + 1) * 2 * F2] = jnp.concatenate(
                pieces[2 * tile : 2 * tile + 2], axis=1
            )
    wbig_ref[...] = wt_s[...].T.astype(BF16)

    def spread(row, repeats):
        o = lax.broadcasted_iota(jnp.int32, (2 * F2, repeats * F2), 0)
        lane = lax.broadcasted_iota(jnp.int32, (2 * F2, repeats * F2), 1) % F2
        total = jnp.zeros((16, repeats * F2), F32)
        for ref, skip, side in ((own_ref, 0, c), (oth_ref, behind, 1 - c)):
            pick = ((lane == side * half + o - F2) & (o >= F2) & (o < F2 + half)).astype(BF16)
            value = ref[skip : skip + 16, :].astype(F32)[row : row + 1]
            value = jnp.broadcast_to(value, (16, 2 * F2)).astype(BF16)
            total = total + jnp.dot(value, pick, preferred_element_type=F32)
        return total

    q = lax.broadcasted_iota(jnp.int32, (16, 8 * F2), 0)
    k = lax.broadcasted_iota(jnp.int32, (16, 8 * F2), 1)
    head_ref[...] = jnp.where(
        q == 2 * ((k % (4 * F2)) // F2) + k // (4 * F2), spread(9, 8), 0.0
    ).astype(BF16)
    side_ref[0:1, :] = spread(8, 4)[:1]
    minus = F32(-jnp.inf)
    block = lax.broadcasted_iota(jnp.int32, (BAND + 1, count), 1)

    def live_at(y, variant):
        at_row = jnp.sum(jnp.where(block == i + variant, mask_ref[...], 0), axis=1, keepdims=True)
        offset = lax.broadcasted_iota(jnp.int32, (BAND + 1, 1), 0)

        def entry(u):
            return jnp.sum(
                jnp.where(offset == 2 * c + u - variant, at_row, 0), axis=0, keepdims=True
            )

        value = jnp.where(
            y < 0,
            entry(-1),
            jnp.where(y < bins, entry(0), jnp.where(y < columns, entry(1), entry(2))),
        )
        column = first_col + y
        return (value != 0) & (column >= 0) & (column < length)

    b_index = lax.broadcasted_iota(jnp.int32, (columns, 2 * F2), 0)
    low = lax.broadcasted_iota(jnp.int32, (columns, 2 * F2), 1) < F2
    masks = {}
    for variant in (-1, 0, 1):
        for r in range(3):
            masks[variant, r] = jnp.where(
                live_at(b_index + (r - 1) * D2, variant), 0.0, minus
            )
    for at, (v0, v1) in enumerate(((-1, 0), (0, 0), (0, 1))):
        col_mask_ref[at, :, : 2 * F2] = jnp.where(low, masks[v0, 0], masks[v0, 1])
        col_mask_ref[at, :, 2 * F2 : 4 * F2] = jnp.where(low, masks[v0, 2], masks[v1, 0])
        col_mask_ref[at, :, 4 * F2 :] = jnp.where(low, masks[v1, 1], masks[v1, 2])

    side_ref[1:2, : 2 * F2] = jnp.where(
        live_at(lax.broadcasted_iota(jnp.int32, (1, columns), 1), 0), 1.0, 0.0
    )


def window_kernel(own_ref, r2_ref, odd_ref, even_ref, h_ref):
    core = lax.axis_index("chan")
    parity = lax.rem(lax.axis_index("blk"), 2)
    bins = own_ref.shape[1]
    half = own_ref.shape[2]

    def fill(before_ref, after_ref):
        for part in range(2):
            lanes = slice(part * half, (part + 1) * half)
            held = 1 - part
            before = before_ref[held, bins - RIM :, :].astype(F32)
            h_ref[:HALO, lanes] = before[RIM - HALO :]
            h_ref[HALO : HALO + bins, lanes] = own_ref[held].astype(F32)
            h_ref[HALO + bins : HALO + 2 * bins, lanes] = after_ref[held].astype(F32)
            h_ref[HALO + 2 * bins :, lanes] = r2_ref[held].astype(F32)[:HALO]

    @pl.when((core == 1) & (parity == 0))
    def _():
        fill(odd_ref, even_ref)

    @pl.when((core == 1) & (parity == 1))
    def _():
        fill(even_ref, odd_ref)


def trunk_kernel(*refs):
    packed_ref, cols_ref, both_ref = refs[-4:-1]
    ready = both_ref.shape[0] - packed_ref.shape[0]
    both_ref[ready:, :] = packed_ref[...]

    @pl.when(lax.axis_index("chan") == 0)
    def _():
        cols_ref[...] = jnp.zeros_like(cols_ref)
        both_ref[:ready, :] = jnp.zeros((ready, 2 * F2), BF16)

    @pl.when(lax.axis_index("chan") == 1)
    def _():
        trunk(*refs)


def trunk(
    length_ref,
    window_ref,
    w_own_ref,
    pw_ref,
    w_oth_ref,
    small_ref,
    cb_oth_ref,
    packed_ref,
    cols_ref,
    both_ref,
    h_s,
):
    rows = window_ref.shape[0]
    half = window_ref.shape[1] // 2
    held = cols_ref.shape[0]
    bins = held - 2 * HALO
    count = lax.axis_size("blk")
    i = lax.axis_index("blk")
    bin_index = i * bins - HALO + lax.broadcasted_iota(jnp.int32, (rows, 2 * F2), 0)
    valid = (bin_index >= 0) & (bin_index < length_ref[0])
    inside = ((bin_index >= 0) & (bin_index < count * bins))[:, :1]

    for at in range(0, 2 * half, 128):
        h_s[:, at : at + 128] = jnp.where(valid, window_ref[:, at : at + 128], 0.0)

    for layer in range(CONV1):
        e = 2 ** (layer + 1)
        hidden = h_s[...]
        taps = [
            (hidden if t == 1 else pltpu.roll(hidden, ((1 - t) * e) % rows, axis=0)).astype(BF16)
            for t in range(3)
        ]
        for at, w_ref, bias_ref in ((half, w_own_ref, small_ref), (0, w_oth_ref, cb_oth_ref)):
            q = jnp.dot(taps[0], w_ref[layer, 0], preferred_element_type=F32)
            q = q + jnp.dot(taps[1], w_ref[layer, 1], preferred_element_type=F32)
            q = q + jnp.dot(taps[2], w_ref[layer, 2], preferred_element_type=F32)
            bias = bias_ref[...].astype(F32)[layer : layer + 1, :]
            lanes = slice(at, at + half)
            new = (h_s[:, lanes] + jnp.maximum(q + bias, 0.0)).astype(BF16).astype(F32)
            h_s[:, lanes] = jnp.where(inside, new, 0.0)

    proj = jnp.dot(h_s[...].astype(BF16), pw_ref[...], preferred_element_type=F32)
    proj = (proj + small_ref[CONV1 : CONV1 + 1, : 2 * F2]).astype(BF16).astype(F32)
    low = lax.broadcasted_iota(jnp.int32, (1, 2 * F2), 1) < F2
    turned = pltpu.roll(proj, F2, axis=1)
    cols = jnp.where(low, turned[:held], proj[rows - held :]).astype(BF16)
    cols_ref[...] = cols
    both_ref[:held, :] = cols
    both_ref[held : 2 * held, :] = jnp.where(valid, jnp.where(low, proj, turned), -jnp.inf)[:held].astype(
        BF16
    )


def near_kernel(*refs):
    @pl.when(lax.axis_index("chan") == 0)
    def _():
        contact_tiles(*refs)


def far_kernel(near_ref, *refs):
    @pl.when(lax.axis_index("chan") == 0)
    def _():
        refs[7][...] = near_ref[...]

    @pl.when(lax.axis_index("chan") == 1)
    def _():
        contact_tiles(*refs)


def contact_tiles(
    length_ref,
    cols_ref,
    rows_ref,
    col_mask_ref,
    wbig_ref,
    side_ref,
    head_ref,
    out_ref,
    pa6_s,
    mix_s,
):
    bins = out_ref.shape[0]
    col_rows = 2 * bins + 2 * HALO
    row_rows = bins + 2 * HALO
    i = lax.axis_index("blk")

    low = lax.broadcasted_iota(jnp.int32, (1, 2 * F2), 1) < F2
    held = bins + 2 * HALO
    pcol = cols_ref[: bins + 2 * HALO, :].astype(F32)
    turned = pltpu.roll(pcol, F2, axis=1)
    pcol = jnp.concatenate(
        [jnp.where(low, pcol, turned), jnp.where(low, turned, pcol)[2 * held - col_rows :]], axis=0
    )
    shifted = [
        pltpu.roll(pcol, col_rows - HALO - (r - 1) * D2, axis=0)[: 2 * bins] for r in range(3)
    ]
    tiles = [
        jnp.where(low, shifted[0], shifted[1]),
        jnp.where(low, shifted[2], shifted[0]),
        jnp.where(low, shifted[1], shifted[2]),
    ]
    tiled = jnp.concatenate(tiles, axis=1)
    col_first, col_mid, col_last = [
        (tiled + col_mask_ref[at]).astype(BF16).reshape(2 * bins // 16, 16, 6 * F2)
        for at in range(3)
    ]
    col_centre = shifted[1].astype(BF16).reshape(2 * bins // 16, 16, 2 * F2)

    prow = rows_ref[row_rows : 2 * row_rows, :].astype(F32)
    prow_next = pltpu.roll(prow, row_rows - D2, axis=0)
    pa6_s[:, : 2 * F2] = prow
    pa6_s[:, 2 * F2 : 4 * F2] = jnp.where(low, prow, prow_next)
    pa6_s[:, 4 * F2 :] = prow_next

    groups = bins // 8
    per_dot = 4
    zero = jnp.zeros((), BF16)
    bias4 = side_ref[0:1, :]
    for v in range(2):
        for start in range(0, groups, per_dot):
            values = {}
            for slot in range(2 * start, 2 * (start + per_dot) + 1):
                at = HALO - D2 + v + 4 * slot
                row = jnp.broadcast_to(pa6_s[at : at + 1, :], (16, 6 * F2)).astype(BF16)
                cols = col_first if slot == 0 else col_last if slot == 2 * groups else col_mid
                values[slot] = jnp.maximum(row[None] + cols, zero).reshape(2 * bins, 6 * F2)
            x = jnp.concatenate(
                [
                    jnp.concatenate([values[2 * g + s] for s in range(3)], axis=1)
                    for g in range(start, start + per_dot)
                ],
                axis=0,
            )
            y = jnp.dot(x, wbig_ref[...], preferred_element_type=F32)
            y = jnp.maximum(y + bias4, 0.0)
            for group in range(start, start + per_dot):
                at = HALO + v + 8 * group
                parts = []
                for k in range(2):
                    row = pa6_s[at + 4 * k : at + 4 * k + 1, 2 * F2 : 4 * F2]
                    row = jnp.broadcast_to(row, (16, 2 * F2)).astype(BF16)
                    parts.append(
                        jnp.maximum(row[None] + col_centre, zero).reshape(2 * bins, 2 * F2)
                    )
                centre = jnp.concatenate(parts, axis=1).astype(F32)
                at_row = (group - start) * 2 * bins
                mixed = y[at_row : at_row + 2 * bins] + centre
                mix_s[group, :, v * 4 * F2 : (v + 1) * 4 * F2] = mixed.astype(BF16)

    lane_live = side_ref[1:2, : 2 * F2] != 0
    value = lax.dot_general(
        head_ref[...],
        mix_s[...].reshape(groups * 2 * bins, 8 * F2),
        (((1,), (1,)), ((), ())),
        preferred_element_type=F32,
    )
    for group in range(groups):
        bin_index = i * bins + 8 * group + lax.broadcasted_iota(jnp.int32, (8, 2 * bins), 0)
        out_ref[8 * group : 8 * group + 8, :] = jnp.where(
            lane_live & (bin_index < length_ref[0]),
            value[:8, 2 * bins * group : 2 * bins * (group + 1)],
            0.0,
        )


def local(
    features,
    chrom_len,
    band_mask,
    conv_weight,
    conv_bias,
    proj_weight,
    proj_bias,
    map_weight,
    map_bias,
    head_weight,
):
    bins, half = features.shape
    rows = 2 * bins + 2 * HALO
    half_out = map_bias.shape[0]
    smem = pl.BlockSpec(memory_space=pltpu.SMEM)
    vmem = pl.BlockSpec(memory_space=pltpu.VMEM)
    anywhere = pl.BlockSpec(memory_space=pl.ANY)
    params = pltpu.CompilerParams(vmem_limit_bytes=24 * 1024 * 1024)

    def in_hbm(value):
        return pltpu.with_memory_space_constraint(value, pltpu.HBM)

    other = chan_swap(features)
    cb_oth = chan_swap(conv_bias)
    own, small, pw = pl.pallas_call(
        front_kernel,
        out_shape=[
            jax.ShapeDtypeStruct(features.shape, BF16),
            jax.ShapeDtypeStruct((8, half), F32),
            jax.ShapeDtypeStruct(proj_weight.shape, BF16),
        ],
        in_specs=[anywhere] * 4,
        out_specs=[vmem] * 3,
        scratch_shapes=[
            pltpu.VMEM(conv_bias.shape, BF16),
            pltpu.VMEM((1, 2 * F2), BF16),
            pltpu.SemaphoreType.DMA((4,)),
        ],
        cost_estimate=pl.CostEstimate(flops=500000000, bytes_accessed=1000000, transcendentals=0),
        compiler_params=params,
    )(in_hbm(features), in_hbm(conv_bias), in_hbm(proj_bias[None]), in_hbm(proj_weight))
    own, cb_oth = lax.optimization_barrier((jnp.stack([own, other]), cb_oth))
    even = pair_permute(own, 0)
    odd = pair_permute(own, 1)
    r2 = line_permute(own[:, :RIM], 2)
    w_in, own = lax.optimization_barrier((conv_weight, own))
    w_oth = chan_swap(w_in)
    window = pl.pallas_call(
        window_kernel,
        out_shape=jax.ShapeDtypeStruct((rows, 2 * half), F32),
        in_specs=[vmem] * 4,
        out_specs=vmem,
        cost_estimate=pl.CostEstimate(flops=4000000000, bytes_accessed=1000000, transcendentals=0),
        compiler_params=params,
    )(own, r2, odd, even)
    mask, packed = pl.pallas_call(
        pack_kernel,
        out_shape=[
            jax.ShapeDtypeStruct(band_mask.shape[::-1], jnp.int32),
            jax.ShapeDtypeStruct((9 * half_out, 2 * F2), BF16),
        ],
        in_specs=[anywhere] * 5,
        out_specs=[vmem] * 2,
        scratch_shapes=[
            pltpu.VMEM(map_weight.shape, BF16),
            pltpu.VMEM((1, half_out), BF16),
            pltpu.VMEM((1, half_out), BF16),
            pltpu.VMEM((32, 2 * F2), F32),
            pltpu.SemaphoreType.DMA((4,)),
        ],
        compiler_params=params,
    )(
        own,
        in_hbm(band_mask.T),
        in_hbm(map_weight),
        in_hbm(map_bias[None]),
        in_hbm(head_weight[None]),
    )
    cols, both = pl.pallas_call(
        trunk_kernel,
        out_shape=[
            jax.ShapeDtypeStruct((bins + 2 * HALO, 2 * F2), BF16),
            jax.ShapeDtypeStruct((2 * bins + 4 * HALO + 9 * half_out, 2 * F2), BF16),
        ],
        in_specs=[smem] + [vmem] * 7,
        out_specs=[vmem] * 2,
        scratch_shapes=[pltpu.VMEM((rows, 2 * half), F32)],
        compiler_params=params,
    )(chrom_len, window, conv_weight, pw, w_oth, small, cb_oth, packed)
    cols_far = line_permute(cols, 2)
    near_both = chan_swap(both)
    prepared = pl.pallas_call(
        prep_kernel,
        out_shape=[
            jax.ShapeDtypeStruct((3, 2 * bins, 6 * F2), F32),
            jax.ShapeDtypeStruct((18 * F2, 4 * F2), BF16),
            jax.ShapeDtypeStruct((8, half), F32),
            jax.ShapeDtypeStruct((16, 8 * F2), BF16),
        ],
        in_specs=[smem] + [vmem] * 3,
        out_specs=[vmem] * 4,
        scratch_shapes=[
            pltpu.VMEM((4 * F2, 18 * F2), F32),
            pltpu.VMEM((9, F2, F2), F32),
        ],
        compiler_params=params,
    )(chrom_len, mask, packed, near_both)
    tiles = functools.partial(
        pl.pallas_call,
        out_shape=jax.ShapeDtypeStruct((bins, 2 * bins), F32),
        out_specs=vmem,
        scratch_shapes=[
            pltpu.VMEM((bins + 2 * HALO, 6 * F2), F32),
            pltpu.VMEM((bins // 8, 2 * bins, 8 * F2), BF16),
        ],
        compiler_params=params,
    )
    near = tiles(near_kernel, in_specs=[smem] + [vmem] * 6)(
        chrom_len, near_both, near_both, *prepared
    )
    return tiles(far_kernel, in_specs=[vmem, smem] + [vmem] * 6)(
        near, chrom_len, cols_far, both, *prepared
    )


def solution(mesh):
    return jax.shard_map(
        local,
        mesh=mesh,
        in_specs=(
            P(("dp", "blk"), "chan"),
            P("dp"),
            P("dp", None),
            P(None, None, None, "chan"),
            P(None, "chan"),
            P(),
            P(),
            P(None, None, "chan", None),
            P("chan"),
            P("chan"),
        ),
        out_specs=P(("dp", "blk"), "chan"),
        check_vma=False,
    )
```

```python
import functools

import jax
import jax.numpy as jnp
from jax import lax
from jax.experimental import pallas as pl
from jax.experimental.pallas import tpu as pltpu
from jax.sharding import PartitionSpec as P

F2 = 64
BAND = 3
CONV1 = 2
D2 = 2
HALO = 8
RIM = 16
F32 = jnp.float32
BF16 = jnp.bfloat16


def chan_swap(value):
    return lax.ppermute(value, "chan", [(0, 1), (1, 0)])


def line_permute(value, step):
    count = lax.axis_size("blk")
    pairs = []
    for i in range(count):
        pairs.append(((i - step) * 2 if i >= step else i * 2 + 1, i * 2))
        pairs.append(((i + step) * 2 + 1 if i + step < count else i * 2, i * 2 + 1))
    return lax.ppermute(value, ("blk", "chan"), pairs)


def pair_permute(value, low):
    count = lax.axis_size("blk")
    source = {}
    for i in range(count):
        source[i, 0] = (i ^ 1, 0)
    for i in range(low, count - 1, 2):
        source[i, 1], source[i + 1, 1] = (i + 1, 1), (i, 1)
    for i in range(count):
        if (i, 1) not in source:
            source[i, 1] = (i ^ 1, 0)
            source[i, 0] = (i, 1)
    pairs = [(j * 2 + d, i * 2 + c) for (i, c), (j, d) in source.items()]
    return lax.ppermute(value, ("blk", "chan"), pairs)


def front_kernel(own_any, cb_any, pb_any, own_ref, small_ref, cb_s, pb_s, sems):
    pairs = ((cb_any, cb_s), (pb_any, pb_s), (own_any, own_ref))
    copies = [
        pltpu.make_async_copy(source, target, sems.at[at])
        for at, (source, target) in enumerate(pairs)
    ]
    for copy in copies:
        copy.start()
    copies[0].wait()
    copies[1].wait()
    small_ref[0:CONV1, :] = cb_s[...].astype(F32)
    small_ref[CONV1 : CONV1 + 1, : 2 * F2] = pb_s[...].astype(F32)
    copies[2].wait()


def pack_kernel(
    after_any,
    mask_any,
    mw_any,
    mb_any,
    hw_any,
    mask_ref,
    packed_ref,
    mw_s,
    mb_s,
    hw_s,
    extra_s,
    sems,
):
    pairs = ((mw_any, mw_s), (mb_any, mb_s), (hw_any, hw_s), (mask_any, mask_ref))
    copies = [
        pltpu.make_async_copy(source, target, sems.at[at])
        for at, (source, target) in enumerate(pairs)
    ]
    for copy in copies:
        copy.start()
    extra_s[...] = jnp.zeros_like(extra_s)
    for copy in copies:
        copy.wait()

    half = mw_any.shape[2]
    extra_s[8:9, :half] = mb_s[...].astype(F32)
    extra_s[9:10, :half] = hw_s[...].astype(F32)
    extra = pltpu.roll(extra_s[...], F2, axis=1)
    for s in range(3):
        for r in range(3):
            at = (3 * s + r) * half
            packed_ref[at : at + half, :F2] = mw_s[s, r]
    packed_ref[:32, F2:] = extra[:, F2:].astype(BF16)


def prep_kernel(
    length_ref,
    mask_ref,
    own_ref,
    oth_ref,
    col_mask_ref,
    wbig_ref,
    side_ref,
    head_ref,
    wt_s,
    taps_s,
):
    half = own_ref.shape[0] // 9
    behind = oth_ref.shape[0] - own_ref.shape[0]
    columns = col_mask_ref.shape[1]
    bins = columns // 2
    count = lax.axis_size("blk")
    i = lax.axis_index("blk")
    c = lax.axis_index("chan")
    first_col = i * bins + c * columns
    length = length_ref[0]

    for source, skip, side in ((own_ref, 0, c), (oth_ref, behind, 1 - c)):
        at = pl.ds(pl.multiple_of(side * half, half), half)
        for tap in range(9):
            row = skip + tap * half
            taps_s[tap, at, :] = source[row : row + half, :F2].astype(F32)
    blank = jnp.zeros((F2, F2), F32)
    for j in range(4):
        pieces = []
        for m in range(6):
            for r in range(3):
                pieces.append(taps_s[3 * (m - j) + r] if 0 <= m - j < 3 else blank)
        for tile in range(9):
            wt_s[j * F2 : (j + 1) * F2, tile * 2 * F2 : (tile + 1) * 2 * F2] = jnp.concatenate(
                pieces[2 * tile : 2 * tile + 2], axis=1
            )
    wbig_ref[...] = wt_s[...].T.astype(BF16)

    def spread(row, repeats):
        o = lax.broadcasted_iota(jnp.int32, (2 * F2, repeats * F2), 0)
        lane = lax.broadcasted_iota(jnp.int32, (2 * F2, repeats * F2), 1) % F2
        total = jnp.zeros((16, repeats * F2), F32)
        for ref, skip, side in ((own_ref, 0, c), (oth_ref, behind, 1 - c)):
            pick = ((lane == side * half + o - F2) & (o >= F2) & (o < F2 + half)).astype(BF16)
            value = ref[skip : skip + 16, :].astype(F32)[row : row + 1]
            value = jnp.broadcast_to(value, (16, 2 * F2)).astype(BF16)
            total = total + jnp.dot(value, pick, preferred_element_type=F32)
        return total

    q = lax.broadcasted_iota(jnp.int32, (16, 8 * F2), 0)
    k = lax.broadcasted_iota(jnp.int32, (16, 8 * F2), 1)
    head_ref[...] = jnp.where(
        q == 2 * ((k % (4 * F2)) // F2) + k // (4 * F2), spread(9, 8), 0.0
    ).astype(BF16)
    side_ref[0:1, :] = spread(8, 4)[:1]
    minus = F32(-jnp.inf)
    block = lax.broadcasted_iota(jnp.int32, (BAND + 1, count), 1)

    def live_at(y, variant):
        at_row = jnp.sum(jnp.where(block == i + variant, mask_ref[...], 0), axis=1, keepdims=True)
        offset = lax.broadcasted_iota(jnp.int32, (BAND + 1, 1), 0)

        def entry(u):
            return jnp.sum(
                jnp.where(offset == 2 * c + u - variant, at_row, 0), axis=0, keepdims=True
            )

        value = jnp.where(
            y < 0,
            entry(-1),
            jnp.where(y < bins, entry(0), jnp.where(y < columns, entry(1), entry(2))),
        )
        column = first_col + y
        return (value != 0) & (column >= 0) & (column < length)

    b_index = lax.broadcasted_iota(jnp.int32, (columns, 2 * F2), 0)
    low = lax.broadcasted_iota(jnp.int32, (columns, 2 * F2), 1) < F2
    masks = {}
    for variant in (-1, 0, 1):
        for r in range(3):
            masks[variant, r] = jnp.where(
                live_at(b_index + (r - 1) * D2, variant), 0.0, minus
            )
    for at, (v0, v1) in enumerate(((-1, 0), (0, 0), (0, 1))):
        col_mask_ref[at, :, : 2 * F2] = jnp.where(low, masks[v0, 0], masks[v0, 1])
        col_mask_ref[at, :, 2 * F2 : 4 * F2] = jnp.where(low, masks[v0, 2], masks[v1, 0])
        col_mask_ref[at, :, 4 * F2 :] = jnp.where(low, masks[v1, 1], masks[v1, 2])

    side_ref[1:2, : 2 * F2] = jnp.where(
        live_at(lax.broadcasted_iota(jnp.int32, (1, columns), 1), 0), 1.0, 0.0
    )


def window_kernel(own_ref, r2_ref, odd_ref, even_ref, h_ref):
    core = lax.axis_index("chan")
    parity = lax.rem(lax.axis_index("blk"), 2)
    bins = own_ref.shape[1]
    half = own_ref.shape[2]

    def fill(before_ref, after_ref):
        for part in range(2):
            lanes = slice(part * half, (part + 1) * half)
            held = 1 - part
            before = before_ref[held, bins - RIM :, :].astype(F32)
            h_ref[:HALO, lanes] = before[RIM - HALO :]
            h_ref[HALO : HALO + bins, lanes] = own_ref[held].astype(F32)
            h_ref[HALO + bins : HALO + 2 * bins, lanes] = after_ref[held].astype(F32)
            h_ref[HALO + 2 * bins :, lanes] = r2_ref[held].astype(F32)[:HALO]

    @pl.when((core == 1) & (parity == 0))
    def _():
        fill(odd_ref, even_ref)

    @pl.when((core == 1) & (parity == 1))
    def _():
        fill(even_ref, odd_ref)


def trunk_kernel(*refs):
    packed_ref, cols_ref, both_ref = refs[-3:]
    ready = both_ref.shape[0] - packed_ref.shape[0]
    both_ref[ready:, :] = packed_ref[...]

    @pl.when(lax.axis_index("chan") == 0)
    def _():
        cols_ref[...] = jnp.zeros_like(cols_ref)
        both_ref[:ready, :] = jnp.zeros((ready, 2 * F2), BF16)

    @pl.when(lax.axis_index("chan") == 1)
    def _():
        trunk(*refs)


def trunk(
    length_ref,
    window_ref,
    w_own_ref,
    pw_ref,
    w_oth_ref,
    small_ref,
    cb_oth_ref,
    packed_ref,
    cols_ref,
    both_ref,
):
    rows = window_ref.shape[0]
    half = window_ref.shape[1] // 2
    held = cols_ref.shape[0]
    bins = held - 2 * HALO
    count = lax.axis_size("blk")
    i = lax.axis_index("blk")
    bin_index = i * bins - HALO + lax.broadcasted_iota(jnp.int32, (rows, 2 * F2), 0)
    valid = (bin_index >= 0) & (bin_index < length_ref[0])
    inside = ((bin_index >= 0) & (bin_index < count * bins))[:, :1]

    wide = jnp.concatenate([valid] * (2 * half // 128), axis=1)
    hidden = jnp.where(wide, window_ref[...], 0.0)
    for layer in range(CONV1):
        e = 2 ** (layer + 1)
        taps = [
            (hidden if t == 1 else pltpu.roll(hidden, ((1 - t) * e) % rows, axis=0)).astype(BF16)
            for t in range(3)
        ]
        sides = []
        for at, w_ref, bias_ref in ((0, w_oth_ref, cb_oth_ref), (half, w_own_ref, small_ref)):
            q = jnp.dot(taps[0], w_ref[layer, 0], preferred_element_type=F32)
            q = q + jnp.dot(taps[1], w_ref[layer, 1], preferred_element_type=F32)
            q = q + jnp.dot(taps[2], w_ref[layer, 2], preferred_element_type=F32)
            bias = bias_ref[...].astype(F32)[layer : layer + 1, :]
            new = (hidden[:, at : at + half] + jnp.maximum(q + bias, 0.0)).astype(BF16)
            sides.append(jnp.where(inside, new.astype(F32), 0.0))
        hidden = jnp.concatenate(sides, axis=1)

    proj = jnp.dot(hidden.astype(BF16), pw_ref[...], preferred_element_type=F32)
    proj = (proj + small_ref[CONV1 : CONV1 + 1, : 2 * F2]).astype(BF16).astype(F32)
    low = lax.broadcasted_iota(jnp.int32, (1, 2 * F2), 1) < F2
    turned = pltpu.roll(proj, F2, axis=1)
    cols = jnp.where(low, turned[:held], proj[rows - held :]).astype(BF16)
    cols_ref[...] = cols
    both_ref[:held, :] = cols
    both_ref[held : 2 * held, :] = jnp.where(valid, jnp.where(low, proj, turned), -jnp.inf)[:held].astype(
        BF16
    )


def near_kernel(*refs):
    @pl.when(lax.axis_index("chan") == 0)
    def _():
        contact_tiles(*refs)


def far_kernel(near_ref, *refs):
    @pl.when(lax.axis_index("chan") == 0)
    def _():
        refs[7][...] = near_ref[...]

    @pl.when(lax.axis_index("chan") == 1)
    def _():
        contact_tiles(*refs)


def contact_tiles(
    length_ref,
    cols_ref,
    rows_ref,
    col_mask_ref,
    wbig_ref,
    side_ref,
    head_ref,
    out_ref,
    pa6_s,
    mix_s,
):
    bins = out_ref.shape[0]
    col_rows = 2 * bins + 2 * HALO
    row_rows = bins + 2 * HALO
    i = lax.axis_index("blk")

    low = lax.broadcasted_iota(jnp.int32, (1, 2 * F2), 1) < F2
    held = bins + 2 * HALO
    pcol = cols_ref[: bins + 2 * HALO, :].astype(F32)
    turned = pltpu.roll(pcol, F2, axis=1)
    pcol = jnp.concatenate(
        [jnp.where(low, pcol, turned), jnp.where(low, turned, pcol)[2 * held - col_rows :]], axis=0
    )
    shifted = [
        pltpu.roll(pcol, col_rows - HALO - (r - 1) * D2, axis=0)[: 2 * bins] for r in range(3)
    ]
    tiles = [
        jnp.where(low, shifted[0], shifted[1]),
        jnp.where(low, shifted[2], shifted[0]),
        jnp.where(low, shifted[1], shifted[2]),
    ]
    tiled = jnp.concatenate(tiles, axis=1)
    col_first, col_mid, col_last = [
        (tiled + col_mask_ref[at]).astype(BF16).reshape(2 * bins // 16, 16, 6 * F2)
        for at in range(3)
    ]
    col_centre = shifted[1].astype(BF16).reshape(2 * bins // 16, 16, 2 * F2)

    prow = rows_ref[row_rows : 2 * row_rows, :].astype(F32)
    prow_next = pltpu.roll(prow, row_rows - D2, axis=0)
    pa6_s[:, : 2 * F2] = prow
    pa6_s[:, 2 * F2 : 4 * F2] = jnp.where(low, prow, prow_next)
    pa6_s[:, 4 * F2 :] = prow_next

    groups = bins // 8
    per_dot = 4
    zero = jnp.zeros((), BF16)
    bias4 = side_ref[0:1, :]
    for v in range(2):
        for start in range(0, groups, per_dot):
            values = {}
            for slot in range(2 * start, 2 * (start + per_dot) + 1):
                at = HALO - D2 + v + 4 * slot
                row = jnp.broadcast_to(pa6_s[at : at + 1, :], (16, 6 * F2)).astype(BF16)
                cols = col_first if slot == 0 else col_last if slot == 2 * groups else col_mid
                values[slot] = jnp.maximum(row[None] + cols, zero).reshape(2 * bins, 6 * F2)
            x = jnp.concatenate(
                [
                    jnp.concatenate([values[2 * g + s] for s in range(3)], axis=1)
                    for g in range(start, start + per_dot)
                ],
                axis=0,
            )
            y = jnp.dot(x, wbig_ref[...], preferred_element_type=F32)
            y = jnp.maximum(y + bias4, 0.0)
            for group in range(start, start + per_dot):
                at = HALO + v + 8 * group
                parts = []
                for k in range(2):
                    row = pa6_s[at + 4 * k : at + 4 * k + 1, 2 * F2 : 4 * F2]
                    row = jnp.broadcast_to(row, (16, 2 * F2)).astype(BF16)
                    parts.append(
                        jnp.maximum(row[None] + col_centre, zero).reshape(2 * bins, 2 * F2)
                    )
                centre = jnp.concatenate(parts, axis=1).astype(F32)
                at_row = (group - start) * 2 * bins
                mixed = y[at_row : at_row + 2 * bins] + centre
                mix_s[group, :, v * 4 * F2 : (v + 1) * 4 * F2] = mixed.astype(BF16)

    lane_live = side_ref[1:2, : 2 * F2] != 0
    for group in range(groups):
        value = lax.dot_general(
            head_ref[...], mix_s[group], (((1,), (1,)), ((), ())), preferred_element_type=F32
        )[:8]
        bin_index = i * bins + 8 * group + lax.broadcasted_iota(jnp.int32, (8, 2 * bins), 0)
        out_ref[8 * group : 8 * group + 8, :] = jnp.where(
            lane_live & (bin_index < length_ref[0]), value, 0.0
        )


def local(
    features,
    chrom_len,
    band_mask,
    conv_weight,
    conv_bias,
    proj_weight,
    proj_bias,
    map_weight,
    map_bias,
    head_weight,
):
    bins, half = features.shape
    rows = 2 * bins + 2 * HALO
    half_out = map_bias.shape[0]
    smem = pl.BlockSpec(memory_space=pltpu.SMEM)
    vmem = pl.BlockSpec(memory_space=pltpu.VMEM)
    anywhere = pl.BlockSpec(memory_space=pl.ANY)
    params = pltpu.CompilerParams(vmem_limit_bytes=24 * 1024 * 1024)

    def in_hbm(value):
        return pltpu.with_memory_space_constraint(value, pltpu.HBM)

    other = chan_swap(features)
    cb_oth = chan_swap(conv_bias)
    own, small = pl.pallas_call(
        front_kernel,
        out_shape=[
            jax.ShapeDtypeStruct(features.shape, BF16),
            jax.ShapeDtypeStruct((8, half), F32),
        ],
        in_specs=[anywhere] * 3,
        out_specs=[vmem] * 2,
        scratch_shapes=[
            pltpu.VMEM(conv_bias.shape, BF16),
            pltpu.VMEM((1, 2 * F2), BF16),
            pltpu.SemaphoreType.DMA((3,)),
        ],
        cost_estimate=pl.CostEstimate(flops=500000000, bytes_accessed=1000000, transcendentals=0),
        compiler_params=params,
    )(in_hbm(features), in_hbm(conv_bias), in_hbm(proj_bias[None]))
    own, cb_oth = lax.optimization_barrier((jnp.stack([own, other]), cb_oth))
    even = pair_permute(own, 0)
    odd = pair_permute(own, 1)
    r2 = line_permute(own[:, :RIM], 2)
    w_in, own = lax.optimization_barrier((conv_weight, own))
    w_oth = chan_swap(w_in)
    window = pl.pallas_call(
        window_kernel,
        out_shape=jax.ShapeDtypeStruct((rows, 2 * half), F32),
        in_specs=[vmem] * 4,
        out_specs=vmem,
        cost_estimate=pl.CostEstimate(flops=4000000000, bytes_accessed=1000000, transcendentals=0),
        compiler_params=params,
    )(own, r2, odd, even)
    mask, packed = pl.pallas_call(
        pack_kernel,
        out_shape=[
            jax.ShapeDtypeStruct(band_mask.shape[::-1], jnp.int32),
            jax.ShapeDtypeStruct((9 * half_out, 2 * F2), BF16),
        ],
        in_specs=[anywhere] * 5,
        out_specs=[vmem] * 2,
        scratch_shapes=[
            pltpu.VMEM(map_weight.shape, BF16),
            pltpu.VMEM((1, half_out), BF16),
            pltpu.VMEM((1, half_out), BF16),
            pltpu.VMEM((32, 2 * F2), F32),
            pltpu.SemaphoreType.DMA((4,)),
        ],
        compiler_params=params,
    )(
        own,
        in_hbm(band_mask.T),
        in_hbm(map_weight),
        in_hbm(map_bias[None]),
        in_hbm(head_weight[None]),
    )
    cols, both = pl.pallas_call(
        trunk_kernel,
        out_shape=[
            jax.ShapeDtypeStruct((bins + 2 * HALO, 2 * F2), BF16),
            jax.ShapeDtypeStruct((2 * bins + 4 * HALO + 9 * half_out, 2 * F2), BF16),
        ],
        in_specs=[smem] + [vmem] * 7,
        out_specs=[vmem] * 2,
        compiler_params=params,
    )(chrom_len, window, conv_weight, proj_weight, w_oth, small, cb_oth, packed)
    cols_far = line_permute(cols, 2)
    near_both = chan_swap(both)
    prepared = pl.pallas_call(
        prep_kernel,
        out_shape=[
            jax.ShapeDtypeStruct((3, 2 * bins, 6 * F2), F32),
            jax.ShapeDtypeStruct((18 * F2, 4 * F2), BF16),
            jax.ShapeDtypeStruct((8, half), F32),
            jax.ShapeDtypeStruct((16, 8 * F2), BF16),
        ],
        in_specs=[smem] + [vmem] * 3,
        out_specs=[vmem] * 4,
        scratch_shapes=[
            pltpu.VMEM((4 * F2, 18 * F2), F32),
            pltpu.VMEM((9, F2, F2), F32),
        ],
        compiler_params=params,
    )(chrom_len, mask, packed, near_both)
    tiles = functools.partial(
        pl.pallas_call,
        out_shape=jax.ShapeDtypeStruct((bins, 2 * bins), F32),
        out_specs=vmem,
        scratch_shapes=[
            pltpu.VMEM((bins + 2 * HALO, 6 * F2), F32),
            pltpu.VMEM((bins // 8, 2 * bins, 8 * F2), BF16),
        ],
        compiler_params=params,
    )
    near = tiles(near_kernel, in_specs=[smem] + [vmem] * 6)(
        chrom_len, near_both, near_both, *prepared
    )
    return tiles(far_kernel, in_specs=[vmem, smem] + [vmem] * 6)(
        near, chrom_len, cols_far, both, *prepared
    )


def solution(mesh):
    return jax.shard_map(
        local,
        mesh=mesh,
        in_specs=(
            P(("dp", "blk"), "chan"),
            P("dp"),
            P("dp", None),
            P(None, None, None, "chan"),
            P(None, "chan"),
            P(),
            P(),
            P(None, None, "chan", None),
            P("chan"),
            P("chan"),
        ),
        out_specs=P(("dp", "blk"), "chan"),
        check_vma=False,
    )
```
